128 devices in a mesh: dp: 32 (over z, x, core), tp: 4 (over y).
Axes of the slice: x: 4, y: 4, z: 4, core: 2. Of those that a mesh axis runs over, the one named last changes fastest.
Arguments:
- queries: bfloat16 [512, 128, 576], P(('dp', 'tp')), may hold values from -16 to 16
- latent_cache: bfloat16 [512, 1024, 576], P(('dp', 'tp')), may hold values from -4 to 4
- lengths: int32 [512], P(('dp', 'tp')), may hold values from 2 to 1024, as said below
- uv_weight: bfloat16 [128, 512, 128], P('tp'), may hold values from -0.25 to 0.25
- out_weight: bfloat16 [16384, 7168], P('tp', 'dp'), may hold values from -0.375 to 0.375
- residual: bfloat16 [512, 7168], P(None, 'dp'), may hold values from -6 to 6
- norm_gain: float32 [7168], replicated, may hold values from 0.1 to 1.9
- gate_weight: bfloat16 [32, 7168, 1024], P('dp', None, 'tp'), may hold values from -0.0625 to 0.0625
- up_weight: bfloat16 [32, 7168, 1024], P('dp', None, 'tp'), may hold values from -0.0625 to 0.0625
- down_weight: bfloat16 [32, 1024, 7168], P('dp', 'tp'), may hold values from -0.1875 to 0.1875
- routes: int32 [512, 8], replicated, may hold values from 0 to 31, all different within a row; in each aligned block of 512 rows (0 to 511, 512 to 1023, ...) at most 384 rows name the same one
- route_weights: float32 [512, 8], replicated, may hold values from 0.1 to 0.6
Outputs:
- block_output: bfloat16 [512, 7168], P('tp', 'dp')
The draws below stay inside these ranges and needn't reach their ends.
Inputs may be any that keep to these rules, and one draw needn't show every extreme that they name: `routes`: each row names 8 different experts; no expert is named by more than 384 of the 512 rows, a bound that some block reaches. `lengths`: some row uses all 1024 positions.
All inputs are finite; a program needn't handle non-finite values.
Results may differ from the reference program's by a relative error of at most 0.01.
Values may be sent and summed in bfloat16 or wider, within the bound.
A program may use at most 128 MiB of HBM per device.

```python
import math
import jax
import jax.numpy as jnp
import numpy as np
from jax import lax

D = 7168
H = 128
LAT = 512
ROPE = 64
VHEAD = 128
E_FF = 1024
TOPK = 8
CTX = 1024
ROWS = 512
EXPERTS = 32
GROUP = 256
CAP = 384
N_TP = 4


def shared_positions(key):
    length_key = jax.random.fold_in(key, 0)
    lengths = jax.random.randint(length_key, (ROWS,), 2, CTX + 1).at[0].set(CTX)
    return lengths


def base_cache(key):
    return jnp.clip(jax.random.normal(jax.random.fold_in(key, 5), (ROWS, CTX, LAT + ROPE), jnp.float32), -4.0, 4.0)


def draw_lengths(key, part):
    lengths = shared_positions(key)
    return lengths


def draw_latent_cache(key, part):
    cache_draw = base_cache(key)
    return cache_draw.astype(jnp.bfloat16)


def draw_queries(key, part):
    key = jax.random.fold_in(key, 11)
    drawn_draw = jnp.clip(jax.random.normal(key, (ROWS, H, LAT + ROPE), jnp.float32), -4.0, 4.0)
    return drawn_draw.astype(jnp.bfloat16)


def level_of(rng, dims, shards, low, high):
    loudness = 1.0
    for position, shards_of in shards:
        draws = jax.random.uniform(jax.random.fold_in(jax.random.fold_in(rng, 6), position), (shards_of,), jnp.float32, low / len(shards), high / len(shards))
        loudness = loudness * jnp.repeat(jnp.exp(draws), dims[position] // shards_of).reshape((-1,) + (1,) * (len(dims) - 1 - position))
    return loudness


def shared_out(stream_key, own, number, rows, count, top, bound, lean):
    ranking = jax.random.permutation(stream_key, count)
    heavy_load, usual = shares(count, rows * top, bound, lean, True), shares(count, rows * top, bound, lean, False)
    places = jnp.arange(count)

    def named(tallies, turn):
        used = int((tallies > 0).sum())
        fixed = max(1, used // 4)
        shifted = fixed + (places - fixed + turn * (used - fixed)) % max(1, count - fixed)
        return jnp.zeros((count,), jnp.int32).at[ranking[jnp.where(places < fixed, places, shifted)]].set(jnp.asarray(tallies, jnp.int32))

    tallies = jnp.where(number % 4 == 0, named(heavy_load, number // 4), named(usual, number - number // 4 - 1))
    mixed = jax.random.permutation(jax.random.fold_in(own, 3), count)
    source_of, receiver = mixed[0:count // 2 * 2:2], mixed[1:count // 2 * 2:2]
    room = jnp.minimum(tallies[source_of] - 1, bound - tallies[receiver]) // 2
    room = jnp.where((source_of == ranking[0]) | (receiver == ranking[0]) | (tallies[receiver] == 0), 0, jnp.maximum(room, 0))
    shifted = jax.random.randint(jax.random.fold_in(own, 4), (count // 2,), 0, 1 << 20) % (room + 1)
    tallies = tallies.at[source_of].add(-shifted).at[receiver].add(shifted)
    items = jnp.searchsorted(jnp.cumsum(tallies), jnp.arange(rows * top), side="right").astype(jnp.int32)
    grid = items.reshape(top, rows).T
    grid = grid[jax.random.permutation(jax.random.fold_in(own, 1), rows)]
    turn = jax.random.randint(jax.random.fold_in(own, 2), (rows, 1), 0, top)
    return jnp.take_along_axis(grid, (jnp.arange(top)[None, :] + turn) % top, axis=1)


def shares(number_of, total, most, slope, full):
    portions = [(1 << 20) // math.isqrt(rank ** slope) + 1 for rank in range(1, number_of + 1)]
    largest = most if full else min(most, max(-(-total // number_of), total * portions[0] // sum(portions)))
    least = 1 if total - largest >= number_of - 1 else 0
    counts, surplus = [largest] + [least] * (number_of - 1), total - largest - least * (number_of - 1)
    while surplus > 0:
        free = [i for i in range(1, number_of) if counts[i] < largest] or [i for i in range(1, number_of) if counts[i] < most]
        whole, remaining = sum([portions[i] for i in free]), surplus
        for i in free:
            extra = min(most - counts[i], max(1, remaining * portions[i] // whole), surplus)
            counts[i] = counts[i] + extra
            surplus = surplus - extra
    return np.array(counts)


def bell_draw(stream_key, shape, deviation, reach, cuts=(), kind=jnp.bfloat16):
    values = deviation * jax.random.normal(stream_key, shape, jnp.float32)
    if cuts:
        values = values * level_of(stream_key, shape, cuts, -0.22, 0.18)
    return jnp.clip(values, -reach, reach).astype(kind)


def setup_inputs(seed: int = 0) -> dict:
    seeds = jax.random.split(jax.random.key(seed), 13)
    queries = draw_queries(jax.random.fold_in(seeds[12], 71), 0)
    latent_cache = draw_latent_cache(jax.random.fold_in(seeds[12], 71), 0)
    lengths = draw_lengths(jax.random.fold_in(seeds[12], 71), 0)
    uv_weight = bell_draw(seeds[3], (H, LAT, VHEAD), LAT ** -0.5, 0.25, ((0, 4),))
    out_weight = bell_draw(seeds[4], (H * VHEAD, D), (3.0 / (H * VHEAD) ** 0.5), 0.375, ((0, 4), (1, 32)))
    residual = bell_draw(seeds[5], (ROWS, D), 1.0, 6.0, ((1, 32),))
    norm_gain = jnp.clip(1.0 + 0.18 * jax.random.normal(seeds[6], (D,), jnp.float32), 0.1, 1.9)
    gate_weight = bell_draw(seeds[7], (EXPERTS, D, E_FF), D ** -0.5, 0.0625, ((0, 32), (2, 4)))
    up_weight = bell_draw(seeds[8], (EXPERTS, D, E_FF), D ** -0.5, 0.0625, ((0, 32), (2, 4)))
    down_weight = bell_draw(seeds[9], (EXPERTS, E_FF, D), E_FF ** -0.5, 0.1875, ((0, 32), (1, 4)))
    routes_keys = jax.random.split(jax.random.fold_in(seeds[10], 1), ROWS // ROWS)
    routes_turns = jax.random.permutation(jax.random.fold_in(seeds[10], 3), ROWS // ROWS)
    routes = jax.vmap(lambda own, number: shared_out(jax.random.fold_in(seeds[10], 2), own, number, ROWS, EXPERTS, TOPK, CAP, 2))(routes_keys, routes_turns).reshape((ROWS, TOPK))
    route_weights = jnp.clip(jax.random.uniform(seeds[11], (ROWS, TOPK), jnp.float32, 0.1, 0.6), 0.1, 0.6)
    return {"queries": queries, "latent_cache": latent_cache, "lengths": lengths, "uv_weight": uv_weight, "out_weight": out_weight, "residual": residual, "norm_gain": norm_gain, "gate_weight": gate_weight, "up_weight": up_weight, "down_weight": down_weight, "routes": routes, "route_weights": route_weights}


score_scale = 192.0 ** (-0.5)
epsilon = 1e-06

def attend(query_row, cache_row, row_length):
    scores = jnp.dot(query_row, cache_row.T, preferred_element_type=jnp.float32) * score_scale
    usable = (jnp.arange(cache_row.shape[0], dtype=jnp.int32) < row_length)[None, :]
    peak_score = lax.optimization_barrier(jnp.max(jnp.where(usable, scores, -1e+30), axis=1, keepdims=True))
    exp_scores = jnp.where(usable, jnp.exp(scores - peak_score), 0.0)
    row_total = lax.optimization_barrier(jnp.sum(exp_scores, axis=1, keepdims=True))
    summed = jnp.dot(exp_scores.astype(jnp.bfloat16), cache_row[:, :LAT], preferred_element_type=jnp.float32)
    return (summed / row_total).astype(jnp.bfloat16)

def slot_layout(routes, experts, capacity):
    expert_ids = jnp.arange(experts, dtype=jnp.int32)
    hit_table = lax.optimization_barrier(jnp.sum((routes[:, :, None] == expert_ids[None, None, :]).astype(jnp.int32), axis=1))
    before = jnp.cumsum(hit_table, axis=0) - hit_table
    total_rows = routes.shape[0]
    row_ids = jnp.broadcast_to(jnp.arange(total_rows, dtype=jnp.int32)[:, None], (total_rows, experts))
    column_ids = jnp.broadcast_to(expert_ids[None, :], (total_rows, experts))
    target = jnp.where(hit_table > 0, before, capacity)
    slot_rows = jnp.full((experts, capacity), total_rows, jnp.int32).at[column_ids, target].set(row_ids, mode='drop')
    return (before, slot_rows)

def rms_scaled(rows, norm_gain):
    values = rows.astype(jnp.float32)
    inverse_rms = lax.rsqrt(lax.optimization_barrier(jnp.mean(values * values, axis=1, keepdims=True)) + epsilon)
    return (values * inverse_rms * norm_gain).astype(jnp.bfloat16)

def expert_output(normed, gate_slice, up_slice, down_slice):
    gate_proj = jnp.dot(normed, gate_slice, preferred_element_type=jnp.float32)
    up_proj = jnp.dot(normed, up_slice, preferred_element_type=jnp.float32)
    activated = (jax.nn.silu(gate_proj) * up_proj).astype(jnp.bfloat16)
    result = jnp.zeros((normed.shape[0], D), jnp.float32)
    for group_index in range(N_TP):
        lower = group_index * GROUP
        partial_value = jnp.dot(activated[:, lower:lower + GROUP], down_slice[lower:lower + GROUP], preferred_element_type=jnp.float32).astype(jnp.bfloat16)
        result = result + lax.optimization_barrier(partial_value).astype(jnp.float32)
    return result

def reference(queries, latent_cache, lengths, uv_weight, out_weight, residual, norm_gain, gate_weight, up_weight, down_weight, routes, route_weights):
    context = lax.map(lambda row_parts: attend(row_parts[0], row_parts[1], row_parts[2]), (queries, latent_cache, lengths))
    head_out = jnp.einsum('rhc,hcv->rhv', context.astype(jnp.float32), uv_weight.astype(jnp.float32)).astype(jnp.bfloat16)
    attention = jnp.dot(head_out.reshape(ROWS, H * VHEAD), out_weight, preferred_element_type=jnp.float32)
    hidden = (residual.astype(jnp.float32) + attention).astype(jnp.bfloat16)
    before, slot_rows = slot_layout(routes, EXPERTS, CAP)
    expert_ids = jnp.arange(EXPERTS, dtype=jnp.int32)
    weight_table = lax.optimization_barrier(jnp.sum(route_weights[:, :, None] * (routes[:, :, None] == expert_ids[None, None, :]).astype(jnp.float32), axis=1))
    weight_table = jnp.concatenate([weight_table, jnp.zeros((1, EXPERTS), jnp.float32)], axis=0)
    padded = jnp.concatenate([hidden, jnp.zeros((1, D), jnp.bfloat16)], axis=0)

    def expert_step(moe_total, inputs):
        expert_index, rows_taken, gate_slice, up_slice, down_slice = inputs
        normed = rms_scaled(padded[rows_taken], norm_gain)
        result = expert_output(normed, gate_slice, up_slice, down_slice)
        weight = weight_table[rows_taken, expert_index]
        return (moe_total.at[rows_taken].add(weight[:, None] * result), None)
    moe_total, unused = lax.scan(expert_step, jnp.zeros((ROWS + 1, D), jnp.float32), (expert_ids, slot_rows, gate_weight, up_weight, down_weight))
    return (hidden.astype(jnp.float32) + moe_total[:ROWS]).astype(jnp.bfloat16)
```

```python
import functools

import jax
import jax.numpy as jnp
from jax import lax
from jax.experimental import pallas as pl
from jax.experimental.pallas import tpu as pltpu
from jax.sharding import PartitionSpec as P

F32 = jnp.float32
BF16 = jnp.bfloat16
MESH = pl.DeviceIdType.MESH

LAT = 512
KEY = 576
CTX = 1024
HEADS = 128
OWN_HEADS = 32
VHEAD = 128
ROWS = 512
OWN_ROWS = 4
DP_ROWS = 16
TP_ROWS = 128
D = 7168
COLS = 224
HALF = 112
INNER = 4096
UNITS = 256
DP = 32

score_scale = 192.0 ** (-0.5)
epsilon = 1e-06

RIGHT = (0, 2)
LEFT = (1, 3)
ORDER = (0, 1, 3, 2)


def tn_dot(a, b):
    return lax.dot_general(a, b, (((0,), (0,)), ((), ())), preferred_element_type=F32)


def nt_dot(a, b):
    return lax.dot_general(a, b, (((1,), (1,)), ((), ())), preferred_element_type=F32)


class Place:
    def __init__(self):
        dp = lax.axis_index("dp")
        self.y = lax.axis_index("tp")
        self.d = dp
        self.c = lax.rem(dp, 2)
        self.x = lax.rem(dp // 2, 4)
        self.z = dp // 8

    def device(self, z=None, x=None, c=None, y=None):
        z = self.z if z is None else z
        x = self.x if x is None else x
        c = self.c if c is None else c
        y = self.y if y is None else y
        return ((z * 4 + x) * 2 + c, y)

    def sibling(self):
        return self.device(c=1 - self.c)

    def tp_peer(self, step):
        return self.device(y=lax.rem(self.y + step, 4))

    def first(self, half):
        return self.x if half == 0 else self.z

    def second(self, half):
        return self.z if half == 0 else self.x

    def first_peer(self, half, step):
        if half == 0:
            return self.device(x=lax.rem(self.x + step, 4))
        return self.device(z=lax.rem(self.z + step, 4))

    def second_peer(self, half, step):
        return self.first_peer(1 - half, step)

    def block(self, half, j, k, c):
        a = lax.rem(self.first(half) + j, 4)
        b = lax.rem(self.second(half) + k, 4)
        z, x = (b, a) if half == 0 else (a, b)
        return (z * 4 + x) * 2 + c


def remote(src, dst, send, recv, device):
    return pltpu.make_async_remote_copy(
        src_ref=src, dst_ref=dst, send_sem=send, recv_sem=recv, device_id=device, device_id_type=MESH
    )


def gather_plane(me, blk, send_sem, recv_sem, sib_send, sib_recv):
    sends = []
    count = [0, 0]

    def send(half, j, k, device, rj, rk):
        ref = blk(me.block(half, j, k, me.c), half)
        copy = remote(
            ref, ref, send_sem.at[half, count[half]], recv_sem.at[half, rj * 4 + rk], device
        )
        count[half] += 1
        copy.start()
        sends.append(copy)

    def to_sibling(half, j, k):
        ref = blk(me.block(half, j, k, me.c), half)
        copy = remote(
            ref, ref, sib_send.at[half, j * 4 + k], sib_recv.at[half, j * 4 + k], me.sibling()
        )
        copy.start()
        sends.append(copy)

    def arrived(half, j, k):
        ref = blk(me.block(half, j, k, me.c), half)
        remote(
            ref, ref, send_sem.at[half, 0], recv_sem.at[half, j * 4 + k], me.sibling()
        ).wait_recv()

    def second_axis(half, j):
        send(half, j, 0, me.second_peer(half, 1), j, 3)
        send(half, j, 0, me.second_peer(half, 3), j, 1)

    for half in range(2):
        for step in (1, 3, 2):
            send(half, 0, 0, me.first_peer(half, step), (4 - step) % 4, 0)
    for half in range(2):
        second_axis(half, 0)
        to_sibling(half, 0, 0)
    for j in (1, 3, 2):
        for half in range(2):
            arrived(half, j, 0)
            second_axis(half, j)
            to_sibling(half, j, 0)
    for j in ORDER:
        for half in range(2):
            arrived(half, j, 3)
            if j in RIGHT:
                send(half, j, 3, me.second_peer(half, 1), j, 2)
            to_sibling(half, j, 3)
            arrived(half, j, 1)
            if j in LEFT:
                send(half, j, 1, me.second_peer(half, 3), j, 2)
            to_sibling(half, j, 1)
    for j in ORDER:
        for half in range(2):
            arrived(half, j, 2)
            to_sibling(half, j, 2)
    for half in range(2):
        for j in range(4):
            for k in range(4):
                ref = blk(me.block(half, j, k, 1 - me.c), half)
                remote(
                    ref, ref, sib_send.at[half, 0], sib_recv.at[half, j * 4 + k], me.sibling()
                ).wait_recv()
    return sends


def kernel(
    lengths, q_hbm, cache_hbm, uv_hbm, out_w_hbm, residual_hbm, gain, gate_hbm, up_hbm, down_hbm,
    routes, route_weights, out,
    qv, cv, uv, out_w, res, gate_w, up_w, down_w,
    ctx, by_head, by_head_f, heads_all, part, part_b, part_r, hid, hid_t, gate_acc, up_acc,
    act, contrib, from_sib, pass_r, ring_r, line_r, plane_sum, plane_sum_b, tp_r, weight_row,
    load_sem, a2a_send, a2a_recv, ag_send, ag_recv, ag_sib_send, ag_sib_recv,
    rs_send, rs_recv, hy_send, hy_recv, ah_send, ah_recv, ah_sib_send, ah_sib_recv,
    sib_send, sib_recv, pass_send, pass_recv, ring_send, ring_recv, line_send, line_recv,
    tp_send, tp_recv,
):
    me = Place()
    y, d = me.y, me.d
    own_lanes = pl.ds(pl.multiple_of(y * TP_ROWS, TP_ROWS), TP_ROWS)

    loads = {}

    def load(name, src, dst, index):
        copy = pltpu.make_async_copy(src, dst, load_sem.at[index])
        copy.start()
        loads[name] = copy

    load("q", q_hbm, qv, 0)
    for i in range(OWN_ROWS):
        load(("cache", i), cache_hbm.at[i], cv.at[i], 1 + i)
    load("uv", uv_hbm, uv, 5)
    load("out_w", out_w_hbm, out_w, 6)
    load("res", residual_hbm.at[own_lanes], res, 7)
    load("gate", gate_hbm, gate_w, 8)
    load("up", up_hbm, up_w, 9)
    load("down", down_hbm, down_w, 10)

    barrier = pltpu.get_barrier_semaphore()
    peers = [me.sibling()]
    for step in (1, 2, 3):
        peers += [me.first_peer(0, step), me.first_peer(1, step), me.tp_peer(step)]
    for peer in peers:
        pl.semaphore_signal(barrier, inc=1, device_id=peer, device_id_type=MESH)
    pl.semaphore_wait(barrier, len(peers))

    a2a = []
    loads["q"].wait()
    for i in range(OWN_ROWS):
        loads[("cache", i)].wait()
        scores = nt_dot(qv[i], cv[i]) * score_scale
        usable = lax.broadcasted_iota(jnp.int32, scores.shape, 1) < lengths[i]
        peak = jnp.max(jnp.where(usable, scores, -1e30), axis=1, keepdims=True)
        soft = jnp.where(usable, jnp.exp(scores - peak), 0.0)
        total = jnp.sum(soft, axis=1, keepdims=True)
        summed = jnp.dot(soft.astype(BF16), cv[i, :, :LAT], preferred_element_type=F32)
        ctx[i] = (summed / total).astype(BF16)
        for step in (2, 1, 3):
            peer_y = lax.rem(y + step, 4)
            copy = remote(
                ctx.at[i, pl.ds(pl.multiple_of(peer_y * OWN_HEADS, OWN_HEADS), OWN_HEADS)],
                by_head.at[y * OWN_ROWS + i],
                a2a_send.at[i, step - 1],
                a2a_recv.at[i, step - 1],
                me.tp_peer(step),
            )
            copy.start()
            a2a.append(copy)
        by_head[y * OWN_ROWS + i] = ctx[i, pl.ds(pl.multiple_of(y * OWN_HEADS, OWN_HEADS), OWN_HEADS), :]
    for i in range(OWN_ROWS):
        for step in (1, 2, 3):
            source = lax.rem(y + 4 - step, 4)
            remote(
                ctx.at[i, pl.ds(0, OWN_HEADS)],
                by_head.at[source * OWN_ROWS + i],
                a2a_send.at[i, step - 1],
                a2a_recv.at[i, step - 1],
                me.tp_peer(step),
            ).wait_recv()

    loads["uv"].wait()
    for part_of in range(LAT // 128):
        piece = by_head[:, :, pl.ds(part_of * 128, 128)]
        by_head_f[part_of] = piece.astype(F32).reshape(DP_ROWS * OWN_HEADS, 128)
    own_rows = pl.ds(pl.multiple_of(d * DP_ROWS, DP_ROWS), DP_ROWS)
    for h in range(OWN_HEADS):
        picked = jnp.concatenate(
            [
                by_head_f[part_of, pl.ds(h, DP_ROWS, stride=OWN_HEADS), :]
                for part_of in range(LAT // 128)
            ],
            axis=1,
        ).astype(BF16)
        heads_all[own_rows, pl.ds(h * VHEAD, VHEAD)] = jnp.dot(
            picked, uv[h], preferred_element_type=F32
        ).astype(BF16)

    def head_block(dp, half):
        return heads_all.at[
            pl.ds(pl.multiple_of(dp * DP_ROWS, DP_ROWS), DP_ROWS), pl.ds(half * (INNER // 2), INNER // 2)
        ]

    ag = gather_plane(me, head_block, ag_send, ag_recv, ag_sib_send, ag_sib_recv)

    loads["out_w"].wait()
    part[...] = jnp.zeros_like(part)

    def out_step(k, carry):
        at = pl.ds(pl.multiple_of(k * 512, 512), 512)
        part[...] += jnp.dot(heads_all[:, at], out_w[at, :], preferred_element_type=F32)
        return carry

    lax.fori_loop(0, INNER // 512, out_step, 0)
    part_b[...] = part[...].astype(BF16)
    rs = []
    for step in (2, 1, 3):
        peer_y = lax.rem(y + step, 4)
        copy = remote(
            part_b.at[pl.ds(pl.multiple_of(peer_y * TP_ROWS, TP_ROWS), TP_ROWS)],
            part_r.at[step - 1],
            rs_send.at[step - 1],
            rs_recv.at[step - 1],
            me.tp_peer(step),
        )
        copy.start()
        rs.append(copy)

    loads["gate"].wait()
    loads["up"].wait()

    def gain_step(i, carry):
        at = pl.ds(pl.multiple_of(i * 128, 128), 128)
        column = jnp.broadcast_to(gain[pl.ds(i, 1), :], (128, 128)).T
        wide = jnp.concatenate([column, column], axis=1)
        gate_w[at, :] = (gate_w[at, :].astype(F32) * wide).astype(BF16)
        up_w[at, :] = (up_w[at, :].astype(F32) * wide).astype(BF16)
        return carry

    lax.fori_loop(0, D // 128, gain_step, 0)

    mine = jnp.sum(jnp.where(routes[...] == d, route_weights[...], 0.0), axis=1, keepdims=True)
    weight_row[...] = jnp.broadcast_to(mine, (ROWS, 128)).T[:8, :]

    loads["res"].wait()
    for copy in rs:
        copy.wait_recv()
    total = res[...].astype(F32) + part[own_lanes, :]
    for step in (1, 2, 3):
        total = total + part_r[step - 1].astype(F32)
    hidden = total.astype(BF16).astype(F32)
    hid[...] = hidden
    turned = jnp.concatenate([hidden, jnp.zeros((TP_ROWS, 256 - COLS), F32)], axis=1).T
    own_cols = pl.ds(pl.multiple_of(d * COLS, 16), COLS)
    hid_t[own_cols, own_lanes] = turned[:COLS].astype(BF16)

    hy = []
    for step in (2, 1, 3):
        ref = hid_t.at[own_cols, own_lanes]
        copy = remote(ref, ref, hy_send.at[step - 1], hy_recv.at[step - 1], me.tp_peer(step))
        copy.start()
        hy.append(copy)
    for step in (1, 2, 3):
        source = lax.rem(y + 4 - step, 4)
        ref = hid_t.at[own_cols, pl.ds(pl.multiple_of(source * TP_ROWS, TP_ROWS), TP_ROWS)]
        remote(ref, ref, hy_send.at[step - 1], hy_recv.at[step - 1], me.tp_peer(step)).wait_recv()

    def hidden_block(dp, half):
        return hid_t.at[pl.ds(pl.multiple_of(dp * COLS + half * HALF, 16), HALF), :]

    ah = gather_plane(me, hidden_block, ah_send, ah_recv, ah_sib_send, ah_sib_recv)

    gate_acc[...] = jnp.zeros_like(gate_acc)
    up_acc[...] = jnp.zeros_like(up_acc)

    def expert_step(k, squares):
        at = pl.ds(pl.multiple_of(k * 1024, 1024), 1024)
        rows = hid_t[at, :]
        gate_acc[...] += tn_dot(gate_w[at, :], rows)
        up_acc[...] += tn_dot(up_w[at, :], rows)
        wide = rows.astype(F32)
        return squares + jnp.sum((wide * wide).reshape(128, 8, ROWS), axis=0)

    squares = lax.fori_loop(0, D // 1024, expert_step, jnp.zeros((8, ROWS), F32))
    inverse_rms = lax.rsqrt(jnp.sum(squares, axis=0, keepdims=True) * (1.0 / D) + epsilon)
    gate_proj = gate_acc[...] * inverse_rms
    up_proj = up_acc[...] * inverse_rms
    silu = gate_proj / (1.0 + jnp.exp(-gate_proj))
    act[...] = (silu * up_proj * weight_row[0:1, :]).astype(BF16)

    loads["down"].wait()

    def down_step(k, carry):
        at = pl.ds(pl.multiple_of(k * 256, 256), 256)
        contrib[at, :] = tn_dot(down_w[:, at], act[...]).astype(BF16)
        return carry

    lax.fori_loop(0, D // 256, down_step, 0)

    def share(half, j, k, c):
        dp = me.block(half, j, k, c)
        return contrib.at[pl.ds(pl.multiple_of(dp * COLS + half * HALF, 16), HALF), :]

    back = []

    def start(copy):
        copy.start()
        back.append(copy)

    for k in (2, 1, 3, 0):
        for j in ORDER:
            for half in range(2):
                start(remote(
                    share(half, j, k, 1 - me.c), from_sib.at[half, j * 4 + k],
                    sib_send.at[half, j * 4 + k], sib_recv.at[half, j * 4 + k], me.sibling(),
                ))

    def with_sibling(half, j, k):
        remote(
            share(half, j, k, me.c), from_sib.at[half, j * 4 + k],
            sib_send.at[half, j * 4 + k], sib_recv.at[half, j * 4 + k], me.sibling(),
        ).wait_recv()
        return share(half, j, k, me.c)[...].astype(F32) + from_sib[half, j * 4 + k].astype(F32)

    for j in ORDER:
        for half in range(2):
            ref = share(half, j, 2, me.c)
            ref[...] = with_sibling(half, j, 2).astype(BF16)
            step = 1 if j in RIGHT else 3
            start(remote(
                ref, pass_r.at[half, j], pass_send.at[half, j], pass_recv.at[half, j],
                me.second_peer(half, step),
            ))
    for j in (1, 0, 3, 2):
        for half in range(2):
            for k in (1, 3) if j in LEFT else (3, 1):
                ref = share(half, j, k, me.c)
                value = with_sibling(half, j, k)
                if (j in RIGHT) == (k == 1):
                    remote(
                        ref, pass_r.at[half, j], pass_send.at[half, j], pass_recv.at[half, j],
                        me.sibling(),
                    ).wait_recv()
                    value = value + pass_r[half, j].astype(F32)
                ref[...] = value.astype(BF16)
                slot = j * 2 + (0 if k == 1 else 1)
                start(remote(
                    ref, ring_r.at[half, slot], ring_send.at[half, slot], ring_recv.at[half, slot],
                    me.second_peer(half, k),
                ))
    for j in (1, 3, 2, 0):
        for half in range(2):
            ref = share(half, j, 0, me.c)
            value = with_sibling(half, j, 0)
            for slot in (j * 2, j * 2 + 1):
                remote(
                    ref, ring_r.at[half, slot], ring_send.at[half, slot], ring_recv.at[half, slot],
                    me.sibling(),
                ).wait_recv()
                value = value + ring_r[half, slot].astype(F32)
            if j == 0:
                plane_sum[pl.ds(half * HALF, HALF), :] = value
            else:
                ref[...] = value.astype(BF16)
                start(remote(
                    ref, line_r.at[half, j - 1], line_send.at[half, j - 1], line_recv.at[half, j - 1],
                    me.first_peer(half, j),
                ))
    for half in range(2):
        at = pl.ds(half * HALF, HALF)
        value = plane_sum[at, :]
        for j in (1, 2, 3):
            remote(
                share(half, j, 0, me.c), line_r.at[half, j - 1], line_send.at[half, j - 1],
                line_recv.at[half, j - 1], me.sibling(),
            ).wait_recv()
            value = value + line_r[half, j - 1].astype(F32)
        plane_sum[at, :] = value
        plane_sum_b[at, :] = value.astype(BF16)
    for step in (2, 1, 3):
        peer_y = lax.rem(y + step, 4)
        start(remote(
            plane_sum_b.at[:, pl.ds(pl.multiple_of(peer_y * TP_ROWS, TP_ROWS), TP_ROWS)],
            tp_r.at[step - 1], tp_send.at[step - 1], tp_recv.at[step - 1], me.tp_peer(step),
        ))
    moe = plane_sum[:, own_lanes]
    for step in (1, 2, 3):
        remote(
            plane_sum_b.at[:, own_lanes], tp_r.at[step - 1], tp_send.at[step - 1],
            tp_recv.at[step - 1], me.tp_peer(step),
        ).wait_recv()
        moe = moe + tp_r[step - 1].astype(F32)
    moe = jnp.concatenate([moe, jnp.zeros((256 - COLS, TP_ROWS), F32)], axis=0).T
    out[...] = (hid[...] + moe[:, :COLS]).astype(BF16)

    for copy in a2a + ag + rs + hy + ah + back:
        copy.wait_send()


def local(
    queries, latent_cache, lengths, uv_weight, out_weight, residual, norm_gain,
    gate_weight, up_weight, down_weight, routes, route_weights,
):
    anywhere = pl.BlockSpec(memory_space=pl.ANY)
    vmem = pl.BlockSpec(memory_space=pltpu.VMEM)
    smem = pl.BlockSpec(memory_space=pltpu.SMEM)
    dma = pltpu.SemaphoreType.DMA
    scratch = [
        pltpu.VMEM((OWN_ROWS, HEADS, KEY), BF16),
        pltpu.VMEM((OWN_ROWS, CTX, KEY), BF16),
        pltpu.VMEM((OWN_HEADS, LAT, VHEAD), BF16),
        pltpu.VMEM((INNER, COLS), BF16),
        pltpu.VMEM((TP_ROWS, COLS), BF16),
        pltpu.VMEM((D, UNITS), BF16),
        pltpu.VMEM((D, UNITS), BF16),
        pltpu.VMEM((UNITS, D), BF16),
        pltpu.VMEM((OWN_ROWS, HEADS, LAT), BF16),
        pltpu.VMEM((DP_ROWS, OWN_HEADS, LAT), BF16),
        pltpu.VMEM((LAT // 128, DP_ROWS * OWN_HEADS, 128), F32),
        pltpu.VMEM((ROWS, INNER), BF16),
        pltpu.VMEM((ROWS, COLS), F32),
        pltpu.VMEM((ROWS, COLS), BF16),
        pltpu.VMEM((3, TP_ROWS, COLS), BF16),
        pltpu.VMEM((TP_ROWS, COLS), F32),
        pltpu.VMEM((D, ROWS), BF16),
        pltpu.VMEM((UNITS, ROWS), F32),
        pltpu.VMEM((UNITS, ROWS), F32),
        pltpu.VMEM((UNITS, ROWS), BF16),
        pltpu.VMEM((D, ROWS), BF16),
        pltpu.VMEM((2, 16, HALF, ROWS), BF16),
        pltpu.VMEM((2, 4, HALF, ROWS), BF16),
        pltpu.VMEM((2, 8, HALF, ROWS), BF16),
        pltpu.VMEM((2, 3, HALF, ROWS), BF16),
        pltpu.VMEM((COLS, ROWS), F32),
        pltpu.VMEM((COLS, ROWS), BF16),
        pltpu.VMEM((3, COLS, TP_ROWS), BF16),
        pltpu.VMEM((8, ROWS), F32),
        dma((11,)),
        dma((4, 3)), dma((4, 3)),
        dma((2, 15)), dma((2, 16)), dma((2, 16)), dma((2, 16)),
        dma((3,)), dma((3,)),
        dma((3,)), dma((3,)),
        dma((2, 15)), dma((2, 16)), dma((2, 16)), dma((2, 16)),
        dma((2, 16)), dma((2, 16)),
        dma((2, 4)), dma((2, 4)),
        dma((2, 8)), dma((2, 8)),
        dma((2, 3)), dma((2, 3)),
        dma((3,)), dma((3,)),
    ]
    return pl.pallas_call(
        kernel,
        out_shape=jax.ShapeDtypeStruct((TP_ROWS, COLS), BF16),
        in_specs=[smem] + [anywhere] * 5 + [vmem] + [anywhere] * 3 + [vmem] * 2,
        out_specs=vmem,
        scratch_shapes=scratch,
        compiler_params=pltpu.CompilerParams(
            collective_id=0, has_side_effects=True, vmem_limit_bytes=62 * 1024 * 1024
        ),
        name="decode_step",
    )(
        lengths, queries, latent_cache, uv_weight, out_weight, residual,
        norm_gain.reshape(D // 128, 128),
        gate_weight[0], up_weight[0], down_weight[0], routes, route_weights,
    )


def solution(mesh):
    placed = (
        P(("dp", "tp"), None, None),
        P(("dp", "tp"), None, None),
        P(("dp", "tp")),
        P("tp", None, None),
        P("tp", "dp"),
        P(None, "dp"),
        P(),
        P("dp", None, "tp"),
        P("dp", None, "tp"),
        P("dp", "tp", None),
        P(),
        P(),
    )
    return jax.shard_map(
        local, mesh=mesh, in_specs=placed, out_specs=P("tp", "dp"), check_vma=False
    )
```

```python
import functools

import jax
import jax.numpy as jnp
from jax import lax
from jax.experimental import pallas as pl
from jax.experimental.pallas import tpu as pltpu
from jax.sharding import PartitionSpec as P

F32 = jnp.float32
BF16 = jnp.bfloat16
MESH = pl.DeviceIdType.MESH

LAT = 512
KEY = 576
CTX = 1024
HEADS = 128
OWN_HEADS = 32
VHEAD = 128
ROWS = 512
OWN_ROWS = 4
DP_ROWS = 16
TP_ROWS = 128
D = 7168
COLS = 224
PART_A = 96
PART_B = 128
INNER = 4096
UNITS = 256
DP = 32

score_scale = 192.0 ** (-0.5)
epsilon = 1e-06

RIGHT = (0, 2)
LEFT = (1, 3)
ORDER = (0, 1, 3, 2)


def tn_dot(a, b):
    return lax.dot_general(a, b, (((0,), (0,)), ((), ())), preferred_element_type=F32)


def nt_dot(a, b):
    return lax.dot_general(a, b, (((1,), (1,)), ((), ())), preferred_element_type=F32)


class Place:
    def __init__(self):
        dp = lax.axis_index("dp")
        self.y = lax.axis_index("tp")
        self.d = dp
        self.c = lax.rem(dp, 2)
        self.x = lax.rem(dp // 2, 4)
        self.z = dp // 8

    def device(self, z=None, x=None, c=None, y=None):
        z = self.z if z is None else z
        x = self.x if x is None else x
        c = self.c if c is None else c
        y = self.y if y is None else y
        return ((z * 4 + x) * 2 + c, y)

    def sibling(self):
        return self.device(c=1 - self.c)

    def tp_peer(self, step):
        return self.device(y=lax.rem(self.y + step, 4))

    def first(self, half):
        return self.x if half == 0 else self.z

    def second(self, half):
        return self.z if half == 0 else self.x

    def first_peer(self, half, step):
        if half == 0:
            return self.device(x=lax.rem(self.x + step, 4))
        return self.device(z=lax.rem(self.z + step, 4))

    def second_peer(self, half, step):
        return self.first_peer(1 - half, step)

    def lanes(self, step):
        at = lax.rem(self.y + step, 4) * TP_ROWS
        return pl.ds(pl.multiple_of(at, TP_ROWS), TP_ROWS)

    def at(self, dz, dx, c):
        return (lax.rem(self.z + dz, 4) * 4 + lax.rem(self.x + dx, 4)) * 2 + c

    def block(self, half, j, k, c):
        a = lax.rem(self.first(half) + j, 4)
        b = lax.rem(self.second(half) + k, 4)
        z, x = (b, a) if half == 0 else (a, b)
        return (z * 4 + x) * 2 + c


def remote(src, dst, send, recv, device):
    return pltpu.make_async_remote_copy(
        src_ref=src, dst_ref=dst, send_sem=send, recv_sem=recv, device_id=device, device_id_type=MESH
    )


def rows_of(dp, offset, count):
    return pl.ds(pl.multiple_of(dp * COLS + offset, 16), count)


def gather_plane(me, blk, start, sems, landed):
    send_sem, recv_sem = sems
    count = [0, 0]

    def ref_of(half, j, k):
        return blk(half, me.block(half, j, k, me.c))

    def send(half, j, k, device, rj, rk):
        ref = ref_of(half, j, k)
        start(remote(
            ref, ref, send_sem.at[half, count[half]], recv_sem.at[half, rj * 4 + rk], device
        ))
        count[half] += 1

    def arrived(half, j, k):
        ref = ref_of(half, j, k)
        remote(
            ref, ref, send_sem.at[half, 0], recv_sem.at[half, j * 4 + k], me.sibling()
        ).wait_recv()

    def second_axis(half, j):
        send(half, j, 0, me.second_peer(half, 1), j, 3)
        send(half, j, 0, me.second_peer(half, 3), j, 1)

    for half in range(2):
        send(half, 0, 0, me.first_peer(half, 1), 3, 0)
        send(half, 0, 0, me.first_peer(half, 3), 1, 0)
    for half in range(2):
        second_axis(half, 0)
    for half in range(2):
        landed(half, 0, 0)
    yield
    for half in range(2):
        arrived(half, 1, 0)
        arrived(half, 3, 0)
        send(half, 3 - 2 * me.c, 0, me.first_peer(half, 1 + 2 * me.c), 2, 0)
    for half in range(2):
        second_axis(half, 1)
        second_axis(half, 3)
    for half in range(2):
        landed(half, 1, 0)
        landed(half, 3, 0)
    yield

    def second_arrivals(j):
        for half in range(2):
            arrived(half, j, 3)
            if j in RIGHT:
                send(half, j, 3, me.second_peer(half, 1), j, 2)
            arrived(half, j, 1)
            if j in LEFT:
                send(half, j, 1, me.second_peer(half, 3), j, 2)
        for half in range(2):
            landed(half, j, 3)
            landed(half, j, 1)

    second_arrivals(0)
    yield
    for half in range(2):
        arrived(half, 2, 0)
        second_axis(half, 2)
    for half in range(2):
        landed(half, 2, 0)
    yield
    for j in (1, 3, 2):
        second_arrivals(j)
        yield
    for j in ORDER:
        for half in range(2):
            arrived(half, j, 2)
            landed(half, j, 2)
        yield


def scatter_plane(me, own, touch, finish, start, bufs, sems):
    pass_r, ring_r, line_r = bufs
    pass_send, pass_recv, ring_send, ring_recv, line_send, line_recv = sems

    def far(half, j, step):
        return remote(
            own(half, j, 2), pass_r.at[half, j], pass_send.at[half, j], pass_recv.at[half, j],
            me.second_peer(half, step),
        )

    def near(half, j, k):
        slot = j * 2 + (0 if k == 1 else 1)
        return remote(
            own(half, j, k), ring_r.at[half, slot], ring_send.at[half, slot],
            ring_recv.at[half, slot], me.second_peer(half, k),
        )

    def line(half, j, slot, step):
        return remote(
            own(half, j, 0), line_r.at[half, slot], line_send.at[half, slot],
            line_recv.at[half, slot], me.first_peer(half, step),
        )

    for j in ORDER:
        for half in range(2):
            own(half, j, 2)[...] = touch(half, j, 2).astype(BF16)
            start(far(half, j, 1 if j in RIGHT else 3))
        yield
    for j in ORDER:
        for half in range(2):
            for k in (1, 3) if j in LEFT else (3, 1):
                value = touch(half, j, k)
                if (j in RIGHT) == (k == 1):
                    far(half, j, 1).wait_recv()
                    value = value + pass_r[half, j].astype(F32)
                own(half, j, k)[...] = value.astype(BF16)
                start(near(half, j, k))
        yield

    def gathered(half, j):
        value = touch(half, j, 0)
        for k in (1, 3):
            near(half, j, k).wait_recv()
            value = value + ring_r[half, j * 2 + (0 if k == 1 else 1)].astype(F32)
        return value

    straight, added = 3 - 2 * me.c, 1 + 2 * me.c
    for half in range(2):
        own(half, 2, 0)[...] = gathered(half, 2).astype(BF16)
        start(line(half, 2, 2, added))
    yield
    for half in range(2):
        for j in (1, 3):
            own(half, j, 0)[...] = gathered(half, j).astype(BF16)
        start(line(half, straight, 0, straight))
    yield
    for half in range(2):
        line(half, 2, 2, added).wait_recv()
        ref = own(half, added, 0)
        ref[...] = (ref[...].astype(F32) + line_r[half, 2].astype(F32)).astype(BF16)
        start(line(half, added, 1, added))
    yield
    for half in range(2):
        value = gathered(half, 0)
        for slot in range(2):
            line(half, 0, slot, 1).wait_recv()
            value = value + line_r[half, slot].astype(F32)
        finish(half, value)
    yield


def kernel(
    lengths, q_hbm, cache_hbm, uv_hbm, out_w_hbm, residual_hbm, gain, gate_hbm, up_hbm, down_hbm,
    routes, route_weights, out,
    qv, cv, uv, out_w, res, down_w, gate_up_t, down_t,
    ctx, by_head, by_head_f, heads_all, part, part_b, part_r, hid, hid_t, gate_up,
    act, contrib, from_sib, plane_sum, plane_sum_b, tp_r, weight_row,
    b_pass, b_ring, b_line, a_pass, a_ring, a_line, a_sum, ya_pass, ya_ring,
    load_sem, a2a_send, a2a_recv, ag_send, ag_recv, ag_sib_send, ag_sib_recv,
    rs_send, rs_recv, hy_send, hy_recv,
    ga_send, ga_recv, gy_send, gy_recv, ga_sib_send, ga_sib_recv,
    gb_send, gb_recv, gb_sib_send, gb_sib_recv,
    sib_send, sib_recv, yp_send, yp_recv, yr_send, yr_recv,
    ap_send, ap_recv, ar_send, ar_recv, al_send, al_recv,
    bp_send, bp_recv, br_send, br_recv, bl_send, bl_recv,
    tp_send, tp_recv,
):
    me = Place()
    y, d = me.y, me.d
    own_lanes = pl.ds(pl.multiple_of(y * TP_ROWS, TP_ROWS), TP_ROWS)

    loads = {}
    sent = []

    def load(name, src, dst, index):
        copy = pltpu.make_async_copy(src, dst, load_sem.at[index])
        copy.start()
        loads[name] = copy

    def ready(name):
        loads.pop(name).wait()

    def start(copy):
        copy.start()
        sent.append(copy)

    load("q", q_hbm, qv, 0)
    for i in range(OWN_ROWS):
        load(("cache", i), cache_hbm.at[i], cv.at[i], 1 + i)

    barrier = pltpu.get_barrier_semaphore()
    peers = [me.sibling()]
    for step in (1, 2, 3):
        peers += [me.first_peer(0, step), me.first_peer(1, step), me.tp_peer(step)]
    for peer in peers:
        pl.semaphore_signal(barrier, inc=1, device_id=peer, device_id_type=MESH)
    pl.semaphore_wait(barrier, len(peers))

    ready("q")
    for i in range(OWN_ROWS):
        ready(("cache", i))
        if i == 1:
            load("uv", uv_hbm, uv, 5)
            load("out_w", out_w_hbm, out_w, 6)
            load("res", residual_hbm.at[:, own_lanes], res, 7)
        if i == 2:
            load("gate", gate_hbm, contrib.at[:, pl.ds(0, UNITS)], 8)
            load("up", up_hbm, contrib.at[:, pl.ds(UNITS, UNITS)], 9)
            load("down", down_hbm, down_w, 10)
        scores = tn_dot(qv[i], cv[i]) * score_scale
        usable = lax.broadcasted_iota(jnp.int32, scores.shape, 1) < lengths[i]
        peak = jnp.max(jnp.where(usable, scores, -1e30), axis=1, keepdims=True)
        soft = jnp.where(usable, jnp.exp(scores - peak), 0.0)
        total = jnp.sum(soft, axis=1, keepdims=True)
        summed = nt_dot(soft.astype(BF16), cv[i, :LAT, :])
        ctx[i] = (summed / total).astype(BF16)
        for step in (2, 1, 3):
            peer_y = lax.rem(y + step, 4)
            start(remote(
                ctx.at[i, pl.ds(pl.multiple_of(peer_y * OWN_HEADS, OWN_HEADS), OWN_HEADS)],
                by_head.at[y * OWN_ROWS + i],
                a2a_send.at[i, step - 1],
                a2a_recv.at[i, step - 1],
                me.tp_peer(step),
            ))
        by_head[y * OWN_ROWS + i] = ctx[i, pl.ds(pl.multiple_of(y * OWN_HEADS, OWN_HEADS), OWN_HEADS), :]
    for i in range(OWN_ROWS):
        for step in (1, 2, 3):
            source = lax.rem(y + 4 - step, 4)
            remote(
                ctx.at[i, pl.ds(0, OWN_HEADS)],
                by_head.at[source * OWN_ROWS + i],
                a2a_send.at[i, step - 1],
                a2a_recv.at[i, step - 1],
                me.tp_peer(step),
            ).wait_recv()

    ready("uv")
    for part_of in range(LAT // 128):
        piece = by_head[:, :, pl.ds(part_of * 128, 128)]
        by_head_f[part_of] = piece.astype(F32).reshape(DP_ROWS * OWN_HEADS, 128)
    own_rows = pl.ds(pl.multiple_of(d * DP_ROWS, DP_ROWS), DP_ROWS)
    for h in range(OWN_HEADS):
        picked = jnp.concatenate(
            [
                by_head_f[part_of, pl.ds(h, DP_ROWS, stride=OWN_HEADS), :]
                for part_of in range(LAT // 128)
            ],
            axis=1,
        ).astype(BF16)
        heads_all[own_rows, pl.ds(h * VHEAD, VHEAD)] = jnp.dot(
            picked, uv[h], preferred_element_type=F32
        ).astype(BF16)

    def head_block(half, dp):
        return heads_all.at[
            pl.ds(pl.multiple_of(dp * DP_ROWS, DP_ROWS), DP_ROWS), pl.ds(half * (INNER // 2), INNER // 2)
        ]

    def head_sibling(half, j, k, c):
        ref = head_block(half, me.block(half, j, k, c))
        return remote(
            ref, ref, ag_sib_send.at[half, j * 4 + k], ag_sib_recv.at[half, j * 4 + k], me.sibling()
        )

    def turn_step(i, carry):
        at = pl.ds(pl.multiple_of(i * 128, 128), 128)
        turned = contrib[at, :].astype(F32).T * gain[pl.ds(i, 1), :]
        gate_up_t[:, at] = turned.astype(BF16)
        down_t[at, :] = down_w[:, at].astype(F32).T.astype(BF16)
        return carry

    turned_to = 0
    for step in gather_plane(
        me, head_block, start, (ag_send, ag_recv), lambda *at: start(head_sibling(*at, me.c))
    ):
        if turned_to == 0:
            ready("gate")
            ready("up")
            ready("down")
        upto = min(turned_to + 7, D // 128)
        lax.fori_loop(turned_to, upto, turn_step, 0)
        turned_to = upto
    for half in range(2):
        for j in range(4):
            for k in range(4):
                head_sibling(half, j, k, 1 - me.c).wait_recv()

    ready("out_w")
    part[...] = jnp.zeros_like(part)

    def out_step(k, carry):
        at = pl.ds(pl.multiple_of(k * 512, 512), 512)
        part[...] += nt_dot(out_w[:, at], heads_all[:, at])
        return carry

    lax.fori_loop(0, INNER // 512, out_step, 0)
    for block in range(4):
        part_b[block] = part[:, block * TP_ROWS : (block + 1) * TP_ROWS].astype(BF16)
    for step in (2, 1, 3):
        start(remote(
            part_b.at[lax.rem(y + step, 4)], part_r.at[step - 1],
            rs_send.at[step - 1], rs_recv.at[step - 1], me.tp_peer(step),
        ))

    weight_row[...] = jnp.sum(
        jnp.where(routes[...] == d, route_weights[...], 0.0), axis=0, keepdims=True
    )

    ready("res")
    total = res[...].astype(F32) + part[:, own_lanes]
    for step in (1, 2, 3):
        remote(
            part_b.at[0], part_r.at[step - 1], rs_send.at[step - 1], rs_recv.at[step - 1],
            me.tp_peer(step),
        ).wait_recv()
        total = total + part_r[step - 1].astype(F32)
    hidden = total.astype(BF16)
    hid[...] = hidden.astype(F32)
    own_cols = pl.ds(pl.multiple_of(d * COLS, 16), COLS)
    hid_t[own_cols, own_lanes] = hidden

    pairs = [(dz, dx) for dz in range(4) for dx in range(4)]

    def a_block(half, dp):
        return hid_t.at[rows_of(dp, half * (PART_A // 2), PART_A // 2), own_lanes]

    def b_block(half, dp):
        return hid_t.at[rows_of(dp, PART_A + half * (PART_B // 2), PART_B // 2), :]

    def pair_of(half, j, k):
        return (k, j) if half == 0 else (j, k)

    def a_tp(pair, slot, lanes, step):
        ref = hid_t.at[rows_of(me.at(*pair, me.c), 0, PART_A), lanes]
        n = pair[0] * 4 + pair[1]
        return remote(ref, ref, gy_send.at[n, slot], gy_recv.at[n, slot], me.tp_peer(step))

    def a_sibling(pair, c):
        ref = hid_t.at[rows_of(me.at(*pair, c), 0, PART_A), :]
        n = pair[0] * 4 + pair[1]
        return remote(ref, ref, ga_sib_send.at[n], ga_sib_recv.at[n], me.sibling())

    a_halves, a_landed = set(), []

    def a_here(half, j, k):
        pair = pair_of(half, j, k)
        if pair in a_halves:
            a_landed.append(pair)
            start(a_tp(pair, 0, me.lanes(0), 1))
            start(a_tp(pair, 1, me.lanes(0), 3))
        a_halves.add(pair)

    a_passed, a_done = [0], [0]

    def a_pass_on(count):
        for pair in a_landed[a_passed[0] : a_passed[0] + count]:
            if sum(pair) % 2 == 0:
                a_tp(pair, 0, me.lanes(3), 1).wait_recv()
                start(a_tp(pair, 2, me.lanes(3), 1))
            else:
                a_tp(pair, 1, me.lanes(1), 3).wait_recv()
                start(a_tp(pair, 2, me.lanes(1), 3))
        a_passed[0] += count

    def a_finish(count):
        for pair in a_landed[a_done[0] : a_done[0] + count]:
            slot, step = (1, 1) if sum(pair) % 2 == 0 else (0, 3)
            a_tp(pair, slot, me.lanes(step), step).wait_recv()
            a_tp(pair, 2, me.lanes(2), 1).wait_recv()
            start(a_sibling(pair, me.c))
        a_done[0] += count

    def b_sibling(half, j, k, c):
        ref = b_block(half, me.block(half, j, k, c))
        return remote(
            ref, ref, gb_sib_send.at[half, j * 4 + k], gb_sib_recv.at[half, j * 4 + k], me.sibling()
        )

    def b_tp(slot, lanes, step):
        ref = hid_t.at[rows_of(d, PART_A, PART_B), lanes]
        return remote(ref, ref, hy_send.at[slot], hy_recv.at[slot], me.tp_peer(step))

    a_plane = gather_plane(me, a_block, start, (ga_send, ga_recv), a_here)
    b_plane = gather_plane(
        me, b_block, start, (gb_send, gb_recv), lambda *at: start(b_sibling(*at, me.c))
    )
    start(b_tp(0, me.lanes(0), 1))
    start(b_tp(1, me.lanes(0), 3))
    next(a_plane)
    b_tp(0, me.lanes(3), 1).wait_recv()
    b_tp(1, me.lanes(1), 1).wait_recv()
    start(b_tp(2, me.lanes(3 - 2 * me.c), 1 + 2 * me.c))
    next(a_plane)
    a_pass_on(1)
    b_tp(2, me.lanes(2), 1).wait_recv()
    next(b_plane)
    for _ in range(5):
        next(a_plane)
    next(b_plane)
    for _ in range(4):
        next(a_plane)
    for _ in range(2):
        next(b_plane)
        a_pass_on(3)
    for _ in range(3):
        next(b_plane)
        a_pass_on(3)
        a_finish(3)
    for _ in range(4):
        next(b_plane)
        a_finish(2)
    a_finish(16 - a_done[0])
    for half in range(2):
        for j in range(4):
            for k in range(4):
                b_sibling(half, j, k, 1 - me.c).wait_recv()
    for pair in pairs:
        a_sibling(pair, 1 - me.c).wait_recv()

    gate_up[...] = jnp.zeros_like(gate_up)

    def expert_step(k, squares):
        at = pl.ds(pl.multiple_of(k * 1024, 1024), 1024)
        rows = hid_t[at, :]
        gate_up[...] += jnp.dot(gate_up_t[:, at], rows, preferred_element_type=F32)
        wide = rows.astype(F32)
        return squares + jnp.sum((wide * wide).reshape(128, 8, ROWS), axis=0)

    squares = lax.fori_loop(0, D // 1024, expert_step, jnp.zeros((8, ROWS), F32))
    inverse_rms = lax.rsqrt(jnp.sum(squares, axis=0, keepdims=True) * (1.0 / D) + epsilon)
    gate_proj = gate_up[:UNITS, :] * inverse_rms
    up_proj = gate_up[UNITS:, :] * inverse_rms
    silu = gate_proj / (1.0 + jnp.exp(-gate_proj))
    act[...] = (silu * up_proj * weight_row[...]).astype(BF16)

    def from_core(pair, c):
        n = pair[0] * 4 + pair[1]
        return remote(
            contrib.at[rows_of(me.at(*pair, c), 0, COLS), :], from_sib.at[n],
            sib_send.at[n], sib_recv.at[n], me.sibling(),
        )

    def compute(pair):
        at = pl.ds(pl.multiple_of(me.at(*pair, 0) * COLS, 16), 2 * COLS)
        contrib[at, :] = jnp.dot(down_t[at, :], act[...], preferred_element_type=F32).astype(BF16)
        start(from_core(pair, 1 - me.c))

    sib_here = set()

    def sibling_here(pair):
        if pair not in sib_here:
            sib_here.add(pair)
            from_core(pair, me.c).wait_recv()

    def ya_far(pair, step):
        n = pair[0] * 4 + pair[1]
        return remote(
            contrib.at[rows_of(me.at(*pair, me.c), 0, PART_A), me.lanes(2)], ya_pass.at[n],
            yp_send.at[n], yp_recv.at[n], me.tp_peer(step),
        )

    def ya_near(pair, step):
        n = pair[0] * 4 + pair[1]
        slot = 0 if step == 1 else 1
        return remote(
            contrib.at[rows_of(me.at(*pair, me.c), 0, PART_A), me.lanes(step)], ya_ring.at[n, slot],
            yr_send.at[n, slot], yr_recv.at[n, slot], me.tp_peer(step),
        )

    def a_first(pair):
        sibling_here(pair)
        at = rows_of(me.at(*pair, me.c), 0, PART_A)
        theirs = from_sib[pair[0] * 4 + pair[1], :PART_A, :]
        contrib[at, :] = (contrib[at, :].astype(F32) + theirs.astype(F32)).astype(BF16)
        far_step = 1 if sum(pair) % 2 == 0 else 3
        start(ya_far(pair, far_step))
        start(ya_near(pair, 4 - far_step))

    def a_second(pair):
        step = 1 if sum(pair) % 2 == 0 else 3
        ya_far(pair, step).wait_recv()
        at = rows_of(me.at(*pair, me.c), 0, PART_A)
        passed = ya_pass[pair[0] * 4 + pair[1]].astype(F32)
        contrib[at, me.lanes(step)] = (contrib[at, me.lanes(step)].astype(F32) + passed).astype(BF16)
        start(ya_near(pair, step))

    def a_third(pair):
        n = pair[0] * 4 + pair[1]
        value = contrib[rows_of(me.at(*pair, me.c), 0, PART_A), own_lanes].astype(F32)
        for step in (1, 3):
            ya_near(pair, step).wait_recv()
            value = value + ya_ring[n, 0 if step == 1 else 1].astype(F32)
        a_sum[n] = value.astype(BF16)

    def a_own(half, j, k):
        a = lax.rem(me.first(half) + j, 4)
        b = lax.rem(me.second(half) + k, 4)
        dz, dx = (k, j) if half == 0 else (j, k)
        return a_sum.at[dz * 4 + dx, pl.ds(half * (PART_A // 2), PART_A // 2), :]

    def a_touch(half, j, k):
        return a_own(half, j, k)[...].astype(F32)

    def a_final(half, value):
        at = pl.ds(half * (PART_A // 2), PART_A // 2)
        out[at, :] = (hid[at, :] + value).astype(BF16)

    def b_own(half, j, k):
        return contrib.at[
            rows_of(me.block(half, j, k, me.c), PART_A + half * (PART_B // 2), PART_B // 2), :
        ]

    def b_touch(half, j, k):
        pair = pair_of(half, j, k)
        sibling_here(pair)
        theirs = from_sib[
            pair[0] * 4 + pair[1], pl.ds(PART_A + half * (PART_B // 2), PART_B // 2), :
        ]
        return b_own(half, j, k)[...].astype(F32) + theirs.astype(F32)

    def b_final(half, value):
        at = pl.ds(half * (PART_B // 2), PART_B // 2)
        plane_sum[at, :] = value
        plane_sum_b[at, :] = value.astype(BF16)

    a_back = scatter_plane(
        me, a_own, a_touch, a_final, start, (a_pass, a_ring, a_line),
        (ap_send, ap_recv, ar_send, ar_recv, al_send, al_recv),
    )
    b_back = scatter_plane(
        me, b_own, b_touch, b_final, start, (b_pass, b_ring, b_line),
        (bp_send, bp_recv, br_send, br_recv, bl_send, bl_recv),
    )
    order = [(2, 2), (2, 0), (0, 2), (2, 1), (1, 2), (2, 3), (3, 2)]
    order += [pair for pair in pairs if pair not in order]
    for n, pair in enumerate(order):
        compute(pair)
        if n >= 8:
            a_first(order[n - 8])
    for n in range(4):
        next(b_back)
        a_first(order[8 + 2 * n])
        a_first(order[9 + 2 * n])
        a_second(order[2 * n])
        a_second(order[2 * n + 1])
    for n in range(4):
        next(b_back)
        a_second(order[8 + 2 * n])
        a_second(order[9 + 2 * n])
        a_third(order[2 * n])
        a_third(order[2 * n + 1])
    for _ in range(2):
        next(b_back)
    for _ in range(4):
        next(a_back)
    for n in range(8, 16):
        a_third(order[n])
    next(b_back)
    for _ in range(4):
        next(a_back)
    next(b_back)

    def b_tp_sum(step):
        return remote(
            plane_sum_b.at[:, me.lanes(step)], tp_r.at[step - 1],
            tp_send.at[step - 1], tp_recv.at[step - 1], me.tp_peer(step),
        )

    for step in (2, 1, 3):
        start(b_tp_sum(step))
    for _ in range(4):
        next(a_back)
    moe = plane_sum[:, own_lanes]
    for step in (1, 2, 3):
        b_tp_sum(step).wait_recv()
        moe = moe + tp_r[step - 1].astype(F32)
    out[PART_A:, :] = (hid[PART_A:, :] + moe).astype(BF16)

    for copy in sent:
        copy.wait_send()


def local(
    queries, latent_cache, lengths, uv_weight, out_weight, residual, norm_gain,
    gate_weight, up_weight, down_weight, routes, route_weights,
):
    anywhere = pl.BlockSpec(memory_space=pl.ANY)
    vmem = pl.BlockSpec(memory_space=pltpu.VMEM)
    smem = pl.BlockSpec(memory_space=pltpu.SMEM)
    dma = pltpu.SemaphoreType.DMA
    scratch = [
        pltpu.VMEM((OWN_ROWS, KEY, HEADS), BF16),
        pltpu.VMEM((OWN_ROWS, KEY, CTX), BF16),
        pltpu.VMEM((OWN_HEADS, LAT, VHEAD), BF16),
        pltpu.VMEM((COLS, INNER), BF16),
        pltpu.VMEM((COLS, TP_ROWS), BF16),
        pltpu.VMEM((UNITS, D), BF16),
        pltpu.VMEM((2 * UNITS, D), BF16),
        pltpu.VMEM((D, UNITS), BF16),
        pltpu.VMEM((OWN_ROWS, HEADS, LAT), BF16),
        pltpu.VMEM((DP_ROWS, OWN_HEADS, LAT), BF16),
        pltpu.VMEM((LAT // 128, DP_ROWS * OWN_HEADS, 128), F32),
        pltpu.VMEM((ROWS, INNER), BF16),
        pltpu.VMEM((COLS, ROWS), F32),
        pltpu.VMEM((4, COLS, TP_ROWS), BF16),
        pltpu.VMEM((3, COLS, TP_ROWS), BF16),
        pltpu.VMEM((COLS, TP_ROWS), F32),
        pltpu.VMEM((D, ROWS), BF16),
        pltpu.VMEM((2 * UNITS, ROWS), F32),
        pltpu.VMEM((UNITS, ROWS), BF16),
        pltpu.VMEM((D, ROWS), BF16),
        pltpu.VMEM((16, COLS, ROWS), BF16),
        pltpu.VMEM((PART_B, ROWS), F32),
        pltpu.VMEM((PART_B, ROWS), BF16),
        pltpu.VMEM((3, PART_B, TP_ROWS), BF16),
        pltpu.VMEM((1, ROWS), F32),
        pltpu.VMEM((2, 4, PART_B // 2, ROWS), BF16),
        pltpu.VMEM((2, 8, PART_B // 2, ROWS), BF16),
        pltpu.VMEM((2, 3, PART_B // 2, ROWS), BF16),
        pltpu.VMEM((2, 4, PART_A // 2, TP_ROWS), BF16),
        pltpu.VMEM((2, 8, PART_A // 2, TP_ROWS), BF16),
        pltpu.VMEM((2, 3, PART_A // 2, TP_ROWS), BF16),
        pltpu.VMEM((16, PART_A, TP_ROWS), BF16),
        pltpu.VMEM((16, PART_A, TP_ROWS), BF16),
        pltpu.VMEM((16, 2, PART_A, TP_ROWS), BF16),
        dma((11,)),
        dma((4, 3)), dma((4, 3)),
        dma((2, 15)), dma((2, 16)), dma((2, 16)), dma((2, 16)),
        dma((3,)), dma((3,)),
        dma((3,)), dma((3,)),
        dma((2, 15)), dma((2, 16)), dma((16, 3)), dma((16, 3)), dma((16,)), dma((16,)),
        dma((2, 15)), dma((2, 16)), dma((2, 16)), dma((2, 16)),
        dma((16,)), dma((16,)), dma((16,)), dma((16,)), dma((16, 2)), dma((16, 2)),
        dma((2, 4)), dma((2, 4)), dma((2, 8)), dma((2, 8)), dma((2, 3)), dma((2, 3)),
        dma((2, 4)), dma((2, 4)), dma((2, 8)), dma((2, 8)), dma((2, 3)), dma((2, 3)),
        dma((3,)), dma((3,)),
    ]
    return pl.pallas_call(
        kernel,
        out_shape=jax.ShapeDtypeStruct((COLS, TP_ROWS), BF16),
        in_specs=[smem] + [anywhere] * 5 + [vmem] + [anywhere] * 3 + [vmem] * 2,
        out_specs=vmem,
        scratch_shapes=scratch,
        compiler_params=pltpu.CompilerParams(
            collective_id=0, has_side_effects=True, vmem_limit_bytes=62 * 1024 * 1024
        ),
        name="decode_step",
    )(
        lengths, jnp.swapaxes(queries, 1, 2), jnp.swapaxes(latent_cache, 1, 2), uv_weight,
        out_weight.T, residual.T, norm_gain.reshape(D // 128, 128),
        gate_weight[0], up_weight[0], down_weight[0], routes.T, route_weights.T,
    ).T


def solution(mesh):
    placed = (
        P(("dp", "tp"), None, None),
        P(("dp", "tp"), None, None),
        P(("dp", "tp")),
        P("tp", None, None),
        P("tp", "dp"),
        P(None, "dp"),
        P(),
        P("dp", None, "tp"),
        P("dp", None, "tp"),
        P("dp", "tp", None),
        P(),
        P(),
    )
    return jax.shard_map(
        local, mesh=mesh, in_specs=placed, out_specs=P("tp", "dp"), check_vma=False
    )
```

```python
import functools

import jax
import jax.numpy as jnp
from jax import lax
from jax.experimental import pallas as pl
from jax.experimental.pallas import tpu as pltpu
from jax.sharding import PartitionSpec as P

F32 = jnp.float32
BF16 = jnp.bfloat16
MESH = pl.DeviceIdType.MESH

LAT = 512
KEY = 576
CTX = 1024
HEADS = 128
OWN_HEADS = 32
VHEAD = 128
ROWS = 512
OWN_ROWS = 4
DP_ROWS = 16
TP_ROWS = 128
D = 7168
COLS = 224
PART_A = 96
PART_B = 128
INNER = 4096
UNITS = 256
DP = 32

score_scale = 192.0 ** (-0.5)
epsilon = 1e-06

SUM_A = 64
SUM_B = 160
PASSED = 10
SUM_PASSED = 8


def tn_dot(a, b):
    return lax.dot_general(a, b, (((0,), (0,)), ((), ())), preferred_element_type=F32)


def nt_dot(a, b):
    return lax.dot_general(a, b, (((1,), (1,)), ((), ())), preferred_element_type=F32)


class Place:
    def __init__(self):
        dp = lax.axis_index("dp")
        self.y = lax.axis_index("tp")
        self.d = dp
        self.c = lax.rem(dp, 2)
        self.x = lax.rem(dp // 2, 4)
        self.z = dp // 8

    def device(self, z=None, x=None, c=None, y=None):
        z = self.z if z is None else z
        x = self.x if x is None else x
        c = self.c if c is None else c
        y = self.y if y is None else y
        return ((z * 4 + x) * 2 + c, y)

    def sibling(self):
        return self.device(c=1 - self.c)

    def tp_peer(self, step):
        return self.device(y=lax.rem(self.y + step, 4))

    def first(self, half):
        return self.x if half == 0 else self.z

    def second(self, half):
        return self.z if half == 0 else self.x

    def first_peer(self, half, step):
        if half == 0:
            return self.device(x=lax.rem(self.x + step, 4))
        return self.device(z=lax.rem(self.z + step, 4))

    def second_peer(self, half, step):
        return self.first_peer(1 - half, step)

    def lanes(self, step):
        at = lax.rem(self.y + step, 4) * TP_ROWS
        return pl.ds(pl.multiple_of(at, TP_ROWS), TP_ROWS)

    def at(self, dz, dx, c):
        return (lax.rem(self.z + dz, 4) * 4 + lax.rem(self.x + dx, 4)) * 2 + c

    def block(self, half, j, k, c):
        a = lax.rem(self.first(half) + j, 4)
        b = lax.rem(self.second(half) + k, 4)
        z, x = (b, a) if half == 0 else (a, b)
        return (z * 4 + x) * 2 + c


def remote(src, dst, send, recv, device):
    return pltpu.make_async_remote_copy(
        src_ref=src, dst_ref=dst, send_sem=send, recv_sem=recv, device_id=device, device_id_type=MESH
    )


def rows_of(dp, offset, count):
    return pl.ds(pl.multiple_of(dp * COLS + offset, 16), count)


def gather_plane(me, blk, start, sems, landed):
    send_sem, recv_sem = sems
    count = [0, 0]

    def ref_of(half, j, k):
        return blk(half, me.block(half, j, k, me.c))

    def send(half, j, k, device, rj, rk):
        ref = ref_of(half, j, k)
        start(remote(
            ref, ref, send_sem.at[half, count[half]], recv_sem.at[half, rj * 4 + rk], device
        ))
        count[half] += 1

    def arrived(half, j, k):
        ref = ref_of(half, j, k)
        remote(
            ref, ref, send_sem.at[half, 0], recv_sem.at[half, j * 4 + k], me.sibling()
        ).wait_recv()

    def second_axis(half, j):
        send(half, j, 0, me.second_peer(half, 1), j, 3)
        send(half, j, 0, me.second_peer(half, 3), j, 1)
        if j > 1:
            send(half, j, 0, me.second_peer(half, 2), j, 2)

    for half in range(2):
        for step in (1, 3, 2):
            send(half, 0, 0, me.first_peer(half, step), 4 - step, 0)
    for half in range(2):
        second_axis(half, 0)
    for half in range(2):
        landed(half, 0, 0)
    yield
    for j in (1, 3):
        for half in range(2):
            arrived(half, j, 0)
            second_axis(half, j)
    for j in (1, 3):
        for half in range(2):
            landed(half, j, 0)
    yield
    for half in range(2):
        arrived(half, 2, 0)
        second_axis(half, 2)
    for half in range(2):
        landed(half, 2, 0)
    yield
    for j in (0, 1, 3, 2):
        for half in range(2):
            arrived(half, j, 3)
            if j == 0:
                send(half, j, 3, me.second_peer(half, 1), j, 2)
            arrived(half, j, 1)
            if j == 1:
                send(half, j, 1, me.second_peer(half, 3), j, 2)
        for half in range(2):
            landed(half, j, 3)
            landed(half, j, 1)
        yield
    for j in (0, 1, 3, 2):
        for half in range(2):
            arrived(half, j, 2)
            landed(half, j, 2)
        yield


def scatter_plane(me, own, touch, finish, start, bufs, sems, passing):
    pass_r, ring_r, line_r = bufs
    pass_send, pass_recv, ring_send, ring_recv, line_send, line_recv = sems

    def far(half, j):
        return remote(
            own(half, j, 2), pass_r.at[half, j - 1], pass_send.at[half, j - 1],
            pass_recv.at[half, j - 1], me.second_peer(half, 1 if j == 2 else 3),
        )

    def near(half, j, k):
        slot = j * 3 + k - 1
        return remote(
            own(half, j, k), ring_r.at[half, slot], ring_send.at[half, slot],
            ring_recv.at[half, slot], me.second_peer(half, k),
        )

    def line(half, j):
        return remote(
            own(half, j, 0), line_r.at[half, j - 1], line_send.at[half, j - 1],
            line_recv.at[half, j - 1], me.first_peer(half, j),
        )

    def give(j, k):
        for half in range(2):
            own(half, j, k)[...] = touch(half, j, k).astype(BF16)
            start(near(half, j, k))

    def give_passed(j, k):
        for half in range(2):
            value = touch(half, j, k)
            far(half, j).wait_recv()
            value = value + pass_r[half, j - 1].astype(F32)
            own(half, j, k)[...] = value.astype(BF16)
            start(near(half, j, k))

    def gathered(half, j):
        value = touch(half, j, 0)
        for k in (1, 3, 2):
            if k == 2 and passing and j in (1, 2):
                continue
            near(half, j, k).wait_recv()
            value = value + ring_r[half, j * 3 + k - 1].astype(F32)
        return value

    for j in (2, 1):
        for half in range(2):
            own(half, j, 2)[...] = touch(half, j, 2).astype(BF16)
            start(far(half, j) if passing else near(half, j, 2))
        yield
    give(2, 3)
    give(1, 1)
    yield
    give(3, 2)
    give(3, 1)
    give(3, 3)
    yield
    (give_passed if passing else give)(2, 1)
    (give_passed if passing else give)(1, 3)
    yield
    give(0, 2)
    give(0, 1)
    give(0, 3)
    yield
    for j in (2, 1, 3):
        for half in range(2):
            own(half, j, 0)[...] = gathered(half, j).astype(BF16)
            start(line(half, j))
        yield
    for half in range(2):
        value = gathered(half, 0)
        for j in (1, 3, 2):
            line(half, j).wait_recv()
            value = value + line_r[half, j - 1].astype(F32)
        finish(half, value)
    yield


def kernel(
    lengths, q_hbm, cache_hbm, uv_hbm, out_w_hbm, residual_hbm, gain, gate_hbm, up_hbm, down_hbm,
    routes, route_weights, out,
    qv, cv, uv, out_w, res, down_w, gate_up_t, down_t,
    ctx, by_head, by_head_f, heads_all, part, part_b, part_r, hid, hid_t, gate_up,
    act, contrib, from_sib, plane_sum, plane_sum_b, tp_r, weight_row,
    b_pass, b_ring, b_line, a_pass, a_ring, a_line, a_sum, ya_pass, ya_ring,
    load_sem, a2a_send, a2a_recv, ag_send, ag_recv, ag_sib_send, ag_sib_recv,
    rs_send, rs_recv, hy_send, hy_recv,
    ga_send, ga_recv, gy_send, gy_recv, ga_sib_send, ga_sib_recv,
    gb_send, gb_recv, gb_sib_send, gb_sib_recv,
    sib_send, sib_recv, yp_send, yp_recv, yr_send, yr_recv,
    ap_send, ap_recv, ar_send, ar_recv, al_send, al_recv,
    bp_send, bp_recv, br_send, br_recv, bl_send, bl_recv,
    tp_send, tp_recv,
):
    me = Place()
    y, d = me.y, me.d
    own_lanes = pl.ds(pl.multiple_of(y * TP_ROWS, TP_ROWS), TP_ROWS)

    loads = {}
    sent = []

    def load(name, src, dst, index):
        copy = pltpu.make_async_copy(src, dst, load_sem.at[index])
        copy.start()
        loads[name] = copy

    def ready(name):
        loads.pop(name).wait()

    def start(copy):
        copy.start()
        sent.append(copy)

    load("q", q_hbm, qv, 0)
    for i in range(OWN_ROWS):
        load(("cache", i), cache_hbm.at[i], cv.at[i], 1 + i)

    barrier = pltpu.get_barrier_semaphore()
    peers = [me.sibling()]
    for step in (1, 2, 3):
        peers += [me.first_peer(0, step), me.first_peer(1, step), me.tp_peer(step)]
    for peer in peers:
        pl.semaphore_signal(barrier, inc=1, device_id=peer, device_id_type=MESH)

    ready("q")
    for i in range(OWN_ROWS):
        ready(("cache", i))
        if i == 1:
            load("uv", uv_hbm, uv, 5)
            load("out_w", out_w_hbm, out_w, 6)
            load("res", residual_hbm.at[:, own_lanes], res, 7)
        if i == 2:
            load("gate", gate_hbm, contrib.at[:, pl.ds(0, UNITS)], 8)
            load("up", up_hbm, contrib.at[:, pl.ds(UNITS, UNITS)], 9)
            load("down", down_hbm, down_w, 10)
        scores = tn_dot(qv[i], cv[i]) * score_scale
        usable = lax.broadcasted_iota(jnp.int32, scores.shape, 1) < lengths[i]
        peak = jnp.max(jnp.where(usable, scores, -1e30), axis=1, keepdims=True)
        soft = jnp.where(usable, jnp.exp(scores - peak), 0.0)
        total = jnp.sum(soft, axis=1, keepdims=True)
        summed = nt_dot(soft.astype(BF16), cv[i, :LAT, :])
        ctx[i] = (summed / total).astype(BF16)
        if i < 2:
            continue
        if i == 2:
            pl.semaphore_wait(barrier, len(peers))
        for row in range(3) if i == 2 else (3,):
            for step in (2, 1, 3):
                to = pl.multiple_of(lax.rem(y + step, 4) * OWN_HEADS, OWN_HEADS)
                start(remote(
                    ctx.at[row, pl.ds(to, OWN_HEADS)], by_head.at[y * OWN_ROWS + row],
                    a2a_send.at[row, step - 1], a2a_recv.at[row, step - 1], me.tp_peer(step),
                ))
            by_head[y * OWN_ROWS + row] = ctx[
                row, pl.ds(pl.multiple_of(y * OWN_HEADS, OWN_HEADS), OWN_HEADS), :
            ]
    for i in range(OWN_ROWS):
        for step in (1, 2, 3):
            source = lax.rem(y + 4 - step, 4)
            remote(
                ctx.at[i, pl.ds(0, OWN_HEADS)],
                by_head.at[source * OWN_ROWS + i],
                a2a_send.at[i, step - 1],
                a2a_recv.at[i, step - 1],
                me.tp_peer(step),
            ).wait_recv()

    ready("uv")
    for part_of in range(LAT // 128):
        piece = by_head[:, :, pl.ds(part_of * 128, 128)]
        by_head_f[part_of] = piece.astype(F32).reshape(DP_ROWS * OWN_HEADS, 128)
    own_rows = pl.ds(pl.multiple_of(d * DP_ROWS, DP_ROWS), DP_ROWS)
    for h in range(OWN_HEADS):
        picked = jnp.concatenate(
            [
                by_head_f[part_of, pl.ds(h, DP_ROWS, stride=OWN_HEADS), :]
                for part_of in range(LAT // 128)
            ],
            axis=1,
        ).astype(BF16)
        heads_all[own_rows, pl.ds(h * VHEAD, VHEAD)] = jnp.dot(
            picked, uv[h], preferred_element_type=F32
        ).astype(BF16)

    def head_block(half, dp):
        return heads_all.at[
            pl.ds(pl.multiple_of(dp * DP_ROWS, DP_ROWS), DP_ROWS), pl.ds(half * (INNER // 2), INNER // 2)
        ]

    def head_sibling(half, j, k, c):
        ref = head_block(half, me.block(half, j, k, c))
        return remote(
            ref, ref, ag_sib_send.at[half, j * 4 + k], ag_sib_recv.at[half, j * 4 + k], me.sibling()
        )

    def turn_step(i, carry):
        at = pl.ds(pl.multiple_of(i * 128, 128), 128)
        turned = contrib[at, :].astype(F32).T * gain[pl.ds(i, 1), :]
        gate_up_t[:, at] = turned.astype(BF16)
        down_t[at, :] = down_w[:, at].astype(F32).T.astype(BF16)
        return carry

    turned_to = 0
    for step in gather_plane(
        me, head_block, start, (ag_send, ag_recv), lambda *at: start(head_sibling(*at, me.c))
    ):
        if turned_to == 0:
            ready("gate")
            ready("up")
            ready("down")
        upto = min(turned_to + 7, D // 128)
        lax.fori_loop(turned_to, upto, turn_step, 0)
        turned_to = upto
    for half in range(2):
        for j in range(4):
            for k in range(4):
                head_sibling(half, j, k, 1 - me.c).wait_recv()

    ready("out_w")
    part[...] = jnp.zeros_like(part)

    def out_step(k, carry):
        at = pl.ds(pl.multiple_of(k * 512, 512), 512)
        part[...] += nt_dot(out_w[:, at], heads_all[:, at])
        return carry

    lax.fori_loop(0, INNER // 512, out_step, 0)
    for block in range(4):
        part_b[block] = part[:, block * TP_ROWS : (block + 1) * TP_ROWS].astype(BF16)
    for step in (2, 1, 3):
        start(remote(
            part_b.at[lax.rem(y + step, 4)], part_r.at[step - 1],
            rs_send.at[step - 1], rs_recv.at[step - 1], me.tp_peer(step),
        ))

    weight_row[...] = jnp.sum(
        jnp.where(routes[...] == d, route_weights[...], 0.0), axis=0, keepdims=True
    )

    ready("res")
    total = res[...].astype(F32) + part[:, own_lanes]
    for step in (1, 2, 3):
        remote(
            part_b.at[0], part_r.at[step - 1], rs_send.at[step - 1], rs_recv.at[step - 1],
            me.tp_peer(step),
        ).wait_recv()
        total = total + part_r[step - 1].astype(F32)
    hidden = total.astype(BF16)
    hid[...] = hidden.astype(F32)
    own_cols = pl.ds(pl.multiple_of(d * COLS, 16), COLS)
    hid_t[own_cols, own_lanes] = hidden

    pairs = [(dz, dx) for dz in range(4) for dx in range(4)]

    def a_block(half, dp):
        return hid_t.at[rows_of(dp, half * (PART_A // 2), PART_A // 2), own_lanes]

    def b_block(half, dp):
        return hid_t.at[rows_of(dp, PART_A + half * (PART_B // 2), PART_B // 2), :]

    def pair_of(half, j, k):
        return (k, j) if half == 0 else (j, k)

    def a_tp(pair, slot, lanes, step):
        ref = hid_t.at[rows_of(me.at(*pair, me.c), 0, PART_A), lanes]
        n = pair[0] * 4 + pair[1]
        return remote(ref, ref, gy_send.at[n, slot], gy_recv.at[n, slot], me.tp_peer(step))

    def a_sibling(pair, c):
        ref = hid_t.at[rows_of(me.at(*pair, c), 0, PART_A), :]
        n = pair[0] * 4 + pair[1]
        return remote(ref, ref, ga_sib_send.at[n], ga_sib_recv.at[n], me.sibling())

    a_halves, a_landed = set(), []

    def a_here(half, j, k):
        pair = pair_of(half, j, k)
        if pair in a_halves:
            a_landed.append(pair)
            start(a_tp(pair, 0, me.lanes(0), 1))
            start(a_tp(pair, 1, me.lanes(0), 3))
            if len(a_landed) > PASSED:
                start(a_tp(pair, 2, me.lanes(0), 2))
        a_halves.add(pair)

    a_passed, a_done = [0], [0]

    def a_pass_on(count):
        for pair in a_landed[a_passed[0] : min(a_passed[0] + count, PASSED)]:
            if sum(pair) % 2 == 0:
                a_tp(pair, 0, me.lanes(3), 1).wait_recv()
                start(a_tp(pair, 2, me.lanes(3), 1))
            else:
                a_tp(pair, 1, me.lanes(1), 3).wait_recv()
                start(a_tp(pair, 2, me.lanes(1), 3))
        a_passed[0] += count

    def a_finish(count):
        for n in range(a_done[0], min(a_done[0] + count, 16)):
            pair = a_landed[n]
            for slot, step in ((1, 1), (0, 3)):
                if n >= PASSED or (step == 1) == (sum(pair) % 2 == 0):
                    a_tp(pair, slot, me.lanes(step), step).wait_recv()
            a_tp(pair, 2, me.lanes(2), 1).wait_recv()
            start(a_sibling(pair, me.c))
        a_done[0] += count

    def b_sibling(half, j, k, c):
        ref = b_block(half, me.block(half, j, k, c))
        return remote(
            ref, ref, gb_sib_send.at[half, j * 4 + k], gb_sib_recv.at[half, j * 4 + k], me.sibling()
        )

    def b_tp(slot, lanes, step):
        ref = hid_t.at[rows_of(d, PART_A, PART_B), lanes]
        return remote(ref, ref, hy_send.at[slot], hy_recv.at[slot], me.tp_peer(step))

    a_plane = gather_plane(me, a_block, start, (ga_send, ga_recv), a_here)
    b_plane = gather_plane(
        me, b_block, start, (gb_send, gb_recv), lambda *at: start(b_sibling(*at, me.c))
    )
    for slot, step in ((0, 1), (1, 3), (2, 2)):
        start(b_tp(slot, me.lanes(0), step))
    next(a_plane)
    next(a_plane)
    a_pass_on(1)
    next(a_plane)
    b_tp(0, me.lanes(3), 1).wait_recv()
    b_tp(1, me.lanes(1), 1).wait_recv()
    b_tp(2, me.lanes(2), 1).wait_recv()
    next(b_plane)
    for _ in range(4):
        next(a_plane)
    a_pass_on(3)
    for _ in range(4):
        next(a_plane)
    next(b_plane)
    next(b_plane)
    a_pass_on(PASSED - 4)
    next(b_plane)
    next(b_plane)
    for _ in range(2):
        a_finish(3)
        next(b_plane)
    for _ in range(4):
        a_finish(2)
        next(b_plane)
    a_finish(16)
    for half in range(2):
        for j in range(4):
            for k in range(4):
                b_sibling(half, j, k, 1 - me.c).wait_recv()
    for pair in pairs:
        a_sibling(pair, 1 - me.c).wait_recv()

    gate_up[...] = jnp.zeros_like(gate_up)

    def expert_step(k, squares):
        at = pl.ds(pl.multiple_of(k * 1024, 1024), 1024)
        rows = hid_t[at, :]
        gate_up[...] += jnp.dot(gate_up_t[:, at], rows, preferred_element_type=F32)
        wide = rows.astype(F32)
        return squares + jnp.sum((wide * wide).reshape(128, 8, ROWS), axis=0)

    squares = lax.fori_loop(0, D // 1024, expert_step, jnp.zeros((8, ROWS), F32))
    inverse_rms = lax.rsqrt(jnp.sum(squares, axis=0, keepdims=True) * (1.0 / D) + epsilon)
    gate_proj = gate_up[:UNITS, :] * inverse_rms
    up_proj = gate_up[UNITS:, :] * inverse_rms
    silu = gate_proj / (1.0 + jnp.exp(-gate_proj))
    act[...] = (silu * up_proj * weight_row[...]).astype(BF16)

    def from_core(pair, c):
        n = pair[0] * 4 + pair[1]
        return remote(
            contrib.at[rows_of(me.at(*pair, c), 0, COLS), :], from_sib.at[n],
            sib_send.at[n], sib_recv.at[n], me.sibling(),
        )

    def compute(pair):
        at = pl.ds(pl.multiple_of(me.at(*pair, 0) * COLS, 16), 2 * COLS)
        contrib[at, :] = jnp.dot(down_t[at, :], act[...], preferred_element_type=F32).astype(BF16)
        start(from_core(pair, 1 - me.c))

    sib_here = set()

    def sibling_here(pair):
        if pair not in sib_here:
            sib_here.add(pair)
            from_core(pair, me.c).wait_recv()

    def ya_rows(pair):
        return rows_of(me.at(*pair, me.c), 0, SUM_A)

    def ya_far(pair, step):
        n = pair[0] * 4 + pair[1]
        return remote(
            contrib.at[ya_rows(pair), me.lanes(2)], ya_pass.at[n],
            yp_send.at[n], yp_recv.at[n], me.tp_peer(step),
        )

    def ya_near(pair, step):
        n = pair[0] * 4 + pair[1]
        return remote(
            contrib.at[ya_rows(pair), me.lanes(step)], ya_ring.at[n, step - 1],
            yr_send.at[n, step - 1], yr_recv.at[n, step - 1], me.tp_peer(step),
        )

    passed_pairs = []

    def a_first(pair):
        sibling_here(pair)
        at = ya_rows(pair)
        theirs = from_sib[pair[0] * 4 + pair[1], :SUM_A, :]
        contrib[at, :] = (contrib[at, :].astype(F32) + theirs.astype(F32)).astype(BF16)
        if len(passed_pairs) < SUM_PASSED:
            passed_pairs.append(pair)
            far_step = 1 if sum(pair) % 2 == 0 else 3
            start(ya_far(pair, far_step))
            start(ya_near(pair, 4 - far_step))
        else:
            for step in (1, 3, 2):
                start(ya_near(pair, step))

    def a_second(pair):
        step = 1 if sum(pair) % 2 == 0 else 3
        ya_far(pair, step).wait_recv()
        at = ya_rows(pair)
        passed = ya_pass[pair[0] * 4 + pair[1]].astype(F32)
        contrib[at, me.lanes(step)] = (contrib[at, me.lanes(step)].astype(F32) + passed).astype(BF16)
        start(ya_near(pair, step))

    def a_third(pair):
        n = pair[0] * 4 + pair[1]
        value = contrib[ya_rows(pair), own_lanes].astype(F32)
        for step in (1, 3) if pair in passed_pairs else (1, 3, 2):
            ya_near(pair, step).wait_recv()
            value = value + ya_ring[n, step - 1].astype(F32)
        a_sum[n] = value.astype(BF16)

    def a_own(half, j, k):
        dz, dx = pair_of(half, j, k)
        return a_sum.at[dz * 4 + dx, pl.ds(half * (SUM_A // 2), SUM_A // 2), :]

    def a_touch(half, j, k):
        return a_own(half, j, k)[...].astype(F32)

    def a_final(half, value):
        at = pl.ds(half * (SUM_A // 2), SUM_A // 2)
        out[at, :] = (hid[at, :] + value).astype(BF16)

    def b_own(half, j, k):
        return contrib.at[
            rows_of(me.block(half, j, k, me.c), SUM_A + half * (SUM_B // 2), SUM_B // 2), :
        ]

    def b_touch(half, j, k):
        pair = pair_of(half, j, k)
        sibling_here(pair)
        theirs = from_sib[
            pair[0] * 4 + pair[1], pl.ds(SUM_A + half * (SUM_B // 2), SUM_B // 2), :
        ]
        return b_own(half, j, k)[...].astype(F32) + theirs.astype(F32)

    def b_final(half, value):
        at = pl.ds(half * (SUM_B // 2), SUM_B // 2)
        plane_sum[at, :] = value
        plane_sum_b[at, :] = value.astype(BF16)

    a_back = scatter_plane(
        me, a_own, a_touch, a_final, start, (a_pass, a_ring, a_line),
        (ap_send, ap_recv, ar_send, ar_recv, al_send, al_recv), False,
    )
    b_back = scatter_plane(
        me, b_own, b_touch, b_final, start, (b_pass, b_ring, b_line),
        (bp_send, bp_recv, br_send, br_recv, bl_send, bl_recv), True,
    )
    order = [(2, 2), (2, 1), (1, 2), (3, 2), (2, 3), (1, 1), (1, 3), (3, 1), (3, 3)]
    order += [(2, 0), (0, 2), (1, 0), (0, 1), (3, 0), (0, 3), (0, 0)]
    for n, pair in enumerate(order):
        compute(pair)
        if n in (3, 6, 9, 12):
            next(b_back)
        if n >= 3:
            a_first(order[n - 3])
        if n >= 14:
            a_second(order[n - 14])
    for n in range(13, 16):
        a_first(order[n])
        a_second(order[n - 11])
    next(b_back)
    next(b_back)
    for n in range(5, SUM_PASSED):
        a_second(order[n])
    for pair in order:
        a_third(pair)
    for _ in range(6):
        next(a_back)
    for _ in range(3):
        next(b_back)
    for _ in range(3):
        next(a_back)
    next(b_back)

    def b_tp_sum(step):
        return remote(
            plane_sum_b.at[:, me.lanes(step)], tp_r.at[step - 1],
            tp_send.at[step - 1], tp_recv.at[step - 1], me.tp_peer(step),
        )

    for step in (2, 1, 3):
        start(b_tp_sum(step))
    next(a_back)
    moe = plane_sum[:, own_lanes]
    for step in (1, 3, 2):
        b_tp_sum(step).wait_recv()
        moe = moe + tp_r[step - 1].astype(F32)
    out[SUM_A:, :] = (hid[SUM_A:, :] + moe).astype(BF16)

    for copy in sent:
        copy.wait_send()


def local(
    queries, latent_cache, lengths, uv_weight, out_weight, residual, norm_gain,
    gate_weight, up_weight, down_weight, routes, route_weights,
):
    anywhere = pl.BlockSpec(memory_space=pl.ANY)
    vmem = pl.BlockSpec(memory_space=pltpu.VMEM)
    smem = pl.BlockSpec(memory_space=pltpu.SMEM)
    dma = pltpu.SemaphoreType.DMA
    scratch = [
        pltpu.VMEM((OWN_ROWS, KEY, HEADS), BF16),
        pltpu.VMEM((OWN_ROWS, KEY, CTX), BF16),
        pltpu.VMEM((OWN_HEADS, LAT, VHEAD), BF16),
        pltpu.VMEM((COLS, INNER), BF16),
        pltpu.VMEM((COLS, TP_ROWS), BF16),
        pltpu.VMEM((UNITS, D), BF16),
        pltpu.VMEM((2 * UNITS, D), BF16),
        pltpu.VMEM((D, UNITS), BF16),
        pltpu.VMEM((OWN_ROWS, HEADS, LAT), BF16),
        pltpu.VMEM((DP_ROWS, OWN_HEADS, LAT), BF16),
        pltpu.VMEM((LAT // 128, DP_ROWS * OWN_HEADS, 128), F32),
        pltpu.VMEM((ROWS, INNER), BF16),
        pltpu.VMEM((COLS, ROWS), F32),
        pltpu.VMEM((4, COLS, TP_ROWS), BF16),
        pltpu.VMEM((3, COLS, TP_ROWS), BF16),
        pltpu.VMEM((COLS, TP_ROWS), F32),
        pltpu.VMEM((D, ROWS), BF16),
        pltpu.VMEM((2 * UNITS, ROWS), F32),
        pltpu.VMEM((UNITS, ROWS), BF16),
        pltpu.VMEM((D, ROWS), BF16),
        pltpu.VMEM((16, COLS, ROWS), BF16),
        pltpu.VMEM((SUM_B, ROWS), F32),
        pltpu.VMEM((SUM_B, ROWS), BF16),
        pltpu.VMEM((3, SUM_B, TP_ROWS), BF16),
        pltpu.VMEM((1, ROWS), F32),
        pltpu.VMEM((2, 2, SUM_B // 2, ROWS), BF16),
        pltpu.VMEM((2, 12, SUM_B // 2, ROWS), BF16),
        pltpu.VMEM((2, 3, SUM_B // 2, ROWS), BF16),
        pltpu.VMEM((2, 2, SUM_A // 2, TP_ROWS), BF16),
        pltpu.VMEM((2, 12, SUM_A // 2, TP_ROWS), BF16),
        pltpu.VMEM((2, 3, SUM_A // 2, TP_ROWS), BF16),
        pltpu.VMEM((16, SUM_A, TP_ROWS), BF16),
        pltpu.VMEM((16, SUM_A, TP_ROWS), BF16),
        pltpu.VMEM((16, 3, SUM_A, TP_ROWS), BF16),
        dma((11,)),
        dma((4, 3)), dma((4, 3)),
        dma((2, 16)), dma((2, 16)), dma((2, 16)), dma((2, 16)),
        dma((3,)), dma((3,)),
        dma((3,)), dma((3,)),
        dma((2, 16)), dma((2, 16)), dma((16, 3)), dma((16, 3)), dma((16,)), dma((16,)),
        dma((2, 16)), dma((2, 16)), dma((2, 16)), dma((2, 16)),
        dma((16,)), dma((16,)), dma((16,)), dma((16,)), dma((16, 3)), dma((16, 3)),
        dma((2, 2)), dma((2, 2)), dma((2, 12)), dma((2, 12)), dma((2, 3)), dma((2, 3)),
        dma((2, 2)), dma((2, 2)), dma((2, 12)), dma((2, 12)), dma((2, 3)), dma((2, 3)),
        dma((3,)), dma((3,)),
    ]
    return pl.pallas_call(
        kernel,
        out_shape=jax.ShapeDtypeStruct((COLS, TP_ROWS), BF16),
        in_specs=[smem] + [anywhere] * 5 + [vmem] + [anywhere] * 3 + [vmem] * 2,
        out_specs=vmem,
        scratch_shapes=scratch,
        compiler_params=pltpu.CompilerParams(
            collective_id=0, has_side_effects=True, vmem_limit_bytes=62 * 1024 * 1024
        ),
        name="decode_step",
    )(
        lengths, jnp.swapaxes(queries, 1, 2), jnp.swapaxes(latent_cache, 1, 2), uv_weight,
        out_weight.T, residual.T, norm_gain.reshape(D // 128, 128),
        gate_weight[0], up_weight[0], down_weight[0], routes.T, route_weights.T,
    ).T


def solution(mesh):
    placed = (
        P(("dp", "tp"), None, None),
        P(("dp", "tp"), None, None),
        P(("dp", "tp")),
        P("tp", None, None),
        P("tp", "dp"),
        P(None, "dp"),
        P(),
        P("dp", None, "tp"),
        P("dp", None, "tp"),
        P("dp", "tp", None),
        P(),
        P(),
    )
    return jax.shard_map(
        local, mesh=mesh, in_specs=placed, out_specs=P("tp", "dp"), check_vma=False
    )
```

```python
import functools

import jax
import jax.numpy as jnp
from jax import lax
from jax.experimental import pallas as pl
from jax.experimental.pallas import tpu as pltpu
from jax.sharding import PartitionSpec as P

F32 = jnp.float32
BF16 = jnp.bfloat16
MESH = pl.DeviceIdType.MESH

LAT = 512
KEY = 576
CTX = 1024
HEADS = 128
OWN_HEADS = 32
HALF_HEADS = 16
VHEAD = 128
ROWS = 512
OWN_ROWS = 4
DP_ROWS = 16
TP_ROWS = 128
D = 7168
COLS = 224
PART_A = 96
PART_B = 128
INNER = 4096
UNITS = 256
DP = 32

score_scale = 192.0 ** (-0.5)
epsilon = 1e-06

SUM_A = 96
SUM_B = 128
PASSED = 12
SUM_PASSED = 12


def tn_dot(a, b):
    return lax.dot_general(a, b, (((0,), (0,)), ((), ())), preferred_element_type=F32)


def nt_dot(a, b):
    return lax.dot_general(a, b, (((1,), (1,)), ((), ())), preferred_element_type=F32)


class Place:
    def __init__(self):
        dp = lax.axis_index("dp")
        self.y = lax.axis_index("tp")
        self.d = dp
        self.c = lax.rem(dp, 2)
        self.x = lax.rem(dp // 2, 4)
        self.z = dp // 8

    def device(self, z=None, x=None, c=None, y=None):
        z = self.z if z is None else z
        x = self.x if x is None else x
        c = self.c if c is None else c
        y = self.y if y is None else y
        return ((z * 4 + x) * 2 + c, y)

    def sibling(self):
        return self.device(c=1 - self.c)

    def tp_peer(self, step):
        return self.device(y=lax.rem(self.y + step, 4))

    def first(self, half):
        return self.x if half == 0 else self.z

    def second(self, half):
        return self.z if half == 0 else self.x

    def first_peer(self, half, step):
        if half == 0:
            return self.device(x=lax.rem(self.x + step, 4))
        return self.device(z=lax.rem(self.z + step, 4))

    def second_peer(self, half, step):
        return self.first_peer(1 - half, step)

    def pair_peer(self, pair):
        return (self.at(*pair, self.c), self.y)

    def lanes(self, step):
        at = lax.rem(self.y + step, 4) * TP_ROWS
        return pl.ds(pl.multiple_of(at, TP_ROWS), TP_ROWS)

    def at(self, dz, dx, c):
        return (lax.rem(self.z + dz, 4) * 4 + lax.rem(self.x + dx, 4)) * 2 + c

    def block(self, half, j, k, c):
        a = lax.rem(self.first(half) + j, 4)
        b = lax.rem(self.second(half) + k, 4)
        z, x = (b, a) if half == 0 else (a, b)
        return (z * 4 + x) * 2 + c


def remote(src, dst, send, recv, device):
    return pltpu.make_async_remote_copy(
        src_ref=src, dst_ref=dst, send_sem=send, recv_sem=recv, device_id=device, device_id_type=MESH
    )


def rows_of(dp, offset, count):
    return pl.ds(pl.multiple_of(dp * COLS + offset, 16), count)


def gather_plane(me, blk, start, sems, landed):
    send_sem, recv_sem = sems
    count = [0, 0]

    def ref_of(half, j, k):
        return blk(half, me.block(half, j, k, me.c))

    def send(half, j, k, device, rj, rk):
        ref = ref_of(half, j, k)
        start(remote(
            ref, ref, send_sem.at[half, count[half]], recv_sem.at[half, rj * 4 + rk], device
        ))
        count[half] += 1

    def arrived(half, j, k):
        ref = ref_of(half, j, k)
        remote(
            ref, ref, send_sem.at[half, 0], recv_sem.at[half, j * 4 + k], me.sibling()
        ).wait_recv()

    def second_axis(half, j):
        send(half, j, 0, me.second_peer(half, 1), j, 3)
        send(half, j, 0, me.second_peer(half, 3), j, 1)
        if j == 2:
            send(half, j, 0, me.second_peer(half, 2), j, 2)

    for half in range(2):
        for step in (1, 3, 2):
            send(half, 0, 0, me.first_peer(half, step), 4 - step, 0)
        second_axis(half, 0)
        landed(half, 0, 0)
        yield
    for j in (1, 3):
        for half in range(2):
            arrived(half, j, 0)
            second_axis(half, j)
    for j in (1, 3):
        for half in range(2):
            landed(half, j, 0)
    yield
    for half in range(2):
        arrived(half, 2, 0)
        second_axis(half, 2)
    for half in range(2):
        landed(half, 2, 0)
    yield
    for j in (0, 1, 3, 2):
        for half in range(2):
            arrived(half, j, 3)
            if j == 0:
                send(half, j, 3, me.second_peer(half, 1), j, 2)
            arrived(half, j, 1)
            if j == 1:
                send(half, j, 1, me.second_peer(half, 3), j, 2)
            if j == 3:
                send(half, j, 3 - 2 * me.c, me.second_peer(half, 1 + 2 * me.c), j, 2)
        for half in range(2):
            landed(half, j, 3)
            landed(half, j, 1)
        yield
    for j in (0, 1, 3, 2):
        for half in range(2):
            arrived(half, j, 2)
            landed(half, j, 2)
        yield


def scatter_plane(me, own, touch, finish, start, bufs, sems):
    pass_r, ring_r, line_r = bufs
    pass_send, pass_recv, ring_send, ring_recv, line_send, line_recv = sems

    def far(half, j):
        return remote(
            own(half, j, 2), pass_r.at[half, j - 1], pass_send.at[half, j - 1],
            pass_recv.at[half, j - 1], me.second_peer(half, 1 if j == 2 else 3),
        )

    def near(half, j, k):
        slot = j * 3 + k - 1
        return remote(
            own(half, j, k), ring_r.at[half, slot], ring_send.at[half, slot],
            ring_recv.at[half, slot], me.second_peer(half, k),
        )

    def line(half, j):
        return remote(
            own(half, j, 0), line_r.at[half, j - 1], line_send.at[half, j - 1],
            line_recv.at[half, j - 1], me.first_peer(half, j),
        )

    def give(j, k):
        for half in range(2):
            own(half, j, k)[...] = touch(half, j, k).astype(BF16)
            start(near(half, j, k))

    def give_passed(j, k):
        for half in range(2):
            value = touch(half, j, k)
            far(half, j).wait_recv()
            value = value + pass_r[half, j - 1].astype(F32)
            own(half, j, k)[...] = value.astype(BF16)
            start(near(half, j, k))

    def gathered(half, j):
        value = touch(half, j, 0)
        for k in (1, 3, 2):
            if k == 2 and j in (1, 2):
                continue
            near(half, j, k).wait_recv()
            value = value + ring_r[half, j * 3 + k - 1].astype(F32)
        return value

    for j in (2, 1):
        for half in range(2):
            own(half, j, 2)[...] = touch(half, j, 2).astype(BF16)
            start(far(half, j))
        yield
    give(2, 3)
    give(1, 1)
    yield
    give(3, 2)
    give(3, 1)
    give(3, 3)
    yield
    give_passed(2, 1)
    give_passed(1, 3)
    yield
    give(0, 2)
    give(0, 1)
    give(0, 3)
    yield
    for j in (2, 1, 3):
        for half in range(2):
            own(half, j, 0)[...] = gathered(half, j).astype(BF16)
            start(line(half, j))
        yield
    for half in range(2):
        value = gathered(half, 0)
        for j in (1, 3, 2):
            line(half, j).wait_recv()
            value = value + line_r[half, j - 1].astype(F32)
        finish(half, value)
    yield


def kernel(
    lengths, q_hbm, cache_hbm, uv_hbm, out_w_hbm, residual_hbm, gain_hbm, gate_hbm, up_hbm, down_hbm,
    routes_hbm, route_weights_hbm, out,
    gain, routes, route_weights, qv, cv, uv, out_w, res, down_w, gate_up_t, down_t,
    ctx, by_head, by_head_f, heads_all, part, part_b, part_r, hid, hid_t, gate_up,
    act, contrib, from_sib, plane_sum, plane_sum_b, tp_r, weight_row,
    b_pass, b_ring, b_line, a_ring, a_sum, ya_pass, ya_ring,
    load_sem, a2a_send, a2a_recv, ag_send, ag_recv, ag_sib_send, ag_sib_recv,
    rs_send, rs_recv, hy_send, hy_recv,
    ga_send, ga_recv, gy_send, gy_recv, ga_sib_send, ga_sib_recv,
    gb_send, gb_recv, gb_sib_send, gb_sib_recv,
    sib_send, sib_recv, yp_send, yp_recv, yr_send, yr_recv,
    ar_send, ar_recv,
    bp_send, bp_recv, br_send, br_recv, bl_send, bl_recv,
    tp_send, tp_recv,
):
    me = Place()
    y, d = me.y, me.d
    own_lanes = pl.ds(pl.multiple_of(y * TP_ROWS, TP_ROWS), TP_ROWS)

    loads = {}
    sent = []

    def load(name, src, dst, index):
        copy = pltpu.make_async_copy(src, dst, load_sem.at[index])
        copy.start()
        loads[name] = copy

    def ready(name):
        loads.pop(name).wait()

    def start(copy):
        copy.start()
        sent.append(copy)

    load("q", q_hbm, qv, 0)
    for i in range(OWN_ROWS):
        load(("cache", i), cache_hbm.at[i], cv.at[i], 1 + i)

    barrier = pltpu.get_barrier_semaphore()
    peers = [me.sibling()]
    for step in (1, 2, 3):
        peers += [me.first_peer(0, step), me.first_peer(1, step), me.tp_peer(step)]
    for peer in peers:
        pl.semaphore_signal(barrier, inc=1, device_id=peer, device_id_type=MESH)

    def heads_out(row, half, step):
        to = lax.rem(y + step, 4) * OWN_HEADS + half * HALF_HEADS
        return remote(
            ctx.at[row, pl.ds(pl.multiple_of(to, HALF_HEADS), HALF_HEADS)],
            by_head.at[y * OWN_ROWS + row, pl.ds(half * HALF_HEADS, HALF_HEADS)],
            a2a_send.at[row, half * 3 + step - 1], a2a_recv.at[row, half * 3 + step - 1],
            me.tp_peer(step),
        )

    ready("q")
    for i in range(OWN_ROWS):
        ready(("cache", i))
        if i == 1:
            load("uv", uv_hbm, uv, 5)
            load("out_w", out_w_hbm, out_w, 6)
            load("res", residual_hbm.at[:, own_lanes], res, 7)
        if i == 2:
            load("gate", gate_hbm, contrib.at[:, pl.ds(0, UNITS)], 8)
            load("up", up_hbm, contrib.at[:, pl.ds(UNITS, UNITS)], 9)
            load("down", down_hbm, down_w, 10)
            load("gain", gain_hbm, gain, 11)
            load("routes", routes_hbm, routes, 12)
            load("route_weights", route_weights_hbm, route_weights, 13)
        scores = tn_dot(qv[i], cv[i]) * score_scale
        usable = lax.broadcasted_iota(jnp.int32, scores.shape, 1) < lengths[i]
        peak = jnp.max(jnp.where(usable, scores, -1e30), axis=1, keepdims=True)
        soft = jnp.where(usable, jnp.exp(scores - peak), 0.0)
        total = jnp.sum(soft, axis=1, keepdims=True)
        summed = nt_dot(soft.astype(BF16), cv[i, :LAT, :])
        ctx[i] = (summed / total).astype(BF16)
        if i == 0:
            pl.semaphore_wait(barrier, len(peers))
        for step in (2, 1, 3):
            start(heads_out(i, 0, step))
        by_head[y * OWN_ROWS + i] = ctx[
            i, pl.ds(pl.multiple_of(y * OWN_HEADS, OWN_HEADS), OWN_HEADS), :
        ]
    for i in range(OWN_ROWS):
        for step in (2, 1, 3):
            start(heads_out(i, 1, step))

    ready("uv")
    own_rows = pl.ds(pl.multiple_of(d * DP_ROWS, DP_ROWS), DP_ROWS)

    def project(half):
        for i in range(OWN_ROWS):
            for step in (1, 3, 2):
                heads_out(i, half, step).wait_recv()
        heads = pl.ds(half * HALF_HEADS, HALF_HEADS)
        for part_of in range(LAT // 128):
            piece = by_head[:, heads, pl.ds(part_of * 128, 128)]
            by_head_f[part_of] = piece.astype(F32).reshape(DP_ROWS * HALF_HEADS, 128)
        for h in range(HALF_HEADS):
            picked = jnp.concatenate(
                [
                    by_head_f[part_of, pl.ds(h, DP_ROWS, stride=HALF_HEADS), :]
                    for part_of in range(LAT // 128)
                ],
                axis=1,
            ).astype(BF16)
            at = half * HALF_HEADS + h
            heads_all[own_rows, pl.ds(at * VHEAD, VHEAD)] = jnp.dot(
                picked, uv[at], preferred_element_type=F32
            ).astype(BF16)

    project(0)
    def head_block(half, dp):
        return heads_all.at[
            pl.ds(pl.multiple_of(dp * DP_ROWS, DP_ROWS), DP_ROWS), pl.ds(half * (INNER // 2), INNER // 2)
        ]

    def head_sibling(half, j, k, c):
        ref = head_block(half, me.block(half, j, k, c))
        return remote(
            ref, ref, ag_sib_send.at[half, j * 4 + k], ag_sib_recv.at[half, j * 4 + k], me.sibling()
        )

    def turn_step(i, carry):
        at = pl.ds(pl.multiple_of(i * 128, 128), 128)
        turned = contrib[at, :].astype(F32).T * gain[pl.ds(i, 1), :]
        gate_up_t[:, at] = turned.astype(BF16)
        down_t[at, :] = down_w[:, at].astype(F32).T.astype(BF16)
        return carry

    turned_to = 0
    heads_plane = gather_plane(
        me, head_block, start, (ag_send, ag_recv), lambda *at: start(head_sibling(*at, me.c))
    )
    next(heads_plane)
    project(1)
    for step in heads_plane:
        if turned_to == 0:
            for name in ("gate", "up", "down", "gain"):
                ready(name)
        upto = min(turned_to + 7, D // 128)
        lax.fori_loop(turned_to, upto, turn_step, 0)
        turned_to = upto

    ready("out_w")
    part[...] = jnp.zeros_like(part)

    def out_step(k, carry):
        at = pl.ds(pl.multiple_of(k * 512, 512), 512)
        part[...] += nt_dot(out_w[:, at], heads_all[:, at])
        return carry

    for half in range(2):
        for j in range(4):
            for k in range(4):
                head_sibling(half, j, k, 1 - me.c).wait_recv()
        lax.fori_loop(half * 4, half * 4 + 4, out_step, 0)
    for block in range(4):
        part_b[block] = part[:, block * TP_ROWS : (block + 1) * TP_ROWS].astype(BF16)
    for step in (2, 1, 3):
        start(remote(
            part_b.at[lax.rem(y + step, 4)], part_r.at[step - 1],
            rs_send.at[step - 1], rs_recv.at[step - 1], me.tp_peer(step),
        ))

    ready("routes")
    ready("route_weights")
    weight_row[...] = jnp.sum(
        jnp.where(routes[...] == d, route_weights[...], 0.0), axis=0, keepdims=True
    )

    ready("res")
    total = res[...].astype(F32) + part[:, own_lanes]
    for step in (1, 2, 3):
        remote(
            part_b.at[0], part_r.at[step - 1], rs_send.at[step - 1], rs_recv.at[step - 1],
            me.tp_peer(step),
        ).wait_recv()
        total = total + part_r[step - 1].astype(F32)
    hidden = total.astype(BF16)
    hid[...] = hidden.astype(F32)
    own_cols = pl.ds(pl.multiple_of(d * COLS, 16), COLS)
    hid_t[own_cols, own_lanes] = hidden

    pairs = [(dz, dx) for dz in range(4) for dx in range(4)]

    def b_block(half, dp):
        return hid_t.at[rows_of(dp, PART_A + half * (PART_B // 2), PART_B // 2), :]

    def pair_of(half, j, k):
        return (k, j) if half == 0 else (j, k)

    def a_tp(pair, slot, lanes, step):
        ref = hid_t.at[rows_of(me.at(*pair, me.c), 0, PART_A), lanes]
        n = pair[0] * 4 + pair[1]
        return remote(ref, ref, gy_send.at[n, slot], gy_recv.at[n, slot], me.tp_peer(step))

    def a_sibling(pair, c):
        ref = hid_t.at[rows_of(me.at(*pair, c), 0, PART_A), :]
        n = pair[0] * 4 + pair[1]
        return remote(ref, ref, ga_sib_send.at[n], ga_sib_recv.at[n], me.sibling())

    def a_plane(pair):
        ref = hid_t.at[rows_of(d, 0, PART_A), own_lanes]
        n, opposite = pair[0] * 4 + pair[1], (4 - pair[0]) % 4 * 4 + (4 - pair[1]) % 4
        return remote(ref, ref, ga_send.at[n], ga_recv.at[opposite], me.pair_peer(pair))

    a_landed = []

    def a_here(pair):
        a_landed.append(pair)
        start(a_tp(pair, 0, me.lanes(0), 1))
        start(a_tp(pair, 1, me.lanes(0), 3))
        if len(a_landed) > PASSED:
            start(a_tp(pair, 2, me.lanes(0), 2))

    a_passed, a_done = [0], [0]

    def a_pass_on(count):
        for pair in a_landed[a_passed[0] : min(a_passed[0] + count, PASSED)]:
            if sum(pair) % 2 == 0:
                a_tp(pair, 0, me.lanes(3), 1).wait_recv()
                start(a_tp(pair, 2, me.lanes(3), 1))
            else:
                a_tp(pair, 1, me.lanes(1), 3).wait_recv()
                start(a_tp(pair, 2, me.lanes(1), 3))
        a_passed[0] += count

    def a_finish(count):
        for n in range(a_done[0], min(a_done[0] + count, 16)):
            pair = a_landed[n]
            for slot, step in ((1, 1), (0, 3)):
                if n >= PASSED or (step == 1) == (sum(pair) % 2 == 0):
                    a_tp(pair, slot, me.lanes(step), step).wait_recv()
            a_tp(pair, 2, me.lanes(2), 1).wait_recv()
            start(a_sibling(pair, me.c))
        a_done[0] += count

    def b_sibling(half, j, k, c):
        ref = b_block(half, me.block(half, j, k, c))
        return remote(
            ref, ref, gb_sib_send.at[half, j * 4 + k], gb_sib_recv.at[half, j * 4 + k], me.sibling()
        )

    def b_tp(slot, lanes, step):
        ref = hid_t.at[rows_of(d, PART_A, PART_B), lanes]
        return remote(ref, ref, hy_send.at[slot], hy_recv.at[slot], me.tp_peer(step))

    b_plane = gather_plane(
        me, b_block, start, (gb_send, gb_recv), lambda *at: start(b_sibling(*at, me.c))
    )
    nearest = sorted(pairs, key=lambda pair: sum((0, 1, 2, 1)[step] for step in pair))
    for slot, step in ((0, 1), (1, 3), (2, 2)):
        start(b_tp(slot, me.lanes(0), step))
    for pair in nearest[1:]:
        start(a_plane(pair))
    a_here((0, 0))
    for pair in nearest[1:5]:
        opposite = ((4 - pair[0]) % 4, (4 - pair[1]) % 4)
        a_plane(opposite).wait_recv()
        a_here(pair)
    b_tp(0, me.lanes(3), 1).wait_recv()
    b_tp(1, me.lanes(1), 1).wait_recv()
    b_tp(2, me.lanes(2), 1).wait_recv()
    next(b_plane)
    next(b_plane)
    a_pass_on(1)
    for pair in nearest[5:]:
        opposite = ((4 - pair[0]) % 4, (4 - pair[1]) % 4)
        a_plane(opposite).wait_recv()
        a_here(pair)
    a_pass_on(3)
    next(b_plane)
    next(b_plane)
    a_pass_on(4)
    next(b_plane)
    a_pass_on(2)
    next(b_plane)
    a_pass_on(2)
    for _ in range(2):
        a_finish(3)
        next(b_plane)
    for _ in range(4):
        a_finish(2)
        next(b_plane)
    a_finish(16)
    for half in range(2):
        for j in range(4):
            for k in range(4):
                b_sibling(half, j, k, 1 - me.c).wait_recv()
    for pair in pairs:
        a_sibling(pair, 1 - me.c).wait_recv()

    gate_up[...] = jnp.zeros_like(gate_up)

    def expert_step(k, squares):
        at = pl.ds(pl.multiple_of(k * 1024, 1024), 1024)
        rows = hid_t[at, :]
        gate_up[...] += jnp.dot(gate_up_t[:, at], rows, preferred_element_type=F32)
        wide = rows.astype(F32)
        return squares + jnp.sum((wide * wide).reshape(128, 8, ROWS), axis=0)

    squares = lax.fori_loop(0, D // 1024, expert_step, jnp.zeros((8, ROWS), F32))
    inverse_rms = lax.rsqrt(jnp.sum(squares, axis=0, keepdims=True) * (1.0 / D) + epsilon)
    gate_proj = gate_up[:UNITS, :] * inverse_rms
    up_proj = gate_up[UNITS:, :] * inverse_rms
    silu = gate_proj / (1.0 + jnp.exp(-gate_proj))
    act[...] = (silu * up_proj * weight_row[...]).astype(BF16)

    def from_core(pair, c):
        n = pair[0] * 4 + pair[1]
        return remote(
            contrib.at[rows_of(me.at(*pair, c), 0, COLS), :], from_sib.at[n],
            sib_send.at[n], sib_recv.at[n], me.sibling(),
        )

    def compute(pair):
        at = pl.ds(pl.multiple_of(me.at(*pair, 0) * COLS, 16), 2 * COLS)
        contrib[at, :] = jnp.dot(down_t[at, :], act[...], preferred_element_type=F32).astype(BF16)
        start(from_core(pair, 1 - me.c))

    sib_here = set()

    def sibling_here(pair):
        if pair not in sib_here:
            sib_here.add(pair)
            from_core(pair, me.c).wait_recv()

    def ya_rows(pair):
        return rows_of(me.at(*pair, me.c), 0, SUM_A)

    def ya_far(pair, step):
        n = pair[0] * 4 + pair[1]
        return remote(
            contrib.at[ya_rows(pair), me.lanes(2)], ya_pass.at[n],
            yp_send.at[n], yp_recv.at[n], me.tp_peer(step),
        )

    def ya_near(pair, step):
        n = pair[0] * 4 + pair[1]
        return remote(
            contrib.at[ya_rows(pair), me.lanes(step)], ya_ring.at[n, step - 1],
            yr_send.at[n, step - 1], yr_recv.at[n, step - 1], me.tp_peer(step),
        )

    passed_pairs = []

    def a_first(pair):
        sibling_here(pair)
        at = ya_rows(pair)
        theirs = from_sib[pair[0] * 4 + pair[1], :SUM_A, :]
        contrib[at, :] = (contrib[at, :].astype(F32) + theirs.astype(F32)).astype(BF16)
        if len(passed_pairs) < SUM_PASSED:
            passed_pairs.append(pair)
            far_step = 1 if sum(pair) % 2 == 0 else 3
            start(ya_far(pair, far_step))
            start(ya_near(pair, 4 - far_step))
        else:
            for step in (1, 3, 2):
                start(ya_near(pair, step))

    def a_second(pair):
        step = 1 if sum(pair) % 2 == 0 else 3
        ya_far(pair, step).wait_recv()
        at = ya_rows(pair)
        passed = ya_pass[pair[0] * 4 + pair[1]].astype(F32)
        contrib[at, me.lanes(step)] = (contrib[at, me.lanes(step)].astype(F32) + passed).astype(BF16)
        start(ya_near(pair, step))

    def a_give(pair):
        n = pair[0] * 4 + pair[1]
        return remote(
            a_sum.at[n], a_ring.at[n - 1], ar_send.at[n - 1], ar_recv.at[n - 1], me.pair_peer(pair)
        )

    def a_third(pair):
        n = pair[0] * 4 + pair[1]
        value = contrib[ya_rows(pair), own_lanes].astype(F32)
        for step in (1, 3) if pair in passed_pairs else (1, 3, 2):
            ya_near(pair, step).wait_recv()
            value = value + ya_ring[n, step - 1].astype(F32)
        a_sum[n] = value.astype(BF16)
        if n:
            start(a_give(pair))

    def b_own(half, j, k):
        return contrib.at[
            rows_of(me.block(half, j, k, me.c), SUM_A + half * (SUM_B // 2), SUM_B // 2), :
        ]

    def b_touch(half, j, k):
        pair = pair_of(half, j, k)
        sibling_here(pair)
        theirs = from_sib[
            pair[0] * 4 + pair[1], pl.ds(SUM_A + half * (SUM_B // 2), SUM_B // 2), :
        ]
        return b_own(half, j, k)[...].astype(F32) + theirs.astype(F32)

    def b_final(half, value):
        at = pl.ds(half * (SUM_B // 2), SUM_B // 2)
        plane_sum[at, :] = value
        plane_sum_b[at, :] = value.astype(BF16)

    b_back = scatter_plane(
        me, b_own, b_touch, b_final, start, (b_pass, b_ring, b_line),
        (bp_send, bp_recv, br_send, br_recv, bl_send, bl_recv),
    )
    order = [(2, 2), (2, 1), (1, 2), (3, 2), (2, 3), (1, 1), (1, 3), (3, 1), (3, 3)]
    order += [(2, 0), (0, 2), (1, 0), (0, 1), (3, 0), (0, 3), (0, 0)]
    for n, pair in enumerate(order):
        compute(pair)
        if n in (3, 6, 9, 12):
            next(b_back)
        if n >= 3:
            a_first(order[n - 3])
        if n >= 14:
            a_second(order[n - 14])
    for n in range(13, 16):
        a_first(order[n])
        a_second(order[n - 11])
    next(b_back)
    next(b_back)
    for n in range(5, SUM_PASSED):
        a_second(order[n])
    for pair in order[:8]:
        a_third(pair)
    for _ in range(3):
        next(b_back)
    for pair in order[8:]:
        a_third(pair)
    next(b_back)

    def b_tp_sum(step):
        return remote(
            plane_sum_b.at[:, me.lanes(step)], tp_r.at[step - 1],
            tp_send.at[step - 1], tp_recv.at[step - 1], me.tp_peer(step),
        )

    for step in (2, 1, 3):
        start(b_tp_sum(step))
    moe = a_sum[0].astype(F32)
    for pair in order[:-1]:
        a_give(pair).wait_recv()
        moe = moe + a_ring[pair[0] * 4 + pair[1] - 1].astype(F32)
    out[:SUM_A, :] = (hid[:SUM_A, :] + moe).astype(BF16)
    moe = plane_sum[:, own_lanes]
    for step in (1, 3, 2):
        b_tp_sum(step).wait_recv()
        moe = moe + tp_r[step - 1].astype(F32)
    out[SUM_A:, :] = (hid[SUM_A:, :] + moe).astype(BF16)

    for copy in sent:
        copy.wait_send()


def local(
    queries, latent_cache, lengths, uv_weight, out_weight, residual, norm_gain,
    gate_weight, up_weight, down_weight, routes, route_weights,
):
    anywhere = pl.BlockSpec(memory_space=pl.ANY)
    vmem = pl.BlockSpec(memory_space=pltpu.VMEM)
    smem = pl.BlockSpec(memory_space=pltpu.SMEM)
    dma = pltpu.SemaphoreType.DMA
    scratch = [
        pltpu.VMEM((D // 128, 128), F32),
        pltpu.VMEM(routes.shape[::-1], jnp.int32),
        pltpu.VMEM(routes.shape[::-1], F32),
        pltpu.VMEM((OWN_ROWS, KEY, HEADS), BF16),
        pltpu.VMEM((OWN_ROWS, KEY, CTX), BF16),
        pltpu.VMEM((OWN_HEADS, LAT, VHEAD), BF16),
        pltpu.VMEM((COLS, INNER), BF16),
        pltpu.VMEM((COLS, TP_ROWS), BF16),
        pltpu.VMEM((UNITS, D), BF16),
        pltpu.VMEM((2 * UNITS, D), BF16),
        pltpu.VMEM((D, UNITS), BF16),
        pltpu.VMEM((OWN_ROWS, HEADS, LAT), BF16),
        pltpu.VMEM((DP_ROWS, OWN_HEADS, LAT), BF16),
        pltpu.VMEM((LAT // 128, DP_ROWS * HALF_HEADS, 128), F32),
        pltpu.VMEM((ROWS, INNER), BF16),
        pltpu.VMEM((COLS, ROWS), F32),
        pltpu.VMEM((4, COLS, TP_ROWS), BF16),
        pltpu.VMEM((3, COLS, TP_ROWS), BF16),
        pltpu.VMEM((COLS, TP_ROWS), F32),
        pltpu.VMEM((D, ROWS), BF16),
        pltpu.VMEM((2 * UNITS, ROWS), F32),
        pltpu.VMEM((UNITS, ROWS), BF16),
        pltpu.VMEM((D, ROWS), BF16),
        pltpu.VMEM((16, COLS, ROWS), BF16),
        pltpu.VMEM((SUM_B, ROWS), F32),
        pltpu.VMEM((SUM_B, ROWS), BF16),
        pltpu.VMEM((3, SUM_B, TP_ROWS), BF16),
        pltpu.VMEM((1, ROWS), F32),
        pltpu.VMEM((2, 2, SUM_B // 2, ROWS), BF16),
        pltpu.VMEM((2, 12, SUM_B // 2, ROWS), BF16),
        pltpu.VMEM((2, 3, SUM_B // 2, ROWS), BF16),
        pltpu.VMEM((15, SUM_A, TP_ROWS), BF16),
        pltpu.VMEM((16, SUM_A, TP_ROWS), BF16),
        pltpu.VMEM((16, SUM_A, TP_ROWS), BF16),
        pltpu.VMEM((16, 3, SUM_A, TP_ROWS), BF16),
        dma((14,)),
        dma((4, 6)), dma((4, 6)),
        dma((2, 16)), dma((2, 16)), dma((2, 16)), dma((2, 16)),
        dma((3,)), dma((3,)),
        dma((3,)), dma((3,)),
        dma((16,)), dma((16,)), dma((16, 3)), dma((16, 3)), dma((16,)), dma((16,)),
        dma((2, 16)), dma((2, 16)), dma((2, 16)), dma((2, 16)),
        dma((16,)), dma((16,)), dma((16,)), dma((16,)), dma((16, 3)), dma((16, 3)),
        dma((15,)), dma((15,)),
        dma((2, 2)), dma((2, 2)), dma((2, 12)), dma((2, 12)), dma((2, 3)), dma((2, 3)),
        dma((3,)), dma((3,)),
    ]
    return pl.pallas_call(
        kernel,
        out_shape=jax.ShapeDtypeStruct((COLS, TP_ROWS), BF16),
        in_specs=[smem] + [anywhere] * 11,
        out_specs=vmem,
        scratch_shapes=scratch,
        compiler_params=pltpu.CompilerParams(
            collective_id=0, has_side_effects=True, vmem_limit_bytes=62 * 1024 * 1024
        ),
        name="decode_step",
    )(
        lengths, jnp.swapaxes(queries, 1, 2), jnp.swapaxes(latent_cache, 1, 2), uv_weight,
        out_weight.T, residual.T, norm_gain.reshape(D // 128, 128),
        gate_weight[0], up_weight[0], down_weight[0], routes.T, route_weights.T,
    ).T


def solution(mesh):
    placed = (
        P(("dp", "tp"), None, None),
        P(("dp", "tp"), None, None),
        P(("dp", "tp")),
        P("tp", None, None),
        P("tp", "dp"),
        P(None, "dp"),
        P(),
        P("dp", None, "tp"),
        P("dp", None, "tp"),
        P("dp", "tp", None),
        P(),
        P(),
    )
    return jax.shard_map(
        local, mesh=mesh, in_specs=placed, out_specs=P("tp", "dp"), check_vma=False
    )
```

```python
import math

import jax
import jax.numpy as jnp
from jax import lax
from jax.experimental import pallas as pl
from jax.experimental.pallas import tpu as pltpu
from jax.sharding import PartitionSpec as P

F32 = jnp.float32
BF16 = jnp.bfloat16
MESH = pl.DeviceIdType.MESH

LAT = 512
KEY = 576
CTX = 1024
HEADS = 128
OWN_HEADS = 32
HALF_HEADS = 16
VHEAD = 128
ROWS = 512
OWN_ROWS = 4
DP_ROWS = 16
TP_ROWS = 128
D = 7168
COLS = 224
PART_A = 96
PART_B = 128
INNER = 4096
UNITS = 256
DP = 32

score_scale = 192.0 ** (-0.5)
epsilon = 1e-06

SUM_A = 96
SUM_B = 128
PASSED = 12
SUM_PASSED = 12


def tn_dot(a, b):
    return lax.dot_general(a, b, (((0,), (0,)), ((), ())), preferred_element_type=F32)


def nt_dot(a, b):
    return lax.dot_general(a, b, (((1,), (1,)), ((), ())), preferred_element_type=F32)


class Place:
    def __init__(self):
        dp = lax.axis_index("dp")
        self.y = lax.axis_index("tp")
        self.d = dp
        self.c = lax.rem(dp, 2)
        self.x = lax.rem(dp // 2, 4)
        self.z = dp // 8

    def device(self, z=None, x=None, c=None, y=None):
        z = self.z if z is None else z
        x = self.x if x is None else x
        c = self.c if c is None else c
        y = self.y if y is None else y
        return ((z * 4 + x) * 2 + c, y)

    def sibling(self):
        return self.device(c=1 - self.c)

    def tp_peer(self, step):
        return self.device(y=lax.rem(self.y + step, 4))

    def first(self, half):
        return self.x if half == 0 else self.z

    def second(self, half):
        return self.z if half == 0 else self.x

    def first_peer(self, half, step):
        if half == 0:
            return self.device(x=lax.rem(self.x + step, 4))
        return self.device(z=lax.rem(self.z + step, 4))

    def second_peer(self, half, step):
        return self.first_peer(1 - half, step)

    def pair_peer(self, pair):
        return (self.at(*pair, self.c), self.y)

    def lanes(self, step):
        at = lax.rem(self.y + step, 4) * TP_ROWS
        return pl.ds(pl.multiple_of(at, TP_ROWS), TP_ROWS)

    def at(self, dz, dx, c):
        return (lax.rem(self.z + dz, 4) * 4 + lax.rem(self.x + dx, 4)) * 2 + c

    def block(self, half, j, k, c):
        a = lax.rem(self.first(half) + j, 4)
        b = lax.rem(self.second(half) + k, 4)
        z, x = (b, a) if half == 0 else (a, b)
        return (z * 4 + x) * 2 + c


class Sends:
    def __init__(self, sems, group):
        self.sem, self.total, self.at = sems.at[group], 0, self

    def __getitem__(self, index):
        return self


class Copy:
    def __init__(self, src, dst, send, recv, device):
        self.sends, self.bytes = send, 2 * math.prod(src.shape)
        self.copy = pltpu.make_async_remote_copy(
            src_ref=src, dst_ref=dst, send_sem=send.sem, recv_sem=recv,
            device_id=device, device_id_type=MESH,
        )

    def start(self):
        self.sends.total += self.bytes
        self.copy.start()

    def wait_recv(self):
        self.copy.wait_recv()


def remote(src, dst, send, recv, device):
    return Copy(src, dst, send, recv, device)


def rows_of(dp, offset, count):
    return pl.ds(pl.multiple_of(dp * COLS + offset, 16), count)


def gather_plane(me, blk, start, sems, landed):
    send_sem, recv_sem = sems

    def ref_of(half, j, k):
        return blk(half, me.block(half, j, k, me.c))

    def send(half, j, k, device, rj, rk):
        ref = ref_of(half, j, k)
        start(remote(
            ref, ref, send_sem, recv_sem.at[half, rj * 4 + rk], device
        ))

    def arrived(half, j, k):
        ref = ref_of(half, j, k)
        remote(
            ref, ref, send_sem, recv_sem.at[half, j * 4 + k], me.sibling()
        ).wait_recv()

    def second_axis(half, j):
        send(half, j, 0, me.second_peer(half, 1), j, 3)
        send(half, j, 0, me.second_peer(half, 3), j, 1)
        if j == 2:
            send(half, j, 0, me.second_peer(half, 2), j, 2)

    for half in range(2):
        for step in (1, 3, 2):
            send(half, 0, 0, me.first_peer(half, step), 4 - step, 0)
        second_axis(half, 0)
        landed(half, 0, 0)
        yield
    for j in (1, 3):
        for half in range(2):
            arrived(half, j, 0)
            second_axis(half, j)
    for j in (1, 3):
        for half in range(2):
            landed(half, j, 0)
    yield
    for half in range(2):
        arrived(half, 2, 0)
        second_axis(half, 2)
    for half in range(2):
        landed(half, 2, 0)
    yield
    for j in (0, 1, 3, 2):
        for half in range(2):
            arrived(half, j, 3)
            if j == 0:
                send(half, j, 3, me.second_peer(half, 1), j, 2)
            arrived(half, j, 1)
            if j == 1:
                send(half, j, 1, me.second_peer(half, 3), j, 2)
            if j == 3:
                send(half, j, 3 - 2 * me.c, me.second_peer(half, 1 + 2 * me.c), j, 2)
        for half in range(2):
            landed(half, j, 3)
            landed(half, j, 1)
        yield
    for j in (0, 1, 3, 2):
        for half in range(2):
            arrived(half, j, 2)
            landed(half, j, 2)
        yield


def scatter_plane(me, own, touch, finish, start, all_here, bufs, sems):
    pass_r, ring_r, line_r = bufs
    sends, pass_recv, ring_recv, line_recv = sems

    def far(half, j):
        return remote(
            own(half, j, 2), pass_r.at[half, j - 1], sends, pass_recv.at[half, j - 1],
            me.second_peer(half, 1 if j == 2 else 3),
        )

    def near(half, j, k):
        slot = j * 3 + k - 1
        return remote(
            own(half, j, k), ring_r.at[half, slot], sends, ring_recv.at[half, j],
            me.second_peer(half, k),
        )

    def line(half, j):
        return remote(
            own(half, j, 0), line_r.at[half, j - 1], sends, line_recv.at[half],
            me.first_peer(half, j),
        )

    def give(j, k):
        for half in range(2):
            own(half, j, k)[...] = touch(half, j, k).astype(BF16)
            start(near(half, j, k))

    def give_passed(j, k):
        for half in range(2):
            value = touch(half, j, k)
            far(half, j).wait_recv()
            value = value + pass_r[half, j - 1].astype(F32)
            own(half, j, k)[...] = value.astype(BF16)
            start(near(half, j, k))

    def gathered(half, j):
        value = touch(half, j, 0)
        steps = (1, 3) if j in (1, 2) else (1, 3, 2)
        all_here(ring_r.at[half, pl.ds(0, len(steps))], ring_recv.at[half, j])
        for k in steps:
            value = value + ring_r[half, j * 3 + k - 1].astype(F32)
        return value

    for j in (2, 1):
        for half in range(2):
            own(half, j, 2)[...] = touch(half, j, 2).astype(BF16)
            start(far(half, j))
        yield
    give(2, 3)
    give(1, 1)
    yield
    give(3, 2)
    give(3, 1)
    give(3, 3)
    yield
    give_passed(2, 1)
    give_passed(1, 3)
    yield
    give(0, 2)
    give(0, 1)
    give(0, 3)
    yield
    for j in (2, 1, 3):
        for half in range(2):
            own(half, j, 0)[...] = gathered(half, j).astype(BF16)
            start(line(half, j))
        yield
    for half in range(2):
        value = gathered(half, 0)
        all_here(line_r.at[half], line_recv.at[half])
        for j in (1, 3, 2):
            value = value + line_r[half, j - 1].astype(F32)
        finish(half, value)
    yield


def kernel(
    lengths, q_hbm, cache_hbm, uv_hbm, out_w_hbm, residual_hbm, gain_hbm, gate_hbm, up_hbm, down_hbm,
    routes_hbm, route_weights_hbm, out,
    gain, routes, route_weights, qv, cv, uv, out_w, res, down_w, gate_up_t, down_t,
    ctx, by_head, by_head_f, heads_all, part, part_b, part_r, hid, hid_t, gate_up,
    act, contrib, from_sib, plane_sum, plane_sum_b, tp_r, weight_row,
    b_pass, b_ring, b_line, a_ring, a_sum, ya_pass, ya_ring,
    load_sem, send_sems, a2a_recv, ag_recv, ag_sib_recv, rs_recv, hy_recv,
    ga_recv, gy_recv, gb_recv, gather_sib_recv,
    sib_recv, yp_recv, yr_recv, ar_recv, bp_recv, br_recv, bl_recv, tp_recv,
):
    me = Place()
    y, d = me.y, me.d
    own_lanes = pl.ds(pl.multiple_of(y * TP_ROWS, TP_ROWS), TP_ROWS)

    loads = {}
    sends = [Sends(send_sems, group) for group in range(6)]
    early_send, rs_send, gather_send, ga_send, sum_send, ar_send = sends

    def load(name, src, dst, index):
        copy = pltpu.make_async_copy(src, dst, load_sem.at[index])
        copy.start()
        loads[name] = copy

    def ready(name):
        loads.pop(name).wait()

    def start(copy):
        copy.start()

    def all_here(ref, recv):
        remote(ref, ref, early_send, recv, me.sibling()).wait_recv()

    load("q", q_hbm, qv, 0)
    for i in range(OWN_ROWS):
        load(("cache", i), cache_hbm.at[i], cv.at[i], 1 + i)

    barrier = pltpu.get_barrier_semaphore()
    peers = [me.sibling()]
    for step in (1, 2, 3):
        peers += [me.first_peer(0, step), me.first_peer(1, step), me.tp_peer(step)]
    for peer in peers:
        pl.semaphore_signal(barrier, inc=1, device_id=peer, device_id_type=MESH)

    def heads_out(row, half, step):
        to = lax.rem(y + step, 4) * OWN_HEADS + half * HALF_HEADS
        return remote(
            ctx.at[row, pl.ds(pl.multiple_of(to, HALF_HEADS), HALF_HEADS)],
            by_head.at[y * OWN_ROWS + row, pl.ds(half * HALF_HEADS, HALF_HEADS)],
            early_send, a2a_recv.at[half], me.tp_peer(step),
        )

    ready("q")
    for i in range(OWN_ROWS):
        ready(("cache", i))
        if i == 1:
            load("uv", uv_hbm, uv, 5)
            load("out_w", out_w_hbm, out_w, 6)
            load("res", residual_hbm.at[:, own_lanes], res, 7)
        if i == 2:
            load("gate", gate_hbm, contrib.at[:, pl.ds(0, UNITS)], 8)
            load("up", up_hbm, contrib.at[:, pl.ds(UNITS, UNITS)], 9)
            load("down", down_hbm, down_w, 10)
            load("gain", gain_hbm, gain, 11)
            load("routes", routes_hbm, routes, 12)
            load("route_weights", route_weights_hbm, route_weights, 13)
        scores = tn_dot(qv[i], cv[i]) * score_scale
        usable = lax.broadcasted_iota(jnp.int32, scores.shape, 1) < lengths[i]
        peak = jnp.max(jnp.where(usable, scores, -1e30), axis=1, keepdims=True)
        soft = jnp.where(usable, jnp.exp(scores - peak), 0.0)
        total = jnp.sum(soft, axis=1, keepdims=True)
        summed = nt_dot(soft.astype(BF16), cv[i, :LAT, :])
        ctx[i] = (summed / total).astype(BF16)
        by_head[y * OWN_ROWS + i] = ctx[
            i, pl.ds(pl.multiple_of(y * OWN_HEADS, OWN_HEADS), OWN_HEADS), :
        ]
        if i == 2:
            pl.semaphore_wait(barrier, len(peers))
        if i >= 2:
            for row in (0, 1, 2) if i == 2 else (3,):
                for step in (2, 1, 3):
                    start(heads_out(row, 0, step))
    for i in range(OWN_ROWS):
        for step in (2, 1, 3):
            start(heads_out(i, 1, step))

    ready("uv")
    own_rows = pl.ds(pl.multiple_of(d * DP_ROWS, DP_ROWS), DP_ROWS)

    def project(half):
        others = by_head.at[pl.ds(0, DP_ROWS - OWN_ROWS), pl.ds(0, HALF_HEADS)]
        all_here(others, a2a_recv.at[half])
        heads = pl.ds(half * HALF_HEADS, HALF_HEADS)
        for part_of in range(LAT // 128):
            piece = by_head[:, heads, pl.ds(part_of * 128, 128)]
            by_head_f[part_of] = piece.astype(F32).reshape(DP_ROWS * HALF_HEADS, 128)
        for h in range(HALF_HEADS):
            picked = jnp.concatenate(
                [
                    by_head_f[part_of, pl.ds(h, DP_ROWS, stride=HALF_HEADS), :]
                    for part_of in range(LAT // 128)
                ],
                axis=1,
            ).astype(BF16)
            at = half * HALF_HEADS + h
            heads_all[own_rows, pl.ds(at * VHEAD, VHEAD)] = jnp.dot(
                picked, uv[at], preferred_element_type=F32
            ).astype(BF16)

    project(0)
    def head_block(half, dp):
        return heads_all.at[
            pl.ds(pl.multiple_of(dp * DP_ROWS, DP_ROWS), DP_ROWS), pl.ds(half * (INNER // 2), INNER // 2)
        ]

    def head_sibling(half, j, k, c):
        ref = head_block(half, me.block(half, j, k, c))
        return remote(
            ref, ref, early_send, ag_sib_recv.at[half], me.sibling()
        )

    def turn_step(i, carry):
        at = pl.ds(pl.multiple_of(i * 128, 128), 128)
        turned = contrib[at, :].astype(F32).T * gain[pl.ds(i, 1), :]
        gate_up_t[:, at] = turned.astype(BF16)
        down_t[at, :] = down_w[:, at].astype(F32).T.astype(BF16)
        return carry

    turned_to = 0
    heads_plane = gather_plane(
        me, head_block, start, (early_send, ag_recv), lambda *at: start(head_sibling(*at, me.c))
    )
    next(heads_plane)
    project(1)
    for step in heads_plane:
        if turned_to == 0:
            for name in ("gate", "up", "down", "gain"):
                ready(name)
        upto = min(turned_to + 7, D // 128)
        lax.fori_loop(turned_to, upto, turn_step, 0)
        turned_to = upto

    ready("out_w")
    part[...] = jnp.zeros_like(part)

    def out_step(k, carry):
        at = pl.ds(pl.multiple_of(k * 512, 512), 512)
        part[...] += nt_dot(out_w[:, at], heads_all[:, at])
        return carry

    for half in range(2):
        all_here(heads_all.at[pl.ds(0, ROWS // 2), pl.ds(0, INNER // 2)], ag_sib_recv.at[half])
        lax.fori_loop(half * 4, half * 4 + 4, out_step, 0)
    for block in range(4):
        part_b[block] = part[:, block * TP_ROWS : (block + 1) * TP_ROWS].astype(BF16)
    for step in (2, 1, 3):
        start(remote(
            part_b.at[lax.rem(y + step, 4)], part_r.at[step - 1],
            rs_send, rs_recv.at[0], me.tp_peer(step),
        ))

    ready("routes")
    ready("route_weights")
    weight_row[...] = jnp.sum(
        jnp.where(routes[...] == d, route_weights[...], 0.0), axis=0, keepdims=True
    )

    ready("res")
    total = res[...].astype(F32) + part[:, own_lanes]
    all_here(part_r, rs_recv.at[0])
    for step in (1, 2, 3):
        total = total + part_r[step - 1].astype(F32)
    hidden = total.astype(BF16)
    hid[...] = hidden.astype(F32)
    own_cols = pl.ds(pl.multiple_of(d * COLS, 16), COLS)
    hid_t[own_cols, own_lanes] = hidden

    pairs = [(dz, dx) for dz in range(4) for dx in range(4)]

    def b_block(half, dp):
        return hid_t.at[rows_of(dp, PART_A + half * (PART_B // 2), PART_B // 2), :]

    def pair_of(half, j, k):
        return (k, j) if half == 0 else (j, k)

    nearest = sorted(pairs, key=lambda pair: sum((0, 1, 2, 1)[step] for step in pair))
    passed_on = nearest[:PASSED]

    def a_tp(pair, slot, lanes, step):
        ref = hid_t.at[rows_of(me.at(*pair, me.c), 0, PART_A), lanes]
        n = pair[0] * 4 + pair[1]
        alone = pair in passed_on and slot == sum(pair) % 2
        return remote(
            ref, ref, gather_send, gy_recv.at[n, 0 if alone else 1], me.tp_peer(step)
        )

    def a_sibling(pair, c):
        ref = hid_t.at[rows_of(me.at(*pair, c), 0, PART_A), :]
        return remote(ref, ref, gather_send, gather_sib_recv.at[0], me.sibling())

    def a_plane(pair):
        ref = hid_t.at[rows_of(d, 0, PART_A), own_lanes]
        opposite = (4 - pair[0]) % 4 * 4 + (4 - pair[1]) % 4
        return remote(ref, ref, ga_send, ga_recv.at[opposite], me.pair_peer(pair))

    a_landed = []

    def a_here(pair):
        a_landed.append(pair)
        start(a_tp(pair, 0, me.lanes(0), 1))
        start(a_tp(pair, 1, me.lanes(0), 3))
        if len(a_landed) > PASSED:
            start(a_tp(pair, 2, me.lanes(0), 2))

    a_passed, a_done = [0], [0]

    def a_pass_on(count):
        for pair in a_landed[a_passed[0] : min(a_passed[0] + count, PASSED)]:
            if sum(pair) % 2 == 0:
                a_tp(pair, 0, me.lanes(3), 1).wait_recv()
                start(a_tp(pair, 2, me.lanes(3), 1))
            else:
                a_tp(pair, 1, me.lanes(1), 3).wait_recv()
                start(a_tp(pair, 2, me.lanes(1), 3))
        a_passed[0] += count

    def a_finish(count):
        for n in range(a_done[0], min(a_done[0] + count, 16)):
            pair = a_landed[n]
            copies = 2 if pair in passed_on else 3
            all_here(ya_pass.at[pl.ds(0, copies)], gy_recv.at[pair[0] * 4 + pair[1], 1])
            start(a_sibling(pair, me.c))
        a_done[0] += count

    def b_sibling(half, j, k, c):
        ref = b_block(half, me.block(half, j, k, c))
        return remote(ref, ref, gather_send, gather_sib_recv.at[0], me.sibling())

    def b_tp(lanes, step):
        ref = hid_t.at[rows_of(d, PART_A, PART_B), lanes]
        return remote(ref, ref, gather_send, hy_recv.at[0], me.tp_peer(step))

    b_plane = gather_plane(
        me, b_block, start, (gather_send, gb_recv), lambda *at: start(b_sibling(*at, me.c))
    )
    for step in (1, 3, 2):
        start(b_tp(me.lanes(0), step))
    for pair in nearest[1:]:
        start(a_plane(pair))
    a_here((0, 0))
    for pair in nearest[1:5]:
        opposite = ((4 - pair[0]) % 4, (4 - pair[1]) % 4)
        a_plane(opposite).wait_recv()
        a_here(pair)
    all_here(tp_r, hy_recv.at[0])
    next(b_plane)
    next(b_plane)
    a_pass_on(1)
    for pair in nearest[5:]:
        opposite = ((4 - pair[0]) % 4, (4 - pair[1]) % 4)
        a_plane(opposite).wait_recv()
        a_here(pair)
    a_pass_on(3)
    next(b_plane)
    next(b_plane)
    a_pass_on(4)
    next(b_plane)
    a_pass_on(2)
    next(b_plane)
    a_pass_on(2)
    for _ in range(2):
        a_finish(3)
        next(b_plane)
    for _ in range(4):
        a_finish(2)
        next(b_plane)
    a_finish(16)
    all_here(hid_t.at[pl.ds(0, D // 2)], gather_sib_recv.at[0])

    gate_up[...] = jnp.zeros_like(gate_up)

    def expert_step(k, squares):
        at = pl.ds(pl.multiple_of(k * 1024, 1024), 1024)
        rows = hid_t[at, :]
        gate_up[...] += jnp.dot(gate_up_t[:, at], rows, preferred_element_type=F32)
        wide = rows.astype(F32)
        return squares + jnp.sum((wide * wide).reshape(128, 8, ROWS), axis=0)

    squares = lax.fori_loop(0, D // 1024, expert_step, jnp.zeros((8, ROWS), F32))
    inverse_rms = lax.rsqrt(jnp.sum(squares, axis=0, keepdims=True) * (1.0 / D) + epsilon)
    gate_proj = gate_up[:UNITS, :] * inverse_rms
    up_proj = gate_up[UNITS:, :] * inverse_rms
    silu = gate_proj / (1.0 + jnp.exp(-gate_proj))
    act[...] = (silu * up_proj * weight_row[...]).astype(BF16)

    def from_core(pair, c):
        n = pair[0] * 4 + pair[1]
        return remote(
            contrib.at[rows_of(me.at(*pair, c), 0, COLS), :], from_sib.at[n],
            sum_send, sib_recv.at[n], me.sibling(),
        )

    def compute(pair):
        at = pl.ds(pl.multiple_of(me.at(*pair, 0) * COLS, 16), 2 * COLS)
        contrib[at, :] = jnp.dot(down_t[at, :], act[...], preferred_element_type=F32).astype(BF16)
        start(from_core(pair, 1 - me.c))

    sib_here = set()

    def sibling_here(pair):
        if pair not in sib_here:
            sib_here.add(pair)
            from_core(pair, me.c).wait_recv()

    def ya_rows(pair):
        return rows_of(me.at(*pair, me.c), 0, SUM_A)

    def ya_far(pair, step):
        n = pair[0] * 4 + pair[1]
        return remote(
            contrib.at[ya_rows(pair), me.lanes(2)], ya_pass.at[n],
            sum_send, yp_recv.at[n], me.tp_peer(step),
        )

    def ya_near(pair, step):
        n = pair[0] * 4 + pair[1]
        return remote(
            contrib.at[ya_rows(pair), me.lanes(step)], ya_ring.at[n, step - 1],
            sum_send, yr_recv.at[n], me.tp_peer(step),
        )

    passed_pairs = []

    def a_first(pair):
        sibling_here(pair)
        at = ya_rows(pair)
        theirs = from_sib[pair[0] * 4 + pair[1], :SUM_A, :]
        contrib[at, :] = (contrib[at, :].astype(F32) + theirs.astype(F32)).astype(BF16)
        if len(passed_pairs) < SUM_PASSED:
            passed_pairs.append(pair)
            far_step = 1 if sum(pair) % 2 == 0 else 3
            start(ya_far(pair, far_step))
            start(ya_near(pair, 4 - far_step))
        else:
            for step in (1, 3, 2):
                start(ya_near(pair, step))

    def a_second(pair):
        step = 1 if sum(pair) % 2 == 0 else 3
        ya_far(pair, step).wait_recv()
        at = ya_rows(pair)
        passed = ya_pass[pair[0] * 4 + pair[1]].astype(F32)
        contrib[at, me.lanes(step)] = (contrib[at, me.lanes(step)].astype(F32) + passed).astype(BF16)
        start(ya_near(pair, step))

    def a_give(pair):
        n = pair[0] * 4 + pair[1]
        return remote(
            a_sum.at[n], a_ring.at[n - 1], ar_send, ar_recv.at[0], me.pair_peer(pair)
        )

    def a_third(pair):
        n = pair[0] * 4 + pair[1]
        value = contrib[ya_rows(pair), own_lanes].astype(F32)
        steps = (1, 3) if pair in passed_pairs else (1, 3, 2)
        all_here(ya_ring.at[n, pl.ds(0, len(steps))], yr_recv.at[n])
        for step in steps:
            value = value + ya_ring[n, step - 1].astype(F32)
        a_sum[n] = value.astype(BF16)
        if n:
            start(a_give(pair))

    def b_own(half, j, k):
        return contrib.at[
            rows_of(me.block(half, j, k, me.c), SUM_A + half * (SUM_B // 2), SUM_B // 2), :
        ]

    def b_touch(half, j, k):
        pair = pair_of(half, j, k)
        sibling_here(pair)
        theirs = from_sib[
            pair[0] * 4 + pair[1], pl.ds(SUM_A + half * (SUM_B // 2), SUM_B // 2), :
        ]
        return b_own(half, j, k)[...].astype(F32) + theirs.astype(F32)

    def b_final(half, value):
        at = pl.ds(half * (SUM_B // 2), SUM_B // 2)
        plane_sum[at, :] = value
        plane_sum_b[at, :] = value.astype(BF16)

    b_back = scatter_plane(
        me, b_own, b_touch, b_final, start, all_here, (b_pass, b_ring, b_line),
        (sum_send, bp_recv, br_recv, bl_recv),
    )
    order = [(2, 2), (2, 1), (1, 2), (3, 2), (2, 3), (1, 1), (1, 3), (3, 1), (3, 3)]
    order += [(2, 0), (0, 2), (1, 0), (0, 1), (3, 0), (0, 3), (0, 0)]
    for n, pair in enumerate(order):
        compute(pair)
        if n in (3, 6, 9, 12):
            next(b_back)
        if n >= 3:
            a_first(order[n - 3])
        if n >= 14:
            a_second(order[n - 14])
    for n in range(13, 16):
        a_first(order[n])
        a_second(order[n - 11])
    next(b_back)
    next(b_back)
    for n in range(5, SUM_PASSED):
        a_second(order[n])
    for n, pair in enumerate(order):
        a_third(pair)
        if n in (3, 7, 11):
            next(b_back)
    next(b_back)

    def b_tp_sum(step):
        return remote(
            plane_sum_b.at[:, me.lanes(step)], tp_r.at[step - 1],
            sum_send, tp_recv.at[0], me.tp_peer(step),
        )

    for step in (2, 1, 3):
        start(b_tp_sum(step))
    moe = a_sum[0].astype(F32)
    all_here(a_ring, ar_recv.at[0])
    for pair in order[:-1]:
        moe = moe + a_ring[pair[0] * 4 + pair[1] - 1].astype(F32)
    out[:SUM_A, :] = (hid[:SUM_A, :] + moe).astype(BF16)
    moe = plane_sum[:, own_lanes]
    all_here(tp_r, tp_recv.at[0])
    for step in (1, 3, 2):
        moe = moe + tp_r[step - 1].astype(F32)
    out[SUM_A:, :] = (hid[SUM_A:, :] + moe).astype(BF16)

    for group in sends:
        sized = {id(rs_send): part_r, id(ga_send): a_ring, id(ar_send): a_ring}.get(id(group))
        if sized is None:
            sized = hid_t.at[pl.ds(0, group.total // (2 * ROWS))]
        assert group.total == 2 * math.prod(sized.shape), group.total
        remote(sized, sized, group, rs_recv.at[0], me.sibling()).copy.wait_send()


def local(
    queries, latent_cache, lengths, uv_weight, out_weight, residual, norm_gain,
    gate_weight, up_weight, down_weight, routes, route_weights,
):
    anywhere = pl.BlockSpec(memory_space=pl.ANY)
    vmem = pl.BlockSpec(memory_space=pltpu.VMEM)
    smem = pl.BlockSpec(memory_space=pltpu.SMEM)
    dma = pltpu.SemaphoreType.DMA
    scratch = [
        pltpu.VMEM((D // 128, 128), F32),
        pltpu.VMEM(routes.shape[::-1], jnp.int32),
        pltpu.VMEM(routes.shape[::-1], F32),
        pltpu.VMEM((OWN_ROWS, KEY, HEADS), BF16),
        pltpu.VMEM((OWN_ROWS, KEY, CTX), BF16),
        pltpu.VMEM((OWN_HEADS, LAT, VHEAD), BF16),
        pltpu.VMEM((COLS, INNER), BF16),
        pltpu.VMEM((COLS, TP_ROWS), BF16),
        pltpu.VMEM((UNITS, D), BF16),
        pltpu.VMEM((2 * UNITS, D), BF16),
        pltpu.VMEM((D, UNITS), BF16),
        pltpu.VMEM((OWN_ROWS, HEADS, LAT), BF16),
        pltpu.VMEM((DP_ROWS, OWN_HEADS, LAT), BF16),
        pltpu.VMEM((LAT // 128, DP_ROWS * HALF_HEADS, 128), F32),
        pltpu.VMEM((ROWS, INNER), BF16),
        pltpu.VMEM((COLS, ROWS), F32),
        pltpu.VMEM((4, COLS, TP_ROWS), BF16),
        pltpu.VMEM((3, COLS, TP_ROWS), BF16),
        pltpu.VMEM((COLS, TP_ROWS), F32),
        pltpu.VMEM((D, ROWS), BF16),
        pltpu.VMEM((2 * UNITS, ROWS), F32),
        pltpu.VMEM((UNITS, ROWS), BF16),
        pltpu.VMEM((D, ROWS), BF16),
        pltpu.VMEM((16, COLS, ROWS), BF16),
        pltpu.VMEM((SUM_B, ROWS), F32),
        pltpu.VMEM((SUM_B, ROWS), BF16),
        pltpu.VMEM((3, SUM_B, TP_ROWS), BF16),
        pltpu.VMEM((1, ROWS), F32),
        pltpu.VMEM((2, 2, SUM_B // 2, ROWS), BF16),
        pltpu.VMEM((2, 12, SUM_B // 2, ROWS), BF16),
        pltpu.VMEM((2, 3, SUM_B // 2, ROWS), BF16),
        pltpu.VMEM((15, SUM_A, TP_ROWS), BF16),
        pltpu.VMEM((16, SUM_A, TP_ROWS), BF16),
        pltpu.VMEM((16, SUM_A, TP_ROWS), BF16),
        pltpu.VMEM((16, 3, SUM_A, TP_ROWS), BF16),
        dma((14,)), dma((6,)),
        dma((2,)), dma((2, 16)), dma((2,)),
        dma((1,)), dma((1,)),
        dma((16,)), dma((16, 2)), dma((2, 16)), dma((1,)),
        dma((16,)), dma((16,)), dma((16,)), dma((1,)),
        dma((2, 2)), dma((2, 4)), dma((2,)), dma((1,)),
    ]
    return pl.pallas_call(
        kernel,
        out_shape=jax.ShapeDtypeStruct((COLS, TP_ROWS), BF16),
        in_specs=[smem] + [anywhere] * 11,
        out_specs=vmem,
        scratch_shapes=scratch,
        compiler_params=pltpu.CompilerParams(
            collective_id=0, has_side_effects=True, vmem_limit_bytes=62 * 1024 * 1024
        ),
        name="decode_step",
    )(
        lengths, jnp.swapaxes(queries, 1, 2), jnp.swapaxes(latent_cache, 1, 2), uv_weight,
        out_weight.T, residual.T, norm_gain.reshape(D // 128, 128),
        gate_weight[0], up_weight[0], down_weight[0], routes.T, route_weights.T,
    ).T


def solution(mesh):
    placed = (
        P(("dp", "tp"), None, None),
        P(("dp", "tp"), None, None),
        P(("dp", "tp")),
        P("tp", None, None),
        P("tp", "dp"),
        P(None, "dp"),
        P(),
        P("dp", None, "tp"),
        P("dp", None, "tp"),
        P("dp", "tp", None),
        P(),
        P(),
    )
    return jax.shard_map(
        local, mesh=mesh, in_specs=placed, out_specs=P("tp", "dp"), check_vma=False
    )
```

```python
import math

import jax
import jax.numpy as jnp
from jax import lax
from jax.experimental import pallas as pl
from jax.experimental.pallas import tpu as pltpu
from jax.sharding import PartitionSpec as P

F32 = jnp.float32
BF16 = jnp.bfloat16
MESH = pl.DeviceIdType.MESH

LAT = 512
KEY = 576
CTX = 1024
HEADS = 128
OWN_HEADS = 32
HALF_HEADS = 16
VHEAD = 128
ROWS = 512
OWN_ROWS = 4
DP_ROWS = 16
TP_ROWS = 128
D = 7168
COLS = 224
PART_A = 96
PART_B = 128
INNER = 4096
UNITS = 256
DP = 32

score_scale = 192.0 ** (-0.5)
epsilon = 1e-06

SUM_A = 96
SUM_B = 128
BY_RIGHT = (2, 0)


def tn_dot(a, b):
    return lax.dot_general(a, b, (((0,), (0,)), ((), ())), preferred_element_type=F32)


def nt_dot(a, b):
    return lax.dot_general(a, b, (((1,), (1,)), ((), ())), preferred_element_type=F32)


class Place:
    def __init__(self):
        dp = lax.axis_index("dp")
        self.y = lax.axis_index("tp")
        self.d = dp
        self.c = lax.rem(dp, 2)
        self.x = lax.rem(dp // 2, 4)
        self.z = dp // 8

    def device(self, z=None, x=None, c=None, y=None):
        z = self.z if z is None else z
        x = self.x if x is None else x
        c = self.c if c is None else c
        y = self.y if y is None else y
        return ((z * 4 + x) * 2 + c, y)

    def sibling(self):
        return self.device(c=1 - self.c)

    def tp_peer(self, step):
        return self.device(y=lax.rem(self.y + step, 4))

    def first(self, half):
        return self.x if half == 0 else self.z

    def second(self, half):
        return self.z if half == 0 else self.x

    def first_peer(self, half, step):
        if half == 0:
            return self.device(x=lax.rem(self.x + step, 4))
        return self.device(z=lax.rem(self.z + step, 4))

    def second_peer(self, half, step):
        return self.first_peer(1 - half, step)

    def pair_peer(self, pair):
        return (self.at(*pair, self.c), self.y)

    def lanes(self, step):
        at = lax.rem(self.y + step, 4) * TP_ROWS
        return pl.ds(pl.multiple_of(at, TP_ROWS), TP_ROWS)

    def at(self, dz, dx, c):
        return (lax.rem(self.z + dz, 4) * 4 + lax.rem(self.x + dx, 4)) * 2 + c

    def block(self, half, j, k, c):
        a = lax.rem(self.first(half) + j, 4)
        b = lax.rem(self.second(half) + k, 4)
        z, x = (b, a) if half == 0 else (a, b)
        return (z * 4 + x) * 2 + c


class Sends:
    def __init__(self, sems, group):
        self.sem, self.total, self.at = sems.at[group], 0, self

    def __getitem__(self, index):
        return self


class Copy:
    def __init__(self, src, dst, send, recv, device):
        self.sends, self.bytes = send, 2 * math.prod(src.shape)
        self.copy = pltpu.make_async_remote_copy(
            src_ref=src, dst_ref=dst, send_sem=send.sem, recv_sem=recv,
            device_id=device, device_id_type=MESH,
        )

    def start(self):
        self.sends.total += self.bytes
        self.copy.start()

    def wait_recv(self):
        self.copy.wait_recv()


def remote(src, dst, send, recv, device):
    return Copy(src, dst, send, recv, device)


def rows_of(dp, offset, count):
    return pl.ds(pl.multiple_of(dp * COLS + offset, 16), count)


def gather_plane(me, blk, start, sems, landed):
    send_sem, recv_sem = sems

    def ref_of(half, j, k):
        return blk(half, me.block(half, j, k, me.c))

    def send(half, j, k, device, rj, rk):
        ref = ref_of(half, j, k)
        start(remote(
            ref, ref, send_sem, recv_sem.at[half, rj * 4 + rk], device
        ))

    def arrived(half, j, k):
        ref = ref_of(half, j, k)
        remote(
            ref, ref, send_sem, recv_sem.at[half, j * 4 + k], me.sibling()
        ).wait_recv()

    def second_axis(half, j):
        send(half, j, 0, me.second_peer(half, 1), j, 3)
        send(half, j, 0, me.second_peer(half, 3), j, 1)
        if j == 2:
            send(half, j, 0, me.second_peer(half, 2), j, 2)

    for half in range(2):
        for step in (1, 3, 2):
            send(half, 0, 0, me.first_peer(half, step), 4 - step, 0)
        second_axis(half, 0)
        landed(half, 0, 0)
        yield
    for j in (1, 3):
        for half in range(2):
            arrived(half, j, 0)
            second_axis(half, j)
    for j in (1, 3):
        for half in range(2):
            landed(half, j, 0)
    yield
    for half in range(2):
        arrived(half, 2, 0)
        second_axis(half, 2)
    for half in range(2):
        landed(half, 2, 0)
    yield
    for j in (0, 1, 3, 2):
        for half in range(2):
            arrived(half, j, 3)
            if j == 0:
                send(half, j, 3, me.second_peer(half, 1), j, 2)
            arrived(half, j, 1)
            if j == 1:
                send(half, j, 1, me.second_peer(half, 3), j, 2)
            if j == 3:
                send(half, j, 3 - 2 * me.c, me.second_peer(half, 1 + 2 * me.c), j, 2)
        for half in range(2):
            landed(half, j, 3)
            landed(half, j, 1)
        yield
    for j in (0, 1, 3, 2):
        for half in range(2):
            arrived(half, j, 2)
            landed(half, j, 2)
        yield


def scatter_plane(me, own, touch, finish, start, all_here, bufs, sems):
    pass_r, ring_r, line_r = bufs
    sends, pass_recv, ring_recv, line_recv = sems

    def far(half, j):
        return remote(
            own(half, j, 2), pass_r.at[half, j], sends, pass_recv.at[half, j],
            me.second_peer(half, 1 if j in BY_RIGHT else 3),
        )

    def near(half, j, k):
        return remote(
            own(half, j, k), ring_r.at[half, j * 2 + k // 2], sends, ring_recv.at[half, j],
            me.second_peer(half, k),
        )

    def line(half, j):
        return remote(
            own(half, j, 0), line_r.at[half, j - 1], sends, line_recv.at[half],
            me.first_peer(half, j),
        )

    def gathered(half, j):
        value = touch(half, j, 0)
        all_here(ring_r.at[half, pl.ds(0, 2)], ring_recv.at[half, j])
        for slot in (j * 2, j * 2 + 1):
            value = value + ring_r[half, slot].astype(F32)
        return value

    for j in (2, 1, 3, 0):
        for half in range(2):
            own(half, j, 2)[...] = touch(half, j, 2).astype(BF16)
            start(far(half, j))
        yield
    for j in (2, 1, 0, 3):
        k = 3 if j in BY_RIGHT else 1
        for half in range(2):
            own(half, j, k)[...] = touch(half, j, k).astype(BF16)
            start(near(half, j, k))
        yield
    for j in (2, 1, 3, 0):
        k = 1 if j in BY_RIGHT else 3
        for half in range(2):
            value = touch(half, j, k)
            far(half, j).wait_recv()
            value = value + pass_r[half, j].astype(F32)
            own(half, j, k)[...] = value.astype(BF16)
            start(near(half, j, k))
        yield
    for j in (2, 1, 3):
        for half in range(2):
            own(half, j, 0)[...] = gathered(half, j).astype(BF16)
            start(line(half, j))
        yield
    for half in range(2):
        value = gathered(half, 0)
        all_here(line_r.at[half], line_recv.at[half])
        for j in (1, 3, 2):
            value = value + line_r[half, j - 1].astype(F32)
        finish(half, value)
    yield


def kernel(
    lengths, q_hbm, cache_hbm, uv_hbm, out_w_hbm, residual_hbm, gain_hbm, gate_hbm, up_hbm, down_hbm,
    routes_hbm, route_weights_hbm, out,
    gain, routes, route_weights, qv, cv, uv, out_w, res, down_w, gate_up_t, down_t,
    ctx, by_head, by_head_f, heads_all, part, part_b, part_r, hid, hid_t, gate_up,
    act, contrib, from_sib, plane_sum, plane_sum_b, tp_r, weight_row,
    b_pass, b_ring, b_line, a_ring, a_sum, ya_pass, ya_ring,
    load_sem, send_sems, a2a_recv, ag_recv, ag_sib_recv, rs_recv, hy_recv,
    ga_recv, gy_recv, gb_recv, gather_sib_recv,
    sib_recv, yp_recv, yr_recv, ar_recv, bp_recv, br_recv, bl_recv, tp_recv,
):
    me = Place()
    y, d = me.y, me.d
    own_lanes = pl.ds(pl.multiple_of(y * TP_ROWS, TP_ROWS), TP_ROWS)

    loads = {}
    sends = [Sends(send_sems, group) for group in range(6)]
    early_send, rs_send, gather_send, ga_send, sum_send, ar_send = sends

    def load(name, src, dst, index):
        copy = pltpu.make_async_copy(src, dst, load_sem.at[index])
        copy.start()
        loads[name] = copy

    def ready(name):
        loads.pop(name).wait()

    def start(copy):
        copy.start()

    def all_here(ref, recv):
        remote(ref, ref, early_send, recv, me.sibling()).wait_recv()

    load("q", q_hbm, qv, 0)
    for i in range(OWN_ROWS):
        load(("cache", i), cache_hbm.at[i], cv.at[i], 1 + i)

    barrier = pltpu.get_barrier_semaphore()
    peers = [me.sibling()]
    for step in (1, 2, 3):
        peers += [me.first_peer(0, step), me.first_peer(1, step), me.tp_peer(step)]
    for peer in peers:
        pl.semaphore_signal(barrier, inc=1, device_id=peer, device_id_type=MESH)

    def heads_out(row, half, step):
        to = lax.rem(y + step, 4) * OWN_HEADS + half * HALF_HEADS
        return remote(
            ctx.at[row, pl.ds(pl.multiple_of(to, HALF_HEADS), HALF_HEADS)],
            by_head.at[y * OWN_ROWS + row, pl.ds(half * HALF_HEADS, HALF_HEADS)],
            early_send, a2a_recv.at[half], me.tp_peer(step),
        )

    ready("q")
    for i in range(OWN_ROWS):
        ready(("cache", i))
        if i == 1:
            load("uv", uv_hbm, uv, 5)
            load("out_w", out_w_hbm, out_w, 6)
            load("res", residual_hbm.at[:, own_lanes], res, 7)
        if i == 2:
            load("gate", gate_hbm, contrib.at[:, pl.ds(0, UNITS)], 8)
            load("up", up_hbm, contrib.at[:, pl.ds(UNITS, UNITS)], 9)
            load("down", down_hbm, down_w, 10)
            load("gain", gain_hbm, gain, 11)
            load("routes", routes_hbm, routes, 12)
            load("route_weights", route_weights_hbm, route_weights, 13)
        scores = tn_dot(qv[i], cv[i]) * score_scale
        usable = lax.broadcasted_iota(jnp.int32, scores.shape, 1) < lengths[i]
        peak = jnp.max(jnp.where(usable, scores, -1e30), axis=1, keepdims=True)
        soft = jnp.where(usable, jnp.exp(scores - peak), 0.0)
        total = jnp.sum(soft, axis=1, keepdims=True)
        summed = nt_dot(soft.astype(BF16), cv[i, :LAT, :])
        ctx[i] = (summed / total).astype(BF16)
        by_head[y * OWN_ROWS + i] = ctx[
            i, pl.ds(pl.multiple_of(y * OWN_HEADS, OWN_HEADS), OWN_HEADS), :
        ]
        if i == 2:
            pl.semaphore_wait(barrier, len(peers))
        if i >= 2:
            for row in (0, 1, 2) if i == 2 else (3,):
                for step in (2, 1, 3):
                    start(heads_out(row, 0, step))
    for i in range(OWN_ROWS):
        for step in (2, 1, 3):
            start(heads_out(i, 1, step))

    ready("uv")
    own_rows = pl.ds(pl.multiple_of(d * DP_ROWS, DP_ROWS), DP_ROWS)

    def project(half):
        others = by_head.at[pl.ds(0, DP_ROWS - OWN_ROWS), pl.ds(0, HALF_HEADS)]
        all_here(others, a2a_recv.at[half])
        heads = pl.ds(half * HALF_HEADS, HALF_HEADS)
        for part_of in range(LAT // 128):
            piece = by_head[:, heads, pl.ds(part_of * 128, 128)]
            by_head_f[part_of] = piece.astype(F32).reshape(DP_ROWS * HALF_HEADS, 128)
        for h in range(HALF_HEADS):
            picked = jnp.concatenate(
                [
                    by_head_f[part_of, pl.ds(h, DP_ROWS, stride=HALF_HEADS), :]
                    for part_of in range(LAT // 128)
                ],
                axis=1,
            ).astype(BF16)
            at = half * HALF_HEADS + h
            heads_all[own_rows, pl.ds(at * VHEAD, VHEAD)] = jnp.dot(
                picked, uv[at], preferred_element_type=F32
            ).astype(BF16)

    project(0)
    def head_block(half, dp):
        return heads_all.at[
            pl.ds(pl.multiple_of(dp * DP_ROWS, DP_ROWS), DP_ROWS), pl.ds(half * (INNER // 2), INNER // 2)
        ]

    def head_sibling(half, j, k, c):
        ref = head_block(half, me.block(half, j, k, c))
        return remote(
            ref, ref, early_send, ag_sib_recv.at[half], me.sibling()
        )

    def turn_step(i, carry):
        at = pl.ds(pl.multiple_of(i * 128, 128), 128)
        turned = contrib[at, :].astype(F32).T * gain[pl.ds(i, 1), :]
        gate_up_t[:, at] = turned.astype(BF16)
        down_t[at, :] = down_w[:, at].astype(F32).T.astype(BF16)
        return carry

    turned_to = 0
    heads_plane = gather_plane(
        me, head_block, start, (early_send, ag_recv), lambda *at: start(head_sibling(*at, me.c))
    )
    next(heads_plane)
    project(1)
    for step in heads_plane:
        if turned_to == 0:
            for name in ("gate", "up", "down", "gain"):
                ready(name)
        upto = min(turned_to + 7, D // 128)
        lax.fori_loop(turned_to, upto, turn_step, 0)
        turned_to = upto

    ready("out_w")
    part[...] = jnp.zeros_like(part)

    def out_step(k, carry):
        at = pl.ds(pl.multiple_of(k * 512, 512), 512)
        part[...] += nt_dot(out_w[:, at], heads_all[:, at])
        return carry

    for half in range(2):
        all_here(heads_all.at[pl.ds(0, ROWS // 2), pl.ds(0, INNER // 2)], ag_sib_recv.at[half])
        lax.fori_loop(half * 4, half * 4 + 4, out_step, 0)
    for block in range(4):
        part_b[block] = part[:, block * TP_ROWS : (block + 1) * TP_ROWS].astype(BF16)
    for step in (2, 1, 3):
        start(remote(
            part_b.at[lax.rem(y + step, 4)], part_r.at[step - 1],
            rs_send, rs_recv.at[0], me.tp_peer(step),
        ))

    ready("routes")
    ready("route_weights")
    weight_row[...] = jnp.sum(
        jnp.where(routes[...] == d, route_weights[...], 0.0), axis=0, keepdims=True
    )

    ready("res")
    total = res[...].astype(F32) + part[:, own_lanes]
    all_here(part_r, rs_recv.at[0])
    for step in (1, 2, 3):
        total = total + part_r[step - 1].astype(F32)
    hidden = total.astype(BF16)
    hid[...] = hidden.astype(F32)
    own_cols = pl.ds(pl.multiple_of(d * COLS, 16), COLS)
    hid_t[own_cols, own_lanes] = hidden

    pairs = [(dz, dx) for dz in range(4) for dx in range(4)]

    def b_block(half, dp):
        return hid_t.at[rows_of(dp, PART_A + half * (PART_B // 2), PART_B // 2), :]

    def pair_of(half, j, k):
        return (k, j) if half == 0 else (j, k)

    nearest = sorted(pairs, key=lambda pair: sum((0, 1, 2, 1)[step] for step in pair))

    def a_tp(pair, slot, lanes, step):
        ref = hid_t.at[rows_of(me.at(*pair, me.c), 0, PART_A), lanes]
        n = pair[0] * 4 + pair[1]
        alone = slot == sum(pair) % 2
        return remote(
            ref, ref, gather_send, gy_recv.at[n, 0 if alone else 1], me.tp_peer(step)
        )

    def a_sibling(pair, c):
        ref = hid_t.at[rows_of(me.at(*pair, c), 0, PART_A), :]
        return remote(ref, ref, gather_send, gather_sib_recv.at[0], me.sibling())

    def a_plane(pair):
        ref = hid_t.at[rows_of(d, 0, PART_A), own_lanes]
        opposite = (4 - pair[0]) % 4 * 4 + (4 - pair[1]) % 4
        return remote(ref, ref, ga_send, ga_recv.at[opposite], me.pair_peer(pair))

    a_landed = []

    def a_here(pair):
        a_landed.append(pair)
        start(a_tp(pair, 0, me.lanes(0), 1))
        start(a_tp(pair, 1, me.lanes(0), 3))

    a_passed, a_done = [0], [0]

    def a_pass_on(count):
        for pair in a_landed[a_passed[0] : a_passed[0] + count]:
            if sum(pair) % 2 == 0:
                a_tp(pair, 0, me.lanes(3), 1).wait_recv()
                start(a_tp(pair, 2, me.lanes(3), 1))
            else:
                a_tp(pair, 1, me.lanes(1), 3).wait_recv()
                start(a_tp(pair, 2, me.lanes(1), 3))
        a_passed[0] += count

    def a_finish(count):
        for n in range(a_done[0], min(a_done[0] + count, 16)):
            pair = a_landed[n]
            all_here(ya_pass.at[pl.ds(0, 2)], gy_recv.at[pair[0] * 4 + pair[1], 1])
            start(a_sibling(pair, me.c))
        a_done[0] += count

    def b_sibling(half, j, k, c):
        ref = b_block(half, me.block(half, j, k, c))
        return remote(ref, ref, gather_send, gather_sib_recv.at[0], me.sibling())

    def b_tp(lanes, step):
        ref = hid_t.at[rows_of(d, PART_A, PART_B), lanes]
        return remote(ref, ref, gather_send, hy_recv.at[0], me.tp_peer(step))

    b_plane = gather_plane(
        me, b_block, start, (gather_send, gb_recv), lambda *at: start(b_sibling(*at, me.c))
    )
    for step in (1, 3, 2):
        start(b_tp(me.lanes(0), step))
    for pair in nearest[1:]:
        start(a_plane(pair))
    a_here((0, 0))
    for pair in nearest[1:5]:
        opposite = ((4 - pair[0]) % 4, (4 - pair[1]) % 4)
        a_plane(opposite).wait_recv()
        a_here(pair)
    all_here(tp_r, hy_recv.at[0])
    next(b_plane)
    next(b_plane)
    a_pass_on(1)
    for pair in nearest[5:]:
        opposite = ((4 - pair[0]) % 4, (4 - pair[1]) % 4)
        a_plane(opposite).wait_recv()
        a_here(pair)
    a_pass_on(3)
    next(b_plane)
    next(b_plane)
    for count in (4, 3, 3, 2):
        a_pass_on(count)
        next(b_plane)
    for _ in range(4):
        a_finish(3)
        next(b_plane)
    a_finish(16)
    all_here(hid_t.at[pl.ds(0, D // 2)], gather_sib_recv.at[0])

    gate_up[...] = jnp.zeros_like(gate_up)

    def expert_step(k, squares):
        at = pl.ds(pl.multiple_of(k * 1024, 1024), 1024)
        rows = hid_t[at, :]
        gate_up[...] += jnp.dot(gate_up_t[:, at], rows, preferred_element_type=F32)
        wide = rows.astype(F32)
        return squares + jnp.sum((wide * wide).reshape(128, 8, ROWS), axis=0)

    squares = lax.fori_loop(0, D // 1024, expert_step, jnp.zeros((8, ROWS), F32))
    inverse_rms = lax.rsqrt(jnp.sum(squares, axis=0, keepdims=True) * (1.0 / D) + epsilon)
    gate_proj = gate_up[:UNITS, :] * inverse_rms
    up_proj = gate_up[UNITS:, :] * inverse_rms
    silu = gate_proj / (1.0 + jnp.exp(-gate_proj))
    act[...] = (silu * up_proj * weight_row[...]).astype(BF16)

    def from_core(pair, c):
        n = pair[0] * 4 + pair[1]
        return remote(
            contrib.at[rows_of(me.at(*pair, c), 0, COLS), :], from_sib.at[n],
            sum_send, sib_recv.at[n], me.sibling(),
        )

    def compute(pair):
        at = pl.ds(pl.multiple_of(me.at(*pair, 0) * COLS, 16), 2 * COLS)
        contrib[at, :] = jnp.dot(down_t[at, :], act[...], preferred_element_type=F32).astype(BF16)
        start(from_core(pair, 1 - me.c))

    sib_here = set()

    def sibling_here(pair):
        if pair not in sib_here:
            sib_here.add(pair)
            from_core(pair, me.c).wait_recv()

    def ya_rows(pair):
        return rows_of(me.at(*pair, me.c), 0, SUM_A)

    def ya_far(pair, step):
        n = pair[0] * 4 + pair[1]
        return remote(
            contrib.at[ya_rows(pair), me.lanes(2)], ya_pass.at[n],
            sum_send, yp_recv.at[n], me.tp_peer(step),
        )

    def ya_near(pair, step):
        n = pair[0] * 4 + pair[1]
        return remote(
            contrib.at[ya_rows(pair), me.lanes(step)], ya_ring.at[n, step // 2],
            sum_send, yr_recv.at[n], me.tp_peer(step),
        )

    def far_step(pair):
        return 1 if sum(pair) % 2 == 0 else 3

    def a_first(pair):
        sibling_here(pair)
        at = ya_rows(pair)
        theirs = from_sib[pair[0] * 4 + pair[1], :SUM_A, :]
        contrib[at, :] = (contrib[at, :].astype(F32) + theirs.astype(F32)).astype(BF16)
        start(ya_far(pair, far_step(pair)))

    def a_second(pair):
        step = far_step(pair)
        ya_far(pair, step).wait_recv()
        at = ya_rows(pair)
        passed = ya_pass[pair[0] * 4 + pair[1]].astype(F32)
        contrib[at, me.lanes(step)] = (contrib[at, me.lanes(step)].astype(F32) + passed).astype(BF16)
        start(ya_near(pair, step))

    def a_give(pair):
        n = pair[0] * 4 + pair[1]
        return remote(
            a_sum.at[n], a_ring.at[n - 1], ar_send, ar_recv.at[0], me.pair_peer(pair)
        )

    def a_third(pair):
        n = pair[0] * 4 + pair[1]
        value = contrib[ya_rows(pair), own_lanes].astype(F32)
        all_here(ya_ring.at[n], yr_recv.at[n])
        for slot in range(2):
            value = value + ya_ring[n, slot].astype(F32)
        a_sum[n] = value.astype(BF16)
        if n:
            start(a_give(pair))

    def b_own(half, j, k):
        return contrib.at[
            rows_of(me.block(half, j, k, me.c), SUM_A + half * (SUM_B // 2), SUM_B // 2), :
        ]

    def b_touch(half, j, k):
        pair = pair_of(half, j, k)
        sibling_here(pair)
        theirs = from_sib[
            pair[0] * 4 + pair[1], pl.ds(SUM_A + half * (SUM_B // 2), SUM_B // 2), :
        ]
        return b_own(half, j, k)[...].astype(F32) + theirs.astype(F32)

    def b_final(half, value):
        at = pl.ds(half * (SUM_B // 2), SUM_B // 2)
        plane_sum[at, :] = value
        plane_sum_b[at, :] = value.astype(BF16)

    b_back = scatter_plane(
        me, b_own, b_touch, b_final, start, all_here, (b_pass, b_ring, b_line),
        (sum_send, bp_recv, br_recv, bl_recv),
    )
    order = [(2, 2), (2, 1), (1, 2), (2, 3), (3, 2), (2, 0), (0, 2), (1, 1)]
    order += [(3, 0), (0, 3), (1, 3), (3, 1), (1, 0), (0, 1), (3, 3), (0, 0)]
    for n, pair in enumerate(order):
        compute(pair)
        if n in (2, 5, 7, 9):
            next(b_back)
        if n >= 3:
            a_first(order[n - 3])
    for n in range(13, 16):
        a_first(order[n])
    for n, pair in enumerate(order):
        start(ya_near(pair, 4 - far_step(pair)))
        if n in (3, 7, 11, 15):
            next(b_back)
    for n, pair in enumerate(order):
        a_second(pair)
        if n in (1, 3, 7, 11):
            next(b_back)
    for n, pair in enumerate(order):
        a_third(pair)
        if n in (3, 7, 11):
            next(b_back)
    next(b_back)

    def b_tp_sum(step):
        return remote(
            plane_sum_b.at[:, me.lanes(step)], tp_r.at[step - 1],
            sum_send, tp_recv.at[0], me.tp_peer(step),
        )

    for step in (2, 1, 3):
        start(b_tp_sum(step))
    moe = a_sum[0].astype(F32)
    all_here(a_ring, ar_recv.at[0])
    for pair in order[:-1]:
        moe = moe + a_ring[pair[0] * 4 + pair[1] - 1].astype(F32)
    out[:SUM_A, :] = (hid[:SUM_A, :] + moe).astype(BF16)
    moe = plane_sum[:, own_lanes]
    all_here(tp_r, tp_recv.at[0])
    for step in (1, 3, 2):
        moe = moe + tp_r[step - 1].astype(F32)
    out[SUM_A:, :] = (hid[SUM_A:, :] + moe).astype(BF16)

    for group in sends:
        sized = {id(rs_send): part_r, id(ga_send): a_ring, id(ar_send): a_ring}.get(id(group))
        if sized is None:
            sized = hid_t.at[pl.ds(0, group.total // (2 * ROWS))]
        assert group.total == 2 * math.prod(sized.shape), group.total
        remote(sized, sized, group, rs_recv.at[0], me.sibling()).copy.wait_send()


def local(
    queries, latent_cache, lengths, uv_weight, out_weight, residual, norm_gain,
    gate_weight, up_weight, down_weight, routes, route_weights,
):
    anywhere = pl.BlockSpec(memory_space=pl.ANY)
    vmem = pl.BlockSpec(memory_space=pltpu.VMEM)
    smem = pl.BlockSpec(memory_space=pltpu.SMEM)
    dma = pltpu.SemaphoreType.DMA
    scratch = [
        pltpu.VMEM((D // 128, 128), F32),
        pltpu.VMEM(routes.shape[::-1], jnp.int32),
        pltpu.VMEM(routes.shape[::-1], F32),
        pltpu.VMEM((OWN_ROWS, KEY, HEADS), BF16),
        pltpu.VMEM((OWN_ROWS, KEY, CTX), BF16),
        pltpu.VMEM((OWN_HEADS, LAT, VHEAD), BF16),
        pltpu.VMEM((COLS, INNER), BF16),
        pltpu.VMEM((COLS, TP_ROWS), BF16),
        pltpu.VMEM((UNITS, D), BF16),
        pltpu.VMEM((2 * UNITS, D), BF16),
        pltpu.VMEM((D, UNITS), BF16),
        pltpu.VMEM((OWN_ROWS, HEADS, LAT), BF16),
        pltpu.VMEM((DP_ROWS, OWN_HEADS, LAT), BF16),
        pltpu.VMEM((LAT // 128, DP_ROWS * HALF_HEADS, 128), F32),
        pltpu.VMEM((ROWS, INNER), BF16),
        pltpu.VMEM((COLS, ROWS), F32),
        pltpu.VMEM((4, COLS, TP_ROWS), BF16),
        pltpu.VMEM((3, COLS, TP_ROWS), BF16),
        pltpu.VMEM((COLS, TP_ROWS), F32),
        pltpu.VMEM((D, ROWS), BF16),
        pltpu.VMEM((2 * UNITS, ROWS), F32),
        pltpu.VMEM((UNITS, ROWS), BF16),
        pltpu.VMEM((D, ROWS), BF16),
        pltpu.VMEM((16, COLS, ROWS), BF16),
        pltpu.VMEM((SUM_B, ROWS), F32),
        pltpu.VMEM((SUM_B, ROWS), BF16),
        pltpu.VMEM((3, SUM_B, TP_ROWS), BF16),
        pltpu.VMEM((1, ROWS), F32),
        pltpu.VMEM((2, 4, SUM_B // 2, ROWS), BF16),
        pltpu.VMEM((2, 8, SUM_B // 2, ROWS), BF16),
        pltpu.VMEM((2, 3, SUM_B // 2, ROWS), BF16),
        pltpu.VMEM((15, SUM_A, TP_ROWS), BF16),
        pltpu.VMEM((16, SUM_A, TP_ROWS), BF16),
        pltpu.VMEM((16, SUM_A, TP_ROWS), BF16),
        pltpu.VMEM((16, 2, SUM_A, TP_ROWS), BF16),
        dma((14,)), dma((6,)),
        dma((2,)), dma((2, 16)), dma((2,)),
        dma((1,)), dma((1,)),
        dma((16,)), dma((16, 2)), dma((2, 16)), dma((1,)),
        dma((16,)), dma((16,)), dma((16,)), dma((1,)),
        dma((2, 4)), dma((2, 4)), dma((2,)), dma((1,)),
    ]
    return pl.pallas_call(
        kernel,
        out_shape=jax.ShapeDtypeStruct((COLS, TP_ROWS), BF16),
        in_specs=[smem] + [anywhere] * 11,
        out_specs=vmem,
        scratch_shapes=scratch,
        compiler_params=pltpu.CompilerParams(
            collective_id=0, has_side_effects=True, vmem_limit_bytes=62 * 1024 * 1024
        ),
        name="decode_step",
    )(
        lengths, jnp.swapaxes(queries, 1, 2), jnp.swapaxes(latent_cache, 1, 2), uv_weight,
        out_weight.T, residual.T, norm_gain.reshape(D // 128, 128),
        gate_weight[0], up_weight[0], down_weight[0], routes.T, route_weights.T,
    ).T


def solution(mesh):
    placed = (
        P(("dp", "tp"), None, None),
        P(("dp", "tp"), None, None),
        P(("dp", "tp")),
        P("tp", None, None),
        P("tp", "dp"),
        P(None, "dp"),
        P(),
        P("dp", None, "tp"),
        P("dp", None, "tp"),
        P("dp", "tp", None),
        P(),
        P(),
    )
    return jax.shard_map(
        local, mesh=mesh, in_specs=placed, out_specs=P("tp", "dp"), check_vma=False
    )
```

```python
import math

import jax
import jax.numpy as jnp
from jax import lax
from jax.experimental import pallas as pl
from jax.experimental.pallas import tpu as pltpu
from jax.sharding import PartitionSpec as P

F32 = jnp.float32
BF16 = jnp.bfloat16
MESH = pl.DeviceIdType.MESH

LAT = 512
KEY = 576
CTX = 1024
HEADS = 128
OWN_HEADS = 32
HALF_HEADS = 16
VHEAD = 128
ROWS = 512
OWN_ROWS = 4
DP_ROWS = 16
TP_ROWS = 128
D = 7168
COLS = 224
PART_A = 96
PART_B = 128
INNER = 4096
UNITS = 256
CHIP = 448
DP = 32

score_scale = 192.0 ** (-0.5)
epsilon = 1e-06

SUM_A = 96
SUM_B = 128
PASSED = 12
SUM_PASSED = 12


def tn_dot(a, b):
    return lax.dot_general(a, b, (((0,), (0,)), ((), ())), preferred_element_type=F32)


def nt_dot(a, b):
    return lax.dot_general(a, b, (((1,), (1,)), ((), ())), preferred_element_type=F32)


class Place:
    def __init__(self):
        dp = lax.axis_index("dp")
        self.y = lax.axis_index("tp")
        self.d = dp
        self.c = lax.rem(dp, 2)
        self.x = lax.rem(dp // 2, 4)
        self.z = dp // 8

    def device(self, z=None, x=None, c=None, y=None):
        z = self.z if z is None else z
        x = self.x if x is None else x
        c = self.c if c is None else c
        y = self.y if y is None else y
        return ((z * 4 + x) * 2 + c, y)

    def sibling(self):
        return self.device(c=1 - self.c)

    def tp_peer(self, step):
        return self.device(y=lax.rem(self.y + step, 4))

    def first(self, half):
        return self.x if half == 0 else self.z

    def second(self, half):
        return self.z if half == 0 else self.x

    def first_peer(self, half, step):
        if half == 0:
            return self.device(x=lax.rem(self.x + step, 4))
        return self.device(z=lax.rem(self.z + step, 4))

    def second_peer(self, half, step):
        return self.first_peer(1 - half, step)

    def pair_peer(self, pair):
        return (self.at(*pair, self.c), self.y)

    def lanes(self, step):
        at = lax.rem(self.y + step, 4) * TP_ROWS
        return pl.ds(pl.multiple_of(at, TP_ROWS), TP_ROWS)

    def at(self, dz, dx, c):
        return (lax.rem(self.z + dz, 4) * 4 + lax.rem(self.x + dx, 4)) * 2 + c

    def block(self, half, j, k, c):
        a = lax.rem(self.first(half) + j, 4)
        b = lax.rem(self.second(half) + k, 4)
        z, x = (b, a) if half == 0 else (a, b)
        return (z * 4 + x) * 2 + c


class Sends:
    def __init__(self, sems, group):
        self.sem, self.total, self.at = sems.at[group], 0, self

    def __getitem__(self, index):
        return self


class Copy:
    def __init__(self, src, dst, send, recv, device):
        self.sends, self.bytes = send, 2 * math.prod(src.shape)
        self.copy = pltpu.make_async_remote_copy(
            src_ref=src, dst_ref=dst, send_sem=send.sem, recv_sem=recv,
            device_id=device, device_id_type=MESH,
        )

    def start(self):
        self.sends.total += self.bytes
        self.copy.start()

    def wait_recv(self):
        self.copy.wait_recv()


def remote(src, dst, send, recv, device):
    return Copy(src, dst, send, recv, device)


def rows_of(dp, offset, count):
    return pl.ds(pl.multiple_of(dp * COLS + offset, 16), count)


def gather_plane(me, blk, start, sems, landed):
    send_sem, recv_sem = sems

    def ref_of(half, j, k):
        return blk(half, me.block(half, j, k, me.c))

    def send(half, j, k, device, rj, rk):
        ref = ref_of(half, j, k)
        start(remote(
            ref, ref, send_sem, recv_sem.at[half, rj * 4 + rk], device
        ))

    def arrived(half, j, k):
        ref = ref_of(half, j, k)
        remote(
            ref, ref, send_sem, recv_sem.at[half, j * 4 + k], me.sibling()
        ).wait_recv()

    def second_axis(half, j):
        send(half, j, 0, me.second_peer(half, 1), j, 3)
        send(half, j, 0, me.second_peer(half, 3), j, 1)
        if j == 2:
            send(half, j, 0, me.second_peer(half, 2), j, 2)

    for half in range(2):
        for step in (1, 3, 2):
            send(half, 0, 0, me.first_peer(half, step), 4 - step, 0)
        second_axis(half, 0)
        landed(half, 0, 0)
        yield
    for j in (1, 3):
        for half in range(2):
            arrived(half, j, 0)
            second_axis(half, j)
    for j in (1, 3):
        for half in range(2):
            landed(half, j, 0)
    yield
    for half in range(2):
        arrived(half, 2, 0)
        second_axis(half, 2)
    for half in range(2):
        landed(half, 2, 0)
    yield
    for j in (0, 1, 3, 2):
        for half in range(2):
            arrived(half, j, 3)
            if j == 0:
                send(half, j, 3, me.second_peer(half, 1), j, 2)
            arrived(half, j, 1)
            if j == 1:
                send(half, j, 1, me.second_peer(half, 3), j, 2)
            if j == 3:
                send(half, j, 3 - 2 * me.c, me.second_peer(half, 1 + 2 * me.c), j, 2)
        for half in range(2):
            landed(half, j, 3)
            landed(half, j, 1)
        yield
    for j in (0, 1, 3, 2):
        for half in range(2):
            arrived(half, j, 2)
            landed(half, j, 2)
        yield


def scatter_plane(me, own, touch, finish, start, all_here, bufs, sems):
    pass_r, ring_r, line_r = bufs
    sends, pass_recv, ring_recv, line_recv = sems

    def far(half, j):
        return remote(
            own(half, j, 2), pass_r.at[half, j - 1], sends, pass_recv.at[half, j - 1],
            me.second_peer(half, 1 if j == 2 else 3),
        )

    def near(half, j, k):
        slot = j * 3 + k - 1
        return remote(
            own(half, j, k), ring_r.at[half, slot], sends, ring_recv.at[half, j],
            me.second_peer(half, k),
        )

    def line(half, j):
        return remote(
            own(half, j, 0), line_r.at[half, j - 1], sends, line_recv.at[half],
            me.first_peer(half, j),
        )

    def give(j, k):
        for half in range(2):
            own(half, j, k)[...] = touch(half, j, k).astype(BF16)
            start(near(half, j, k))

    def give_passed(j, k):
        for half in range(2):
            value = touch(half, j, k)
            far(half, j).wait_recv()
            value = value + pass_r[half, j - 1].astype(F32)
            own(half, j, k)[...] = value.astype(BF16)
            start(near(half, j, k))

    def gathered(half, j):
        value = touch(half, j, 0)
        steps = (1, 3) if j in (1, 2) else (1, 3, 2)
        all_here(ring_r.at[half, pl.ds(0, len(steps))], ring_recv.at[half, j])
        for k in steps:
            value = value + ring_r[half, j * 3 + k - 1].astype(F32)
        return value

    for j in (2, 1):
        for half in range(2):
            own(half, j, 2)[...] = touch(half, j, 2).astype(BF16)
            start(far(half, j))
        yield
    give(2, 3)
    give(1, 1)
    yield
    give(3, 2)
    give(3, 1)
    give(3, 3)
    yield
    give_passed(2, 1)
    give_passed(1, 3)
    yield
    give(0, 2)
    give(0, 1)
    give(0, 3)
    yield
    for j in (2, 1, 3):
        for half in range(2):
            own(half, j, 0)[...] = gathered(half, j).astype(BF16)
            start(line(half, j))
        yield
    for half in range(2):
        value = gathered(half, 0)
        all_here(line_r.at[half], line_recv.at[half])
        for j in (1, 3, 2):
            value = value + line_r[half, j - 1].astype(F32)
        finish(half, value)
    yield


def kernel(
    lengths, q_hbm, cache_hbm, uv_hbm, out_w_hbm, residual_hbm, gain_hbm, gate_hbm, up_hbm, down_hbm,
    routes_hbm, route_weights_hbm, out,
    gain, routes, route_weights, qv, cv, uv, out_w, res, down_w, gate_up_t, down_t,
    ctx, by_head, by_head_f, heads_all, part, part_b, part_r, hid, hid_t, gate_up,
    gain_rows, squares, act, contrib, from_sib, plane_sum, plane_sum_b, tp_r, weight_row,
    b_pass, b_ring, b_line, a_ring, a_sum, ya_pass, ya_ring,
    load_sem, send_sems, a2a_recv, ag_recv, ag_sib_recv, rs_recv, hy_recv,
    ga_recv, gy_recv, gb_recv, gather_sib_recv,
    sib_recv, yp_recv, yr_recv, ar_recv, bp_recv, br_recv, bl_recv, tp_recv,
):
    me = Place()
    y, d = me.y, me.d
    own_lanes = pl.ds(pl.multiple_of(y * TP_ROWS, TP_ROWS), TP_ROWS)

    loads = {}
    sends = [Sends(send_sems, group) for group in range(6)]
    early_send, rs_send, gather_send, ga_send, sum_send, ar_send = sends

    def load(name, src, dst, index):
        copy = pltpu.make_async_copy(src, dst, load_sem.at[index])
        copy.start()
        loads[name] = copy

    def ready(name):
        loads.pop(name).wait()

    def start(copy):
        copy.start()

    def all_here(ref, recv):
        remote(ref, ref, early_send, recv, me.sibling()).wait_recv()

    load("q", q_hbm, qv, 0)
    for i in range(OWN_ROWS):
        load(("cache", i), cache_hbm.at[i], cv.at[i], 1 + i)

    barrier = pltpu.get_barrier_semaphore()
    peers = [me.sibling()]
    for step in (1, 2, 3):
        peers += [me.first_peer(0, step), me.first_peer(1, step), me.tp_peer(step)]
    for peer in peers:
        pl.semaphore_signal(barrier, inc=1, device_id=peer, device_id_type=MESH)

    def heads_out(row, half, step):
        to = lax.rem(y + step, 4) * OWN_HEADS + half * HALF_HEADS
        return remote(
            ctx.at[row, pl.ds(pl.multiple_of(to, HALF_HEADS), HALF_HEADS)],
            by_head.at[y * OWN_ROWS + row, pl.ds(half * HALF_HEADS, HALF_HEADS)],
            early_send, a2a_recv.at[half], me.tp_peer(step),
        )

    ready("q")
    for i in range(OWN_ROWS):
        ready(("cache", i))
        if i == 1:
            load("uv", uv_hbm, uv, 5)
            load("out_w", out_w_hbm, out_w, 6)
            load("res", residual_hbm.at[:, own_lanes], res, 7)
        if i == 2:
            load("gate", gate_hbm, contrib.at[:, pl.ds(0, UNITS)], 8)
            load("up", up_hbm, contrib.at[:, pl.ds(UNITS, UNITS)], 9)
            load("down", down_hbm, down_w, 10)
            load("gain", gain_hbm, gain, 11)
            load("routes", routes_hbm, routes, 12)
            load("route_weights", route_weights_hbm, route_weights, 13)
        scores = tn_dot(qv[i], cv[i]) * score_scale
        usable = lax.broadcasted_iota(jnp.int32, scores.shape, 1) < lengths[i]
        peak = jnp.max(jnp.where(usable, scores, -1e30), axis=1, keepdims=True)
        soft = jnp.where(usable, jnp.exp(scores - peak), 0.0)
        total = jnp.sum(soft, axis=1, keepdims=True)
        summed = nt_dot(soft.astype(BF16), cv[i, :LAT, :])
        ctx[i] = (summed / total).astype(BF16)
        by_head[y * OWN_ROWS + i] = ctx[
            i, pl.ds(pl.multiple_of(y * OWN_HEADS, OWN_HEADS), OWN_HEADS), :
        ]
        if i == 2:
            pl.semaphore_wait(barrier, len(peers))
        if i >= 2:
            for row in (0, 1, 2) if i == 2 else (3,):
                for step in (2, 1, 3):
                    start(heads_out(row, 0, step))
    for i in range(OWN_ROWS):
        for step in (2, 1, 3):
            start(heads_out(i, 1, step))

    ready("uv")
    own_rows = pl.ds(pl.multiple_of(d * DP_ROWS, DP_ROWS), DP_ROWS)

    def project(half):
        others = by_head.at[pl.ds(0, DP_ROWS - OWN_ROWS), pl.ds(0, HALF_HEADS)]
        all_here(others, a2a_recv.at[half])
        heads = pl.ds(half * HALF_HEADS, HALF_HEADS)
        for part_of in range(LAT // 128):
            piece = by_head[:, heads, pl.ds(part_of * 128, 128)]
            by_head_f[part_of] = piece.astype(F32).reshape(DP_ROWS * HALF_HEADS, 128)
        for h in range(HALF_HEADS):
            picked = jnp.concatenate(
                [
                    by_head_f[part_of, pl.ds(h, DP_ROWS, stride=HALF_HEADS), :]
                    for part_of in range(LAT // 128)
                ],
                axis=1,
            ).astype(BF16)
            at = half * HALF_HEADS + h
            heads_all[own_rows, pl.ds(at * VHEAD, VHEAD)] = jnp.dot(
                picked, uv[at], preferred_element_type=F32
            ).astype(BF16)

    project(0)
    def head_block(half, dp):
        return heads_all.at[
            pl.ds(pl.multiple_of(dp * DP_ROWS, DP_ROWS), DP_ROWS), pl.ds(half * (INNER // 2), INNER // 2)
        ]

    def head_sibling(half, j, k, c):
        ref = head_block(half, me.block(half, j, k, c))
        return remote(
            ref, ref, early_send, ag_sib_recv.at[half], me.sibling()
        )

    def spread_gain():
        turned_gain = pltpu.roll(gain[...], 64, axis=1)
        low = lax.broadcasted_iota(jnp.int32, (1, 128), 1) < 64
        for chip in range(D // CHIP):
            for q in range(4):
                at, odd = divmod(chip * CHIP + q * 128, 128)
                row = gain[at : at + 1, :]
                if odd:
                    row = turned_gain[at : at + 1, :]
                    if q < 3:
                        row = jnp.where(low, row, turned_gain[at + 1 : at + 2, :])
                gain_rows[q, chip : chip + 1, :] = row

    def turn_chip(chip, carry):
        for q in range(4):
            width = 128 if q < 3 else 64
            rows = contrib[pl.ds(pl.multiple_of(chip * CHIP + q * 128, 64), width), :]
            turned = rows.astype(F32).T * gain_rows[q, pl.ds(chip, 1), :][:, :width]
            gate_up_t[chip, :, q * 128 : q * 128 + width] = turned.astype(BF16)
        return carry

    def turn_step(i, carry):
        at = pl.ds(pl.multiple_of(i * 128, 128), 128)
        down_t[at, :] = down_w[:, at].astype(F32).T.astype(BF16)
        return carry

    turned_to = 0
    heads_plane = gather_plane(
        me, head_block, start, (early_send, ag_recv), lambda *at: start(head_sibling(*at, me.c))
    )
    next(heads_plane)
    project(1)
    for step in heads_plane:
        if turned_to == 0:
            for name in ("gate", "up", "down", "gain"):
                ready(name)
            spread_gain()
        if turned_to < D // 128:
            lax.fori_loop(turned_to // 7 * 2, turned_to // 7 * 2 + 2, turn_chip, 0)
            lax.fori_loop(turned_to, turned_to + 7, turn_step, 0)
            turned_to += 7

    ready("out_w")
    part[...] = jnp.zeros_like(part)

    def out_step(k, carry):
        at = pl.ds(pl.multiple_of(k * 512, 512), 512)
        part[...] += nt_dot(out_w[:, at], heads_all[:, at])
        return carry

    for half in range(2):
        all_here(heads_all.at[pl.ds(0, ROWS // 2), pl.ds(0, INNER // 2)], ag_sib_recv.at[half])
        lax.fori_loop(half * 4, half * 4 + 4, out_step, 0)
    for block in range(4):
        part_b[block] = part[:, block * TP_ROWS : (block + 1) * TP_ROWS].astype(BF16)
    for step in (2, 1, 3):
        start(remote(
            part_b.at[lax.rem(y + step, 4)], part_r.at[step - 1],
            rs_send, rs_recv.at[0], me.tp_peer(step),
        ))

    ready("routes")
    ready("route_weights")
    weight_row[...] = jnp.sum(
        jnp.where(routes[...] == d, route_weights[...], 0.0), axis=0, keepdims=True
    )

    ready("res")
    total = res[...].astype(F32) + part[:, own_lanes]
    all_here(part_r, rs_recv.at[0])
    for step in (1, 2, 3):
        total = total + part_r[step - 1].astype(F32)
    hidden = total.astype(BF16)
    hid[...] = hidden.astype(F32)
    own_cols = pl.ds(pl.multiple_of(d * COLS, 16), COLS)
    hid_t[own_cols, own_lanes] = hidden

    pairs = [(dz, dx) for dz in range(4) for dx in range(4)]

    def b_block(half, dp):
        return hid_t.at[rows_of(dp, PART_A + half * (PART_B // 2), PART_B // 2), :]

    def pair_of(half, j, k):
        return (k, j) if half == 0 else (j, k)

    nearest = sorted(pairs, key=lambda pair: (2 in pair, sum((0, 1, 2, 1)[step] for step in pair)))
    passed_on = nearest[:PASSED]

    def a_tp(pair, slot, lanes, step):
        ref = hid_t.at[rows_of(me.at(*pair, me.c), 0, PART_A), lanes]
        n = pair[0] * 4 + pair[1]
        alone = pair in passed_on and slot == sum(pair) % 2
        return remote(
            ref, ref, gather_send, gy_recv.at[n, 0 if alone else 1], me.tp_peer(step)
        )

    def a_sibling(pair, c):
        ref = hid_t.at[rows_of(me.at(*pair, c), 0, PART_A), :]
        late = 1 if 2 in pair else 0
        return remote(ref, ref, gather_send, gather_sib_recv.at[late], me.sibling())

    def a_plane(pair):
        ref = hid_t.at[rows_of(d, 0, PART_A), own_lanes]
        opposite = (4 - pair[0]) % 4 * 4 + (4 - pair[1]) % 4
        return remote(ref, ref, ga_send, ga_recv.at[opposite], me.pair_peer(pair))

    a_landed = []

    def a_here(pair):
        a_landed.append(pair)
        start(a_tp(pair, 0, me.lanes(0), 1))
        start(a_tp(pair, 1, me.lanes(0), 3))
        if len(a_landed) > PASSED:
            start(a_tp(pair, 2, me.lanes(0), 2))

    a_passed, a_done = [0], [0]

    def a_pass_on(count):
        for pair in a_landed[a_passed[0] : min(a_passed[0] + count, PASSED)]:
            if sum(pair) % 2 == 0:
                a_tp(pair, 0, me.lanes(3), 1).wait_recv()
                start(a_tp(pair, 2, me.lanes(3), 1))
            else:
                a_tp(pair, 1, me.lanes(1), 3).wait_recv()
                start(a_tp(pair, 2, me.lanes(1), 3))
        a_passed[0] += count

    def a_finish(count):
        for n in range(a_done[0], min(a_done[0] + count, 16)):
            pair = a_landed[n]
            copies = 2 if pair in passed_on else 3
            all_here(ya_pass.at[pl.ds(0, copies)], gy_recv.at[pair[0] * 4 + pair[1], 1])
            start(a_sibling(pair, me.c))
        a_done[0] += count

    def b_sibling(half, j, k, c):
        ref = b_block(half, me.block(half, j, k, c))
        late = 1 if 2 in (j, k) else 0
        return remote(ref, ref, gather_send, gather_sib_recv.at[late], me.sibling())

    def b_tp(lanes, step):
        ref = hid_t.at[rows_of(d, PART_A, PART_B), lanes]
        return remote(ref, ref, gather_send, hy_recv.at[0], me.tp_peer(step))

    b_plane = gather_plane(
        me, b_block, start, (gather_send, gb_recv), lambda *at: start(b_sibling(*at, me.c))
    )
    for step in (1, 3, 2):
        start(b_tp(me.lanes(0), step))
    for pair in nearest[1:]:
        start(a_plane(pair))
    a_here((0, 0))
    for pair in nearest[1:5]:
        opposite = ((4 - pair[0]) % 4, (4 - pair[1]) % 4)
        a_plane(opposite).wait_recv()
        a_here(pair)
    all_here(tp_r, hy_recv.at[0])
    next(b_plane)
    next(b_plane)
    a_pass_on(1)
    for pair in nearest[5:]:
        opposite = ((4 - pair[0]) % 4, (4 - pair[1]) % 4)
        a_plane(opposite).wait_recv()
        a_here(pair)
    a_pass_on(3)
    next(b_plane)
    next(b_plane)
    a_pass_on(4)
    next(b_plane)
    a_pass_on(2)
    next(b_plane)
    a_pass_on(2)
    next(b_plane)
    next(b_plane)

    gate_up[...] = jnp.zeros_like(gate_up)
    squares[...] = jnp.zeros_like(squares)

    def expert(pair):
        chip = me.at(*pair, 0) // 2
        rows = hid_t[pl.ds(pl.multiple_of(chip * CHIP, 64), CHIP), :]
        gate_up[...] += jnp.dot(gate_up_t[chip], rows, preferred_element_type=F32)
        wide = rows.astype(F32)
        squares[...] += jnp.sum((wide * wide).reshape(CHIP // 8, 8, ROWS), axis=0)

    early = nearest[:9]
    a_finish(9)
    next(b_plane)
    a_finish(1)
    next(b_plane)
    all_here(hid_t.at[pl.ds(0, 9 * COLS)], gather_sib_recv.at[0])
    for n in range(2):
        for pair in early[3 * n : 3 * n + 3]:
            expert(pair)
        a_finish(2)
        next(b_plane)
    a_finish(16)
    for pair in early[6:]:
        expert(pair)
    all_here(hid_t.at[pl.ds(0, 7 * COLS)], gather_sib_recv.at[1])
    for pair in nearest[9:]:
        expert(pair)

    inverse_rms = lax.rsqrt(jnp.sum(squares[...], axis=0, keepdims=True) * (1.0 / D) + epsilon)
    gate_proj = gate_up[:UNITS, :] * inverse_rms
    up_proj = gate_up[UNITS:, :] * inverse_rms
    silu = gate_proj / (1.0 + jnp.exp(-gate_proj))
    act[...] = (silu * up_proj * weight_row[...]).astype(BF16)

    def from_core(pair, c):
        n = pair[0] * 4 + pair[1]
        return remote(
            contrib.at[rows_of(me.at(*pair, c), 0, COLS), :], from_sib.at[n],
            sum_send, sib_recv.at[n], me.sibling(),
        )

    def compute(pair):
        at = pl.ds(pl.multiple_of(me.at(*pair, 0) * COLS, 16), 2 * COLS)
        contrib[at, :] = jnp.dot(down_t[at, :], act[...], preferred_element_type=F32).astype(BF16)
        start(from_core(pair, 1 - me.c))

    sib_here = set()

    def sibling_here(pair):
        if pair not in sib_here:
            sib_here.add(pair)
            from_core(pair, me.c).wait_recv()

    def ya_rows(pair):
        return rows_of(me.at(*pair, me.c), 0, SUM_A)

    def ya_far(pair, step):
        n = pair[0] * 4 + pair[1]
        return remote(
            contrib.at[ya_rows(pair), me.lanes(2)], ya_pass.at[n],
            sum_send, yp_recv.at[n], me.tp_peer(step),
        )

    def ya_near(pair, step):
        n = pair[0] * 4 + pair[1]
        return remote(
            contrib.at[ya_rows(pair), me.lanes(step)], ya_ring.at[n, step - 1],
            sum_send, yr_recv.at[n], me.tp_peer(step),
        )

    passed_pairs = []

    def a_first(pair):
        sibling_here(pair)
        at = ya_rows(pair)
        theirs = from_sib[pair[0] * 4 + pair[1], :SUM_A, :]
        contrib[at, :] = (contrib[at, :].astype(F32) + theirs.astype(F32)).astype(BF16)
        if len(passed_pairs) < SUM_PASSED:
            passed_pairs.append(pair)
            far_step = 1 if sum(pair) % 2 == 0 else 3
            start(ya_far(pair, far_step))
            start(ya_near(pair, 4 - far_step))
        else:
            for step in (1, 3, 2):
                start(ya_near(pair, step))

    def a_second(pair):
        step = 1 if sum(pair) % 2 == 0 else 3
        ya_far(pair, step).wait_recv()
        at = ya_rows(pair)
        passed = ya_pass[pair[0] * 4 + pair[1]].astype(F32)
        contrib[at, me.lanes(step)] = (contrib[at, me.lanes(step)].astype(F32) + passed).astype(BF16)
        start(ya_near(pair, step))

    def a_give(pair):
        n = pair[0] * 4 + pair[1]
        return remote(
            a_sum.at[n], a_ring.at[n - 1], ar_send, ar_recv.at[0], me.pair_peer(pair)
        )

    def a_third(pair):
        n = pair[0] * 4 + pair[1]
        value = contrib[ya_rows(pair), own_lanes].astype(F32)
        steps = (1, 3) if pair in passed_pairs else (1, 3, 2)
        all_here(ya_ring.at[n, pl.ds(0, len(steps))], yr_recv.at[n])
        for step in steps:
            value = value + ya_ring[n, step - 1].astype(F32)
        a_sum[n] = value.astype(BF16)
        if n:
            start(a_give(pair))

    def b_own(half, j, k):
        return contrib.at[
            rows_of(me.block(half, j, k, me.c), SUM_A + half * (SUM_B // 2), SUM_B // 2), :
        ]

    def b_touch(half, j, k):
        pair = pair_of(half, j, k)
        sibling_here(pair)
        theirs = from_sib[
            pair[0] * 4 + pair[1], pl.ds(SUM_A + half * (SUM_B // 2), SUM_B // 2), :
        ]
        return b_own(half, j, k)[...].astype(F32) + theirs.astype(F32)

    def b_final(half, value):
        at = pl.ds(half * (SUM_B // 2), SUM_B // 2)
        plane_sum[at, :] = value
        plane_sum_b[at, :] = value.astype(BF16)

    b_back = scatter_plane(
        me, b_own, b_touch, b_final, start, all_here, (b_pass, b_ring, b_line),
        (sum_send, bp_recv, br_recv, bl_recv),
    )
    order = [(2, 2), (2, 1), (1, 2), (3, 2), (2, 3), (1, 1), (1, 3), (3, 1), (3, 3)]
    order += [(2, 0), (0, 2), (1, 0), (0, 1), (3, 0), (0, 3), (0, 0)]
    for n, pair in enumerate(order):
        compute(pair)
        if n in (3, 6, 9, 12):
            next(b_back)
        if n >= 3:
            a_first(order[n - 3])
        if n >= 14:
            a_second(order[n - 14])
    for n in range(13, 16):
        a_first(order[n])
        a_second(order[n - 11])
    next(b_back)
    next(b_back)
    for n in range(5, SUM_PASSED):
        a_second(order[n])
    for n, pair in enumerate(order):
        a_third(pair)
        if n in (3, 7, 11):
            next(b_back)
    next(b_back)

    def b_tp_sum(step):
        return remote(
            plane_sum_b.at[:, me.lanes(step)], tp_r.at[step - 1],
            sum_send, tp_recv.at[0], me.tp_peer(step),
        )

    for step in (2, 1, 3):
        start(b_tp_sum(step))
    moe = a_sum[0].astype(F32)
    all_here(a_ring, ar_recv.at[0])
    for pair in order[:-1]:
        moe = moe + a_ring[pair[0] * 4 + pair[1] - 1].astype(F32)
    out[:SUM_A, :] = (hid[:SUM_A, :] + moe).astype(BF16)
    moe = plane_sum[:, own_lanes]
    all_here(tp_r, tp_recv.at[0])
    for step in (1, 3, 2):
        moe = moe + tp_r[step - 1].astype(F32)
    out[SUM_A:, :] = (hid[SUM_A:, :] + moe).astype(BF16)

    for group in sends:
        sized = {id(rs_send): part_r, id(ga_send): a_ring, id(ar_send): a_ring}.get(id(group))
        if sized is None:
            sized = hid_t.at[pl.ds(0, group.total // (2 * ROWS))]
        assert group.total == 2 * math.prod(sized.shape), group.total
        remote(sized, sized, group, rs_recv.at[0], me.sibling()).copy.wait_send()


def local(
    queries, latent_cache, lengths, uv_weight, out_weight, residual, norm_gain,
    gate_weight, up_weight, down_weight, routes, route_weights,
):
    anywhere = pl.BlockSpec(memory_space=pl.ANY)
    vmem = pl.BlockSpec(memory_space=pltpu.VMEM)
    smem = pl.BlockSpec(memory_space=pltpu.SMEM)
    dma = pltpu.SemaphoreType.DMA
    scratch = [
        pltpu.VMEM((D // 128, 128), F32),
        pltpu.VMEM(routes.shape[::-1], jnp.int32),
        pltpu.VMEM(routes.shape[::-1], F32),
        pltpu.VMEM((OWN_ROWS, KEY, HEADS), BF16),
        pltpu.VMEM((OWN_ROWS, KEY, CTX), BF16),
        pltpu.VMEM((OWN_HEADS, LAT, VHEAD), BF16),
        pltpu.VMEM((COLS, INNER), BF16),
        pltpu.VMEM((COLS, TP_ROWS), BF16),
        pltpu.VMEM((UNITS, D), BF16),
        pltpu.VMEM((D // CHIP, 2 * UNITS, CHIP), BF16),
        pltpu.VMEM((D, UNITS), BF16),
        pltpu.VMEM((OWN_ROWS, HEADS, LAT), BF16),
        pltpu.VMEM((DP_ROWS, OWN_HEADS, LAT), BF16),
        pltpu.VMEM((LAT // 128, DP_ROWS * HALF_HEADS, 128), F32),
        pltpu.VMEM((ROWS, INNER), BF16),
        pltpu.VMEM((COLS, ROWS), F32),
        pltpu.VMEM((4, COLS, TP_ROWS), BF16),
        pltpu.VMEM((3, COLS, TP_ROWS), BF16),
        pltpu.VMEM((COLS, TP_ROWS), F32),
        pltpu.VMEM((D, ROWS), BF16),
        pltpu.VMEM((2 * UNITS, ROWS), F32),
        pltpu.VMEM((4, D // CHIP, 128), F32),
        pltpu.VMEM((8, ROWS), F32),
        pltpu.VMEM((UNITS, ROWS), BF16),
        pltpu.VMEM((D, ROWS), BF16),
        pltpu.VMEM((16, COLS, ROWS), BF16),
        pltpu.VMEM((SUM_B, ROWS), F32),
        pltpu.VMEM((SUM_B, ROWS), BF16),
        pltpu.VMEM((3, SUM_B, TP_ROWS), BF16),
        pltpu.VMEM((1, ROWS), F32),
        pltpu.VMEM((2, 2, SUM_B // 2, ROWS), BF16),
        pltpu.VMEM((2, 12, SUM_B // 2, ROWS), BF16),
        pltpu.VMEM((2, 3, SUM_B // 2, ROWS), BF16),
        pltpu.VMEM((15, SUM_A, TP_ROWS), BF16),
        pltpu.VMEM((16, SUM_A, TP_ROWS), BF16),
        pltpu.VMEM((16, SUM_A, TP_ROWS), BF16),
        pltpu.VMEM((16, 3, SUM_A, TP_ROWS), BF16),
        dma((14,)), dma((6,)),
        dma((2,)), dma((2, 16)), dma((2,)),
        dma((1,)), dma((1,)),
        dma((16,)), dma((16, 2)), dma((2, 16)), dma((2,)),
        dma((16,)), dma((16,)), dma((16,)), dma((1,)),
        dma((2, 2)), dma((2, 4)), dma((2,)), dma((1,)),
    ]
    return pl.pallas_call(
        kernel,
        out_shape=jax.ShapeDtypeStruct((COLS, TP_ROWS), BF16),
        in_specs=[smem] + [anywhere] * 11,
        out_specs=vmem,
        scratch_shapes=scratch,
        compiler_params=pltpu.CompilerParams(
            collective_id=0, has_side_effects=True, vmem_limit_bytes=62 * 1024 * 1024
        ),
        name="decode_step",
    )(
        lengths, jnp.swapaxes(queries, 1, 2), jnp.swapaxes(latent_cache, 1, 2), uv_weight,
        out_weight.T, residual.T, norm_gain.reshape(D // 128, 128),
        gate_weight[0], up_weight[0], down_weight[0], routes.T, route_weights.T,
    ).T


def solution(mesh):
    placed = (
        P(("dp", "tp"), None, None),
        P(("dp", "tp"), None, None),
        P(("dp", "tp")),
        P("tp", None, None),
        P("tp", "dp"),
        P(None, "dp"),
        P(),
        P("dp", None, "tp"),
        P("dp", None, "tp"),
        P("dp", "tp", None),
        P(),
        P(),
    )
    return jax.shard_map(
        local, mesh=mesh, in_specs=placed, out_specs=P("tp", "dp"), check_vma=False
    )
```

```python
import math

import jax
import jax.numpy as jnp
from jax import lax
from jax.experimental import pallas as pl
from jax.experimental.pallas import tpu as pltpu
from jax.sharding import PartitionSpec as P

F32 = jnp.float32
BF16 = jnp.bfloat16
MESH = pl.DeviceIdType.MESH

LAT = 512
KEY = 576
CTX = 1024
HEADS = 128
OWN_HEADS = 32
HALF_HEADS = 16
VHEAD = 128
ROWS = 512
OWN_ROWS = 4
DP_ROWS = 16
TP_ROWS = 128
D = 7168
COLS = 224
PART_A = 96
PART_B = 128
INNER = 4096
UNITS = 256
CHIP = 448
DP = 32

score_scale = 192.0 ** (-0.5)
epsilon = 1e-06

SUM_A = 96
SUM_B = 128
PASSED = 12
SUM_PASSED = 12


def tn_dot(a, b):
    return lax.dot_general(a, b, (((0,), (0,)), ((), ())), preferred_element_type=F32)


def nt_dot(a, b):
    return lax.dot_general(a, b, (((1,), (1,)), ((), ())), preferred_element_type=F32)


class Place:
    def __init__(self):
        dp = lax.axis_index("dp")
        self.y = lax.axis_index("tp")
        self.d = dp
        self.c = lax.rem(dp, 2)
        self.x = lax.rem(dp // 2, 4)
        self.z = dp // 8

    def device(self, z=None, x=None, c=None, y=None):
        z = self.z if z is None else z
        x = self.x if x is None else x
        c = self.c if c is None else c
        y = self.y if y is None else y
        return ((z * 4 + x) * 2 + c, y)

    def sibling(self):
        return self.device(c=1 - self.c)

    def tp_peer(self, step):
        return self.device(y=lax.rem(self.y + step, 4))

    def first(self, half):
        return self.x if half == 0 else self.z

    def second(self, half):
        return self.z if half == 0 else self.x

    def first_peer(self, half, step):
        if half == 0:
            return self.device(x=lax.rem(self.x + step, 4))
        return self.device(z=lax.rem(self.z + step, 4))

    def second_peer(self, half, step):
        return self.first_peer(1 - half, step)

    def pair_peer(self, pair):
        return (self.at(*pair, self.c), self.y)

    def lanes(self, step):
        at = lax.rem(self.y + step, 4) * TP_ROWS
        return pl.ds(pl.multiple_of(at, TP_ROWS), TP_ROWS)

    def at(self, dz, dx, c):
        return (lax.rem(self.z + dz, 4) * 4 + lax.rem(self.x + dx, 4)) * 2 + c

    def block(self, half, j, k, c):
        a = lax.rem(self.first(half) + j, 4)
        b = lax.rem(self.second(half) + k, 4)
        z, x = (b, a) if half == 0 else (a, b)
        return (z * 4 + x) * 2 + c


class Sends:
    def __init__(self, sems, group):
        self.sem, self.total, self.at = sems.at[group], 0, self

    def __getitem__(self, index):
        return self


class Copy:
    def __init__(self, src, dst, send, recv, device):
        self.sends, self.bytes = send, 2 * math.prod(src.shape)
        self.copy = pltpu.make_async_remote_copy(
            src_ref=src, dst_ref=dst, send_sem=send.sem, recv_sem=recv,
            device_id=device, device_id_type=MESH,
        )

    def start(self):
        self.sends.total += self.bytes
        self.copy.start()

    def wait_recv(self):
        self.copy.wait_recv()


def remote(src, dst, send, recv, device):
    return Copy(src, dst, send, recv, device)


def rows_of(dp, offset, count):
    return pl.ds(pl.multiple_of(dp * COLS + offset, 16), count)


def gather_plane(me, blk, start, sems, landed):
    send_sem, recv_sem = sems

    def ref_of(half, j, k):
        return blk(half, me.block(half, j, k, me.c))

    def send(half, j, k, device, rj, rk):
        ref = ref_of(half, j, k)
        start(remote(
            ref, ref, send_sem, recv_sem.at[half, rj * 4 + rk], device
        ))

    def arrived(half, j, k):
        ref = ref_of(half, j, k)
        remote(
            ref, ref, send_sem, recv_sem.at[half, j * 4 + k], me.sibling()
        ).wait_recv()

    def second_axis(half, j):
        send(half, j, 0, me.second_peer(half, 1), j, 3)
        send(half, j, 0, me.second_peer(half, 3), j, 1)
        if j == 2:
            send(half, j, 0, me.second_peer(half, 2), j, 2)

    for half in range(2):
        for step in (1, 3, 2):
            send(half, 0, 0, me.first_peer(half, step), 4 - step, 0)
        second_axis(half, 0)
        landed(half, 0, 0)
        yield
    for j in (1, 3):
        for half in range(2):
            arrived(half, j, 0)
            second_axis(half, j)
    for j in (1, 3):
        for half in range(2):
            landed(half, j, 0)
    yield
    for half in range(2):
        arrived(half, 2, 0)
        second_axis(half, 2)
    for half in range(2):
        landed(half, 2, 0)
    yield
    for j in (0, 1, 3, 2):
        for half in range(2):
            arrived(half, j, 3)
            if j == 0:
                send(half, j, 3, me.second_peer(half, 1), j, 2)
            arrived(half, j, 1)
            if j == 1:
                send(half, j, 1, me.second_peer(half, 3), j, 2)
            if j == 3:
                send(half, j, 3 - 2 * me.c, me.second_peer(half, 1 + 2 * me.c), j, 2)
        for half in range(2):
            landed(half, j, 3)
            landed(half, j, 1)
        yield
    for j in (0, 1, 3, 2):
        for half in range(2):
            arrived(half, j, 2)
            landed(half, j, 2)
        yield


def scatter_plane(me, own, touch, finish, start, all_here, bufs, sems):
    pass_r, ring_r, line_r = bufs
    sends, pass_recv, ring_recv, line_recv = sems

    def far(half, j):
        return remote(
            own(half, j, 2), pass_r.at[half, j - 1], sends, pass_recv.at[half, j - 1],
            me.second_peer(half, 1 if j == 2 else 3),
        )

    def near(half, j, k):
        slot = j * 3 + k - 1
        return remote(
            own(half, j, k), ring_r.at[half, slot], sends, ring_recv.at[half, j],
            me.second_peer(half, k),
        )

    def line(half, j):
        return remote(
            own(half, j, 0), line_r.at[half, j - 1], sends, line_recv.at[half],
            me.first_peer(half, j),
        )

    def give(j, k):
        for half in range(2):
            own(half, j, k)[...] = touch(half, j, k).astype(BF16)
            start(near(half, j, k))

    def give_passed(j, k):
        for half in range(2):
            value = touch(half, j, k)
            far(half, j).wait_recv()
            value = value + pass_r[half, j - 1].astype(F32)
            own(half, j, k)[...] = value.astype(BF16)
            start(near(half, j, k))

    def gathered(half, j):
        value = touch(half, j, 0)
        steps = (1, 3) if j in (1, 2) else (1, 3, 2)
        all_here(ring_r.at[half, pl.ds(0, len(steps))], ring_recv.at[half, j])
        for k in steps:
            value = value + ring_r[half, j * 3 + k - 1].astype(F32)
        return value

    for j in (2, 1):
        for half in range(2):
            own(half, j, 2)[...] = touch(half, j, 2).astype(BF16)
            start(far(half, j))
        yield
    give(2, 3)
    give(1, 1)
    yield
    give(3, 2)
    give(3, 1)
    give(3, 3)
    yield
    give_passed(2, 1)
    give_passed(1, 3)
    yield
    give(0, 2)
    give(0, 1)
    give(0, 3)
    yield
    for j in (2, 1, 3):
        for half in range(2):
            own(half, j, 0)[...] = gathered(half, j).astype(BF16)
            start(line(half, j))
        yield
    for half in range(2):
        value = gathered(half, 0)
        all_here(line_r.at[half], line_recv.at[half])
        for j in (1, 3, 2):
            value = value + line_r[half, j - 1].astype(F32)
        finish(half, value)
    yield


def kernel(
    lengths, q_hbm, cache_hbm, uv_hbm, out_w_hbm, residual_hbm, gain_hbm, gate_hbm, up_hbm, down_hbm,
    routes_hbm, route_weights_hbm, out,
    gain, routes, route_weights, qv, cv, uv, out_w, res, down_w, gate_up_t, down_t,
    ctx, by_head, by_head_f, heads_all, part, part_b, part_r, hid, hid_t, gate_up,
    gain_rows, squares, act, contrib, from_sib, plane_sum, plane_sum_b, tp_r, weight_row,
    b_pass, b_ring, b_line, a_ring, a_sum, ya_pass, ya_ring,
    load_sem, send_sems, a2a_recv, ag_recv, ag_sib_recv, rs_recv, hy_recv,
    ga_recv, gy_recv, gb_recv, gather_sib_recv,
    sib_recv, yp_recv, yr_recv, ar_recv, bp_recv, br_recv, bl_recv, tp_recv,
):
    me = Place()
    y, d = me.y, me.d
    own_lanes = pl.ds(pl.multiple_of(y * TP_ROWS, TP_ROWS), TP_ROWS)

    loads = {}
    sends = [Sends(send_sems, group) for group in range(6)]
    early_send, rs_send, gather_send, ga_send, sum_send, ar_send = sends

    def load(name, src, dst, index):
        copy = pltpu.make_async_copy(src, dst, load_sem.at[index])
        copy.start()
        loads[name] = copy

    def ready(name):
        loads.pop(name).wait()

    def start(copy):
        copy.start()

    def all_here(ref, recv):
        remote(ref, ref, early_send, recv, me.sibling()).wait_recv()

    load("q", q_hbm, qv, 0)
    for i in range(OWN_ROWS):
        load(("cache", i), cache_hbm.at[i], cv.at[i], 1 + i)

    barrier = pltpu.get_barrier_semaphore()
    peers = [me.sibling()]
    for step in (1, 2, 3):
        peers += [me.first_peer(0, step), me.first_peer(1, step), me.tp_peer(step)]
    for peer in peers:
        pl.semaphore_signal(barrier, inc=1, device_id=peer, device_id_type=MESH)

    def heads_out(row, half, step):
        to = lax.rem(y + step, 4) * OWN_HEADS + half * HALF_HEADS
        return remote(
            ctx.at[row, pl.ds(pl.multiple_of(to, HALF_HEADS), HALF_HEADS)],
            by_head.at[y * OWN_ROWS + row, pl.ds(half * HALF_HEADS, HALF_HEADS)],
            early_send, a2a_recv.at[half], me.tp_peer(step),
        )

    ready("q")
    for i in range(OWN_ROWS):
        ready(("cache", i))
        if i == 0:
            load("gain", gain_hbm, gain, 11)
            load("gate", gate_hbm, contrib.at[:, pl.ds(0, UNITS)], 8)
            load("up", up_hbm, contrib.at[:, pl.ds(UNITS, UNITS)], 9)
            load("down", down_hbm, down_w, 10)
        if i == 2:
            load("uv", uv_hbm, uv, 5)
            load("out_w", out_w_hbm, out_w, 6)
            load("res", residual_hbm.at[:, own_lanes], res, 7)
            load("routes", routes_hbm, routes, 12)
            load("route_weights", route_weights_hbm, route_weights, 13)
        scores = tn_dot(qv[i], cv[i]) * score_scale
        usable = lax.broadcasted_iota(jnp.int32, scores.shape, 1) < lengths[i]
        peak = jnp.max(jnp.where(usable, scores, -1e30), axis=1, keepdims=True)
        soft = jnp.where(usable, jnp.exp(scores - peak), 0.0)
        total = jnp.sum(soft, axis=1, keepdims=True)
        summed = nt_dot(soft.astype(BF16), cv[i, :LAT, :])
        ctx[i] = (summed / total).astype(BF16)
        by_head[y * OWN_ROWS + i] = ctx[
            i, pl.ds(pl.multiple_of(y * OWN_HEADS, OWN_HEADS), OWN_HEADS), :
        ]
        if i == 2:
            pl.semaphore_wait(barrier, len(peers))
        if i >= 2:
            for row in (0, 1, 2) if i == 2 else (3,):
                for step in (2, 1, 3):
                    start(heads_out(row, 0, step))
    for i in range(OWN_ROWS):
        for step in (2, 1, 3):
            start(heads_out(i, 1, step))

    def spread_gain():
        turned_gain = pltpu.roll(gain[...], 64, axis=1)
        low = lax.broadcasted_iota(jnp.int32, (1, 128), 1) < 64
        for chip in range(D // CHIP):
            for q in range(4):
                at, odd = divmod(chip * CHIP + q * 128, 128)
                row = gain[at : at + 1, :]
                if odd:
                    row = turned_gain[at : at + 1, :]
                    if q < 3:
                        row = jnp.where(low, row, turned_gain[at + 1 : at + 2, :])
                gain_rows[q, chip : chip + 1, :] = row

    def turn_chip(chip, carry):
        for q in range(4):
            width = 128 if q < 3 else 64
            rows = contrib[pl.ds(pl.multiple_of(chip * CHIP + q * 128, 64), width), :]
            turned = rows.astype(F32).T * gain_rows[q, pl.ds(chip, 1), :][:, :width]
            gate_up_t[chip, :, q * 128 : q * 128 + width] = turned.astype(BF16)
        return carry

    def turn_step(i, carry):
        at = pl.ds(pl.multiple_of(i * 128, 128), 128)
        down_t[at, :] = down_w[:, at].astype(F32).T.astype(BF16)
        return carry

    for name in ("gain", "gate", "up", "down"):
        ready(name)
    spread_gain()
    lax.fori_loop(0, D // CHIP, turn_chip, 0)

    ready("uv")
    own_rows = pl.ds(pl.multiple_of(d * DP_ROWS, DP_ROWS), DP_ROWS)

    def project(half):
        others = by_head.at[pl.ds(0, DP_ROWS - OWN_ROWS), pl.ds(0, HALF_HEADS)]
        all_here(others, a2a_recv.at[half])
        heads = pl.ds(half * HALF_HEADS, HALF_HEADS)
        for part_of in range(LAT // 128):
            piece = by_head[:, heads, pl.ds(part_of * 128, 128)]
            by_head_f[part_of] = piece.astype(F32).reshape(DP_ROWS * HALF_HEADS, 128)
        for h in range(HALF_HEADS):
            picked = jnp.concatenate(
                [
                    by_head_f[part_of, pl.ds(h, DP_ROWS, stride=HALF_HEADS), :]
                    for part_of in range(LAT // 128)
                ],
                axis=1,
            ).astype(BF16)
            at = half * HALF_HEADS + h
            heads_all[own_rows, pl.ds(at * VHEAD, VHEAD)] = jnp.dot(
                picked, uv[at], preferred_element_type=F32
            ).astype(BF16)

    project(0)
    def head_block(half, dp):
        return heads_all.at[
            pl.ds(pl.multiple_of(dp * DP_ROWS, DP_ROWS), DP_ROWS), pl.ds(half * (INNER // 2), INNER // 2)
        ]

    def head_sibling(half, j, k, c):
        ref = head_block(half, me.block(half, j, k, c))
        return remote(
            ref, ref, early_send, ag_sib_recv.at[half], me.sibling()
        )

    heads_plane = gather_plane(
        me, head_block, start, (early_send, ag_recv), lambda *at: start(head_sibling(*at, me.c))
    )
    next(heads_plane)
    project(1)
    turned_to = 0
    for step in heads_plane:
        if turned_to < D // 128:
            lax.fori_loop(turned_to, turned_to + 7, turn_step, 0)
            turned_to += 7

    ready("out_w")
    part[...] = jnp.zeros_like(part)

    def out_step(k, carry):
        at = pl.ds(pl.multiple_of(k * 1024, 1024), 1024)
        part[...] += nt_dot(out_w[:, at], heads_all[:, at])
        return carry

    for half in range(2):
        all_here(heads_all.at[pl.ds(0, ROWS // 2), pl.ds(0, INNER // 2)], ag_sib_recv.at[half])
        lax.fori_loop(half * 2, half * 2 + 2, out_step, 0)
    for block in range(4):
        part_b[block] = part[:, block * TP_ROWS : (block + 1) * TP_ROWS].astype(BF16)
    for step in (2, 1, 3):
        start(remote(
            part_b.at[lax.rem(y + step, 4)], part_r.at[step - 1],
            rs_send, rs_recv.at[0], me.tp_peer(step),
        ))

    ready("routes")
    ready("route_weights")
    weight_row[...] = jnp.sum(
        jnp.where(routes[...] == d, route_weights[...], 0.0), axis=0, keepdims=True
    )

    ready("res")
    total = res[...].astype(F32) + part[:, own_lanes]
    all_here(part_r, rs_recv.at[0])
    for step in (1, 2, 3):
        total = total + part_r[step - 1].astype(F32)
    hidden = total.astype(BF16)
    hid[...] = hidden.astype(F32)
    own_cols = pl.ds(pl.multiple_of(d * COLS, 16), COLS)
    hid_t[own_cols, own_lanes] = hidden

    pairs = [(dz, dx) for dz in range(4) for dx in range(4)]

    def b_block(half, dp):
        return hid_t.at[rows_of(dp, PART_A + half * (PART_B // 2), PART_B // 2), :]

    def pair_of(half, j, k):
        return (k, j) if half == 0 else (j, k)

    nearest = sorted(pairs, key=lambda pair: (2 in pair, sum((0, 1, 2, 1)[step] for step in pair)))
    passed_on = nearest[:PASSED]

    def a_tp(pair, slot, lanes, step):
        ref = hid_t.at[rows_of(me.at(*pair, me.c), 0, PART_A), lanes]
        n = pair[0] * 4 + pair[1]
        alone = pair in passed_on and slot == sum(pair) % 2
        return remote(
            ref, ref, gather_send, gy_recv.at[n, 0 if alone else 1], me.tp_peer(step)
        )

    def a_sibling(pair, c):
        ref = hid_t.at[rows_of(me.at(*pair, c), 0, PART_A), :]
        late = 1 if 2 in pair else 0
        return remote(ref, ref, gather_send, gather_sib_recv.at[late], me.sibling())

    def a_plane(pair):
        ref = hid_t.at[rows_of(d, 0, PART_A), own_lanes]
        opposite = (4 - pair[0]) % 4 * 4 + (4 - pair[1]) % 4
        return remote(ref, ref, ga_send, ga_recv.at[opposite], me.pair_peer(pair))

    a_landed = []

    def a_here(pair):
        a_landed.append(pair)
        start(a_tp(pair, 0, me.lanes(0), 1))
        start(a_tp(pair, 1, me.lanes(0), 3))
        if len(a_landed) > PASSED:
            start(a_tp(pair, 2, me.lanes(0), 2))

    a_passed, a_done = [0], [0]

    def a_pass_on(count):
        for pair in a_landed[a_passed[0] : min(a_passed[0] + count, PASSED)]:
            if sum(pair) % 2 == 0:
                a_tp(pair, 0, me.lanes(3), 1).wait_recv()
                start(a_tp(pair, 2, me.lanes(3), 1))
            else:
                a_tp(pair, 1, me.lanes(1), 3).wait_recv()
                start(a_tp(pair, 2, me.lanes(1), 3))
        a_passed[0] += count

    def a_finish(count):
        for n in range(a_done[0], min(a_done[0] + count, 16)):
            pair = a_landed[n]
            copies = 2 if pair in passed_on else 3
            all_here(ya_pass.at[pl.ds(0, copies)], gy_recv.at[pair[0] * 4 + pair[1], 1])
            start(a_sibling(pair, me.c))
        a_done[0] += count

    def b_sibling(half, j, k, c):
        ref = b_block(half, me.block(half, j, k, c))
        late = 1 if 2 in (j, k) else 0
        return remote(ref, ref, gather_send, gather_sib_recv.at[late], me.sibling())

    def b_tp(lanes, step):
        ref = hid_t.at[rows_of(d, PART_A, PART_B), lanes]
        return remote(ref, ref, gather_send, hy_recv.at[0], me.tp_peer(step))

    b_plane = gather_plane(
        me, b_block, start, (gather_send, gb_recv), lambda *at: start(b_sibling(*at, me.c))
    )
    for step in (1, 3, 2):
        start(b_tp(me.lanes(0), step))
    for pair in nearest[1:]:
        start(a_plane(pair))
    a_here((0, 0))
    for pair in nearest[1:5]:
        opposite = ((4 - pair[0]) % 4, (4 - pair[1]) % 4)
        a_plane(opposite).wait_recv()
        a_here(pair)
    all_here(tp_r, hy_recv.at[0])
    next(b_plane)
    next(b_plane)
    a_pass_on(1)
    for pair in nearest[5:]:
        opposite = ((4 - pair[0]) % 4, (4 - pair[1]) % 4)
        a_plane(opposite).wait_recv()
        a_here(pair)
    a_pass_on(3)
    next(b_plane)
    next(b_plane)
    a_pass_on(4)
    next(b_plane)
    a_pass_on(2)
    next(b_plane)
    a_pass_on(2)
    next(b_plane)
    next(b_plane)

    gate_up[...] = jnp.zeros_like(gate_up)
    squares[...] = jnp.zeros_like(squares)

    def expert(pair):
        chip = me.at(*pair, 0) // 2
        rows = hid_t[pl.ds(pl.multiple_of(chip * CHIP, 64), CHIP), :]
        gate_up[...] += jnp.dot(gate_up_t[chip], rows, preferred_element_type=F32)
        wide = rows.astype(F32)
        squares[...] += jnp.sum((wide * wide).reshape(CHIP // 8, 8, ROWS), axis=0)

    early = nearest[:9]
    a_finish(9)
    next(b_plane)
    a_finish(1)
    next(b_plane)
    all_here(hid_t.at[pl.ds(0, 9 * COLS)], gather_sib_recv.at[0])
    for n in range(2):
        for pair in early[3 * n : 3 * n + 3]:
            expert(pair)
        a_finish(2)
        next(b_plane)
    a_finish(16)
    for pair in early[6:]:
        expert(pair)
    all_here(hid_t.at[pl.ds(0, 7 * COLS)], gather_sib_recv.at[1])
    for pair in nearest[9:]:
        expert(pair)

    inverse_rms = lax.rsqrt(jnp.sum(squares[...], axis=0, keepdims=True) * (1.0 / D) + epsilon)
    gate_proj = gate_up[:UNITS, :] * inverse_rms
    up_proj = gate_up[UNITS:, :] * inverse_rms
    silu = gate_proj / (1.0 + jnp.exp(-gate_proj))
    act[...] = (silu * up_proj * weight_row[...]).astype(BF16)

    def from_core(pair, c):
        n = pair[0] * 4 + pair[1]
        return remote(
            contrib.at[rows_of(me.at(*pair, c), 0, COLS), :], from_sib.at[n],
            sum_send, sib_recv.at[n], me.sibling(),
        )

    def compute(pair):
        at = pl.ds(pl.multiple_of(me.at(*pair, 0) * COLS, 16), 2 * COLS)
        contrib[at, :] = jnp.dot(down_t[at, :], act[...], preferred_element_type=F32).astype(BF16)
        start(from_core(pair, 1 - me.c))

    sib_here = set()

    def sibling_here(pair):
        if pair not in sib_here:
            sib_here.add(pair)
            from_core(pair, me.c).wait_recv()

    def ya_rows(pair):
        return rows_of(me.at(*pair, me.c), 0, SUM_A)

    def ya_far(pair, step):
        n = pair[0] * 4 + pair[1]
        return remote(
            contrib.at[ya_rows(pair), me.lanes(2)], ya_pass.at[n],
            sum_send, yp_recv.at[n], me.tp_peer(step),
        )

    def ya_near(pair, step):
        n = pair[0] * 4 + pair[1]
        return remote(
            contrib.at[ya_rows(pair), me.lanes(step)], ya_ring.at[n, step - 1],
            sum_send, yr_recv.at[n], me.tp_peer(step),
        )

    passed_pairs = []

    def a_first(pair):
        sibling_here(pair)
        at = ya_rows(pair)
        theirs = from_sib[pair[0] * 4 + pair[1], :SUM_A, :]
        contrib[at, :] = (contrib[at, :].astype(F32) + theirs.astype(F32)).astype(BF16)
        if len(passed_pairs) < SUM_PASSED:
            passed_pairs.append(pair)
            far_step = 1 if sum(pair) % 2 == 0 else 3
            start(ya_far(pair, far_step))
            start(ya_near(pair, 4 - far_step))
        else:
            for step in (1, 3, 2):
                start(ya_near(pair, step))

    def a_second(pair):
        step = 1 if sum(pair) % 2 == 0 else 3
        ya_far(pair, step).wait_recv()
        at = ya_rows(pair)
        passed = ya_pass[pair[0] * 4 + pair[1]].astype(F32)
        contrib[at, me.lanes(step)] = (contrib[at, me.lanes(step)].astype(F32) + passed).astype(BF16)
        start(ya_near(pair, step))

    def a_give(pair):
        n = pair[0] * 4 + pair[1]
        return remote(
            a_sum.at[n], a_ring.at[n - 1], ar_send, ar_recv.at[0], me.pair_peer(pair)
        )

    def a_third(pair):
        n = pair[0] * 4 + pair[1]
        value = contrib[ya_rows(pair), own_lanes].astype(F32)
        steps = (1, 3) if pair in passed_pairs else (1, 3, 2)
        all_here(ya_ring.at[n, pl.ds(0, len(steps))], yr_recv.at[n])
        for step in steps:
            value = value + ya_ring[n, step - 1].astype(F32)
        a_sum[n] = value.astype(BF16)
        if n:
            start(a_give(pair))

    def b_own(half, j, k):
        return contrib.at[
            rows_of(me.block(half, j, k, me.c), SUM_A + half * (SUM_B // 2), SUM_B // 2), :
        ]

    def b_touch(half, j, k):
        pair = pair_of(half, j, k)
        sibling_here(pair)
        theirs = from_sib[
            pair[0] * 4 + pair[1], pl.ds(SUM_A + half * (SUM_B // 2), SUM_B // 2), :
        ]
        return b_own(half, j, k)[...].astype(F32) + theirs.astype(F32)

    def b_final(half, value):
        at = pl.ds(half * (SUM_B // 2), SUM_B // 2)
        plane_sum[at, :] = value
        plane_sum_b[at, :] = value.astype(BF16)

    b_back = scatter_plane(
        me, b_own, b_touch, b_final, start, all_here, (b_pass, b_ring, b_line),
        (sum_send, bp_recv, br_recv, bl_recv),
    )
    order = [(2, 2), (2, 1), (1, 2), (3, 2), (2, 3), (1, 1), (1, 3), (3, 1), (3, 3)]
    order += [(2, 0), (0, 2), (1, 0), (0, 1), (3, 0), (0, 3), (0, 0)]
    for n, pair in enumerate(order):
        compute(pair)
        if n in (3, 6, 9, 12):
            next(b_back)
        if n >= 3:
            a_first(order[n - 3])
        if n >= 14:
            a_second(order[n - 14])
    for n in range(13, 16):
        a_first(order[n])
        a_second(order[n - 11])
    next(b_back)
    next(b_back)
    for n in range(5, SUM_PASSED):
        a_second(order[n])
    for n, pair in enumerate(order):
        a_third(pair)
        if n in (3, 7, 11):
            next(b_back)
    next(b_back)

    def b_tp_sum(step):
        return remote(
            plane_sum_b.at[:, me.lanes(step)], tp_r.at[step - 1],
            sum_send, tp_recv.at[0], me.tp_peer(step),
        )

    for step in (2, 1, 3):
        start(b_tp_sum(step))
    moe = a_sum[0].astype(F32)
    all_here(a_ring, ar_recv.at[0])
    for pair in order[:-1]:
        moe = moe + a_ring[pair[0] * 4 + pair[1] - 1].astype(F32)
    out[:SUM_A, :] = (hid[:SUM_A, :] + moe).astype(BF16)
    moe = plane_sum[:, own_lanes]
    all_here(tp_r, tp_recv.at[0])
    for step in (1, 3, 2):
        moe = moe + tp_r[step - 1].astype(F32)
    out[SUM_A:, :] = (hid[SUM_A:, :] + moe).astype(BF16)

    for group in sends:
        sized = {id(rs_send): part_r, id(ga_send): a_ring, id(ar_send): a_ring}.get(id(group))
        if sized is None:
            sized = hid_t.at[pl.ds(0, group.total // (2 * ROWS))]
        assert group.total == 2 * math.prod(sized.shape), group.total
        remote(sized, sized, group, rs_recv.at[0], me.sibling()).copy.wait_send()


def local(
    queries, latent_cache, lengths, uv_weight, out_weight, residual, norm_gain,
    gate_weight, up_weight, down_weight, routes, route_weights,
):
    anywhere = pl.BlockSpec(memory_space=pl.ANY)
    vmem = pl.BlockSpec(memory_space=pltpu.VMEM)
    smem = pl.BlockSpec(memory_space=pltpu.SMEM)
    dma = pltpu.SemaphoreType.DMA
    scratch = [
        pltpu.VMEM((D // 128, 128), F32),
        pltpu.VMEM(routes.shape[::-1], jnp.int32),
        pltpu.VMEM(routes.shape[::-1], F32),
        pltpu.VMEM((OWN_ROWS, KEY, HEADS), BF16),
        pltpu.VMEM((OWN_ROWS, KEY, CTX), BF16),
        pltpu.VMEM((OWN_HEADS, LAT, VHEAD), BF16),
        pltpu.VMEM((COLS, INNER), BF16),
        pltpu.VMEM((COLS, TP_ROWS), BF16),
        pltpu.VMEM((UNITS, D), BF16),
        pltpu.VMEM((D // CHIP, 2 * UNITS, CHIP), BF16),
        pltpu.VMEM((D, UNITS), BF16),
        pltpu.VMEM((OWN_ROWS, HEADS, LAT), BF16),
        pltpu.VMEM((DP_ROWS, OWN_HEADS, LAT), BF16),
        pltpu.VMEM((LAT // 128, DP_ROWS * HALF_HEADS, 128), F32),
        pltpu.VMEM((ROWS, INNER), BF16),
        pltpu.VMEM((COLS, ROWS), F32),
        pltpu.VMEM((4, COLS, TP_ROWS), BF16),
        pltpu.VMEM((3, COLS, TP_ROWS), BF16),
        pltpu.VMEM((COLS, TP_ROWS), F32),
        pltpu.VMEM((D, ROWS), BF16),
        pltpu.VMEM((2 * UNITS, ROWS), F32),
        pltpu.VMEM((4, D // CHIP, 128), F32),
        pltpu.VMEM((8, ROWS), F32),
        pltpu.VMEM((UNITS, ROWS), BF16),
        pltpu.VMEM((D, ROWS), BF16),
        pltpu.VMEM((16, COLS, ROWS), BF16),
        pltpu.VMEM((SUM_B, ROWS), F32),
        pltpu.VMEM((SUM_B, ROWS), BF16),
        pltpu.VMEM((3, SUM_B, TP_ROWS), BF16),
        pltpu.VMEM((1, ROWS), F32),
        pltpu.VMEM((2, 2, SUM_B // 2, ROWS), BF16),
        pltpu.VMEM((2, 12, SUM_B // 2, ROWS), BF16),
        pltpu.VMEM((2, 3, SUM_B // 2, ROWS), BF16),
        pltpu.VMEM((15, SUM_A, TP_ROWS), BF16),
        pltpu.VMEM((16, SUM_A, TP_ROWS), BF16),
        pltpu.VMEM((16, SUM_A, TP_ROWS), BF16),
        pltpu.VMEM((16, 3, SUM_A, TP_ROWS), BF16),
        dma((14,)), dma((6,)),
        dma((2,)), dma((2, 16)), dma((2,)),
        dma((1,)), dma((1,)),
        dma((16,)), dma((16, 2)), dma((2, 16)), dma((2,)),
        dma((16,)), dma((16,)), dma((16,)), dma((1,)),
        dma((2, 2)), dma((2, 4)), dma((2,)), dma((1,)),
    ]
    return pl.pallas_call(
        kernel,
        out_shape=jax.ShapeDtypeStruct((COLS, TP_ROWS), BF16),
        in_specs=[smem] + [anywhere] * 11,
        out_specs=vmem,
        scratch_shapes=scratch,
        compiler_params=pltpu.CompilerParams(
            collective_id=0, has_side_effects=True, vmem_limit_bytes=62 * 1024 * 1024
        ),
        name="decode_step",
    )(
        lengths, jnp.swapaxes(queries, 1, 2), jnp.swapaxes(latent_cache, 1, 2), uv_weight,
        out_weight.T, residual.T, norm_gain.reshape(D // 128, 128),
        gate_weight[0], up_weight[0], down_weight[0], routes.T, route_weights.T,
    ).T


def solution(mesh):
    placed = (
        P(("dp", "tp"), None, None),
        P(("dp", "tp"), None, None),
        P(("dp", "tp")),
        P("tp", None, None),
        P("tp", "dp"),
        P(None, "dp"),
        P(),
        P("dp", None, "tp"),
        P("dp", None, "tp"),
        P("dp", "tp", None),
        P(),
        P(),
    )
    return jax.shard_map(
        local, mesh=mesh, in_specs=placed, out_specs=P("tp", "dp"), check_vma=False
    )
```

```python
import math

import jax
import jax.numpy as jnp
from jax import lax
from jax.experimental import pallas as pl
from jax.experimental.pallas import tpu as pltpu
from jax.sharding import PartitionSpec as P

F32 = jnp.float32
BF16 = jnp.bfloat16
MESH = pl.DeviceIdType.MESH

LAT = 512
KEY = 576
CTX = 1024
HEADS = 128
OWN_HEADS = 32
HALF_HEADS = 16
VHEAD = 128
ROWS = 512
OWN_ROWS = 4
DP_ROWS = 16
TP_ROWS = 128
D = 7168
COLS = 224
PART_A = 96
PART_B = 128
INNER = 4096
UNITS = 256
CHIP = 448
DP = 32

score_scale = 192.0 ** (-0.5)
epsilon = 1e-06

SUM_A = 64
SUM_B = 160
PASSED = 12
SUM_PASSED = 12


def tn_dot(a, b):
    return lax.dot_general(a, b, (((0,), (0,)), ((), ())), preferred_element_type=F32)


def nt_dot(a, b):
    return lax.dot_general(a, b, (((1,), (1,)), ((), ())), preferred_element_type=F32)


class Place:
    def __init__(self):
        dp = lax.axis_index("dp")
        self.y = lax.axis_index("tp")
        self.d = dp
        self.c = lax.rem(dp, 2)
        self.x = lax.rem(dp // 2, 4)
        self.z = dp // 8

    def device(self, z=None, x=None, c=None, y=None):
        z = self.z if z is None else z
        x = self.x if x is None else x
        c = self.c if c is None else c
        y = self.y if y is None else y
        return ((z * 4 + x) * 2 + c, y)

    def sibling(self):
        return self.device(c=1 - self.c)

    def tp_peer(self, step):
        return self.device(y=lax.rem(self.y + step, 4))

    def first(self, half):
        return self.x if half == 0 else self.z

    def second(self, half):
        return self.z if half == 0 else self.x

    def first_peer(self, half, step):
        if half == 0:
            return self.device(x=lax.rem(self.x + step, 4))
        return self.device(z=lax.rem(self.z + step, 4))

    def second_peer(self, half, step):
        return self.first_peer(1 - half, step)

    def pair_peer(self, pair):
        return (self.at(*pair, self.c), self.y)

    def lanes(self, step):
        at = lax.rem(self.y + step, 4) * TP_ROWS
        return pl.ds(pl.multiple_of(at, TP_ROWS), TP_ROWS)

    def at(self, dz, dx, c):
        return (lax.rem(self.z + dz, 4) * 4 + lax.rem(self.x + dx, 4)) * 2 + c

    def block(self, half, j, k, c):
        a = lax.rem(self.first(half) + j, 4)
        b = lax.rem(self.second(half) + k, 4)
        z, x = (b, a) if half == 0 else (a, b)
        return (z * 4 + x) * 2 + c


class Sends:
    def __init__(self, sems, group):
        self.sem, self.total, self.at = sems.at[group], 0, self

    def __getitem__(self, index):
        return self


class Copy:
    def __init__(self, src, dst, send, recv, device):
        self.sends, self.bytes = send, 2 * math.prod(src.shape)
        self.copy = pltpu.make_async_remote_copy(
            src_ref=src, dst_ref=dst, send_sem=send.sem, recv_sem=recv,
            device_id=device, device_id_type=MESH,
        )

    def start(self):
        self.sends.total += self.bytes
        self.copy.start()

    def wait_recv(self):
        self.copy.wait_recv()


def remote(src, dst, send, recv, device):
    return Copy(src, dst, send, recv, device)


def rows_of(dp, offset, count):
    return pl.ds(pl.multiple_of(dp * COLS + offset, 16), count)


def gather_plane(me, blk, start, sems, landed):
    send_sem, recv_sem = sems

    def ref_of(half, j, k):
        return blk(half, me.block(half, j, k, me.c))

    def send(half, j, k, device, rj, rk):
        ref = ref_of(half, j, k)
        start(remote(
            ref, ref, send_sem, recv_sem.at[half, rj * 4 + rk], device
        ))

    def arrived(half, j, k):
        ref = ref_of(half, j, k)
        remote(
            ref, ref, send_sem, recv_sem.at[half, j * 4 + k], me.sibling()
        ).wait_recv()

    def second_axis(half, j):
        send(half, j, 0, me.second_peer(half, 1), j, 3)
        send(half, j, 0, me.second_peer(half, 3), j, 1)
        if j == 2:
            send(half, j, 0, me.second_peer(half, 2), j, 2)

    for half in range(2):
        for step in (1, 3, 2):
            send(half, 0, 0, me.first_peer(half, step), 4 - step, 0)
        second_axis(half, 0)
        landed(half, 0, 0)
        yield
    for j in (1, 3):
        for half in range(2):
            arrived(half, j, 0)
            second_axis(half, j)
    for j in (1, 3):
        for half in range(2):
            landed(half, j, 0)
    yield
    for half in range(2):
        arrived(half, 2, 0)
        second_axis(half, 2)
    for half in range(2):
        landed(half, 2, 0)
    yield
    for j in (0, 1, 3, 2):
        for half in range(2):
            arrived(half, j, 3)
            if j == 0:
                send(half, j, 3, me.second_peer(half, 1), j, 2)
            arrived(half, j, 1)
            if j == 1:
                send(half, j, 1, me.second_peer(half, 3), j, 2)
            if j == 3:
                send(half, j, 3 - 2 * me.c, me.second_peer(half, 1 + 2 * me.c), j, 2)
        for half in range(2):
            landed(half, j, 3)
            landed(half, j, 1)
        yield
    for j in (0, 1, 3, 2):
        for half in range(2):
            arrived(half, j, 2)
            landed(half, j, 2)
        yield


def scatter_plane(me, own, touch, finish, start, all_here, bufs, sems):
    pass_r, ring_r, line_r = bufs
    sends, pass_recv, ring_recv, line_recv = sems

    def far(half, j):
        return remote(
            own(half, j, 2), pass_r.at[half, j - 1], sends, pass_recv.at[half, j - 1],
            me.second_peer(half, 1 if j == 2 else 3),
        )

    def near(half, j, k):
        slot = j * 3 + k - 1
        return remote(
            own(half, j, k), ring_r.at[half, slot], sends, ring_recv.at[half, j],
            me.second_peer(half, k),
        )

    def line(half, j):
        return remote(
            own(half, j, 0), line_r.at[half, j - 1], sends, line_recv.at[half],
            me.first_peer(half, j),
        )

    def give(j, k):
        for half in range(2):
            own(half, j, k)[...] = touch(half, j, k).astype(BF16)
            start(near(half, j, k))

    def give_passed(j, k):
        for half in range(2):
            value = touch(half, j, k)
            far(half, j).wait_recv()
            value = value + pass_r[half, j - 1].astype(F32)
            own(half, j, k)[...] = value.astype(BF16)
            start(near(half, j, k))

    def gathered(half, j):
        value = touch(half, j, 0)
        steps = (1, 3) if j in (1, 2) else (1, 3, 2)
        all_here(ring_r.at[half, pl.ds(0, len(steps))], ring_recv.at[half, j])
        for k in steps:
            value = value + ring_r[half, j * 3 + k - 1].astype(F32)
        return value

    for j in (2, 1):
        for half in range(2):
            own(half, j, 2)[...] = touch(half, j, 2).astype(BF16)
            start(far(half, j))
        yield
    give(2, 3)
    give(1, 1)
    yield
    give(3, 2)
    give(3, 1)
    give(3, 3)
    yield
    give_passed(2, 1)
    give_passed(1, 3)
    yield
    give(0, 2)
    give(0, 1)
    give(0, 3)
    yield
    for j in (2, 1, 3):
        for half in range(2):
            own(half, j, 0)[...] = gathered(half, j).astype(BF16)
            start(line(half, j))
        yield
    for half in range(2):
        value = gathered(half, 0)
        all_here(line_r.at[half], line_recv.at[half])
        for j in (1, 3, 2):
            value = value + line_r[half, j - 1].astype(F32)
        finish(half, value)
    yield


def kernel(
    lengths, q_hbm, cache_hbm, uv_hbm, out_w_hbm, residual_hbm, gain_hbm, gate_hbm, up_hbm, down_hbm,
    routes_hbm, route_weights_hbm, out,
    gain, routes, route_weights, qv, cv, uv, out_w, res, down_w, gate_up_t, down_t,
    ctx, by_head, by_head_f, heads_all, part, part_b, part_r, hid, hid_t, gate_up,
    gain_rows, squares, act, contrib, from_sib, plane_sum, plane_sum_b, tp_r, weight_row,
    b_pass, b_ring, b_line, a_ring, a_sum, ya_pass, ya_ring,
    load_sem, send_sems, a2a_recv, ag_recv, ag_sib_recv, rs_recv, hy_recv,
    ga_recv, gy_recv, gb_recv, gather_sib_recv,
    sib_recv, yp_recv, yr_recv, ar_recv, bp_recv, br_recv, bl_recv, tp_recv,
):
    me = Place()
    y, d = me.y, me.d
    own_lanes = pl.ds(pl.multiple_of(y * TP_ROWS, TP_ROWS), TP_ROWS)

    loads = {}
    sends = [Sends(send_sems, group) for group in range(7)]
    early_send, rs_send, gather_send, ga_send, sum_send, ar_send, tp_send = sends

    def load(name, src, dst, index):
        copy = pltpu.make_async_copy(src, dst, load_sem.at[index])
        copy.start()
        loads[name] = copy

    def ready(name):
        loads.pop(name).wait()

    def start(copy):
        copy.start()

    def all_here(ref, recv):
        remote(ref, ref, early_send, recv, me.sibling()).wait_recv()

    load("q", q_hbm, qv, 0)
    for i in range(OWN_ROWS):
        load(("cache", i), cache_hbm.at[i], cv.at[i], 1 + i)

    barrier = pltpu.get_barrier_semaphore()
    peers = [me.sibling()]
    for step in (1, 2, 3):
        peers += [me.first_peer(0, step), me.first_peer(1, step), me.tp_peer(step)]
    for peer in peers:
        pl.semaphore_signal(barrier, inc=1, device_id=peer, device_id_type=MESH)

    def heads_out(row, half, step):
        to = lax.rem(y + step, 4) * OWN_HEADS + half * HALF_HEADS
        return remote(
            ctx.at[row, pl.ds(pl.multiple_of(to, HALF_HEADS), HALF_HEADS)],
            by_head.at[y * OWN_ROWS + row, pl.ds(half * HALF_HEADS, HALF_HEADS)],
            early_send, a2a_recv.at[half], me.tp_peer(step),
        )

    ready("q")
    for i in range(OWN_ROWS):
        ready(("cache", i))
        if i == 0:
            load("gain", gain_hbm, gain, 11)
            load("gate", gate_hbm, contrib.at[:, pl.ds(0, UNITS)], 8)
            load("up", up_hbm, contrib.at[:, pl.ds(UNITS, UNITS)], 9)
            load("down", down_hbm, down_w, 10)
        if i == 2:
            load("uv", uv_hbm, uv, 5)
            load("out_w", out_w_hbm, out_w, 6)
            load("res", residual_hbm.at[:, own_lanes], res, 7)
            load("routes", routes_hbm, routes, 12)
            load("route_weights", route_weights_hbm, route_weights, 13)
        scores = tn_dot(qv[i], cv[i]) * score_scale
        usable = lax.broadcasted_iota(jnp.int32, scores.shape, 1) < lengths[i]
        peak = jnp.max(jnp.where(usable, scores, -1e30), axis=1, keepdims=True)
        soft = jnp.where(usable, jnp.exp(scores - peak), 0.0)
        total = jnp.sum(soft, axis=1, keepdims=True)
        summed = nt_dot(soft.astype(BF16), cv[i, :LAT, :])
        ctx[i] = (summed / total).astype(BF16)
        by_head[y * OWN_ROWS + i] = ctx[
            i, pl.ds(pl.multiple_of(y * OWN_HEADS, OWN_HEADS), OWN_HEADS), :
        ]
        if i == 2:
            pl.semaphore_wait(barrier, len(peers))
        if i >= 2:
            for row in (0, 1, 2) if i == 2 else (3,):
                for step in (2, 1, 3):
                    start(heads_out(row, 0, step))
    for i in range(OWN_ROWS):
        for step in (2, 1, 3):
            start(heads_out(i, 1, step))

    def spread_gain():
        turned_gain = pltpu.roll(gain[...], 64, axis=1)
        low = lax.broadcasted_iota(jnp.int32, (1, 128), 1) < 64
        for chip in range(D // CHIP):
            for q in range(4):
                at, odd = divmod(chip * CHIP + q * 128, 128)
                row = gain[at : at + 1, :]
                if odd:
                    row = turned_gain[at : at + 1, :]
                    if q < 3:
                        row = jnp.where(low, row, turned_gain[at + 1 : at + 2, :])
                gain_rows[q, chip : chip + 1, :] = row

    def turn_chip(chip, carry):
        for q in range(4):
            width = 128 if q < 3 else 64
            rows = contrib[pl.ds(pl.multiple_of(chip * CHIP + q * 128, 64), width), :]
            turned = rows.astype(F32).T * gain_rows[q, pl.ds(chip, 1), :][:, :width]
            gate_up_t[chip, :, q * 128 : q * 128 + width] = turned.astype(BF16)
        return carry

    def turn_step(i, carry):
        at = pl.ds(pl.multiple_of(i * 128, 128), 128)
        down_t[at, :] = down_w[:, at].astype(F32).T.astype(BF16)
        return carry

    for name in ("gain", "gate", "up", "down"):
        ready(name)
    spread_gain()
    lax.fori_loop(0, D // CHIP, turn_chip, 0)

    ready("uv")
    own_rows = pl.ds(pl.multiple_of(d * DP_ROWS, DP_ROWS), DP_ROWS)

    def project(half):
        others = by_head.at[pl.ds(0, DP_ROWS - OWN_ROWS), pl.ds(0, HALF_HEADS)]
        all_here(others, a2a_recv.at[half])
        heads = pl.ds(half * HALF_HEADS, HALF_HEADS)
        for part_of in range(LAT // 128):
            piece = by_head[:, heads, pl.ds(part_of * 128, 128)]
            by_head_f[part_of] = piece.astype(F32).reshape(DP_ROWS * HALF_HEADS, 128)
        for h in range(HALF_HEADS):
            picked = jnp.concatenate(
                [
                    by_head_f[part_of, pl.ds(h, DP_ROWS, stride=HALF_HEADS), :]
                    for part_of in range(LAT // 128)
                ],
                axis=1,
            ).astype(BF16)
            at = half * HALF_HEADS + h
            heads_all[own_rows, pl.ds(at * VHEAD, VHEAD)] = jnp.dot(
                picked, uv[at], preferred_element_type=F32
            ).astype(BF16)

    project(0)
    def head_block(half, dp):
        return heads_all.at[
            pl.ds(pl.multiple_of(dp * DP_ROWS, DP_ROWS), DP_ROWS), pl.ds(half * (INNER // 2), INNER // 2)
        ]

    def head_sibling(half, j, k, c):
        ref = head_block(half, me.block(half, j, k, c))
        return remote(
            ref, ref, early_send, ag_sib_recv.at[half], me.sibling()
        )

    heads_plane = gather_plane(
        me, head_block, start, (early_send, ag_recv), lambda *at: start(head_sibling(*at, me.c))
    )
    next(heads_plane)
    project(1)
    turned_to = 0
    for step in heads_plane:
        if turned_to < D // 128:
            lax.fori_loop(turned_to, turned_to + 7, turn_step, 0)
            turned_to += 7

    ready("out_w")
    part[...] = jnp.zeros_like(part)

    def out_step(k, carry):
        at = pl.ds(pl.multiple_of(k * 1024, 1024), 1024)
        part[...] += nt_dot(out_w[:, at], heads_all[:, at])
        return carry

    for half in range(2):
        all_here(heads_all.at[pl.ds(0, ROWS // 2), pl.ds(0, INNER // 2)], ag_sib_recv.at[half])
        lax.fori_loop(half * 2, half * 2 + 2, out_step, 0)
    for block in range(4):
        part_b[block] = part[:, block * TP_ROWS : (block + 1) * TP_ROWS].astype(BF16)
    for step in (2, 1, 3):
        start(remote(
            part_b.at[lax.rem(y + step, 4)], part_r.at[step - 1],
            rs_send, rs_recv.at[0], me.tp_peer(step),
        ))

    ready("routes")
    ready("route_weights")
    weight_row[...] = jnp.sum(
        jnp.where(routes[...] == d, route_weights[...], 0.0), axis=0, keepdims=True
    )

    ready("res")
    total = res[...].astype(F32) + part[:, own_lanes]
    all_here(part_r, rs_recv.at[0])
    for step in (1, 2, 3):
        total = total + part_r[step - 1].astype(F32)
    hidden = total.astype(BF16)
    hid[...] = hidden.astype(F32)
    own_cols = pl.ds(pl.multiple_of(d * COLS, 16), COLS)
    hid_t[own_cols, own_lanes] = hidden

    pairs = [(dz, dx) for dz in range(4) for dx in range(4)]

    def b_block(half, dp):
        return hid_t.at[rows_of(dp, PART_A + half * (PART_B // 2), PART_B // 2), :]

    def pair_of(half, j, k):
        return (k, j) if half == 0 else (j, k)

    nearest = sorted(pairs, key=lambda pair: (2 in pair, sum((0, 1, 2, 1)[step] for step in pair)))
    passed_on = nearest[:PASSED]

    def a_tp(pair, slot, lanes, step):
        ref = hid_t.at[rows_of(me.at(*pair, me.c), 0, PART_A), lanes]
        n = pair[0] * 4 + pair[1]
        alone = pair in passed_on and slot == sum(pair) % 2
        return remote(
            ref, ref, gather_send, gy_recv.at[n, 0 if alone else 1], me.tp_peer(step)
        )

    def a_sibling(pair, c):
        ref = hid_t.at[rows_of(me.at(*pair, c), 0, PART_A), :]
        late = 1 if 2 in pair else 0
        return remote(ref, ref, gather_send, gather_sib_recv.at[late], me.sibling())

    def a_plane(pair):
        ref = hid_t.at[rows_of(d, 0, PART_A), own_lanes]
        opposite = (4 - pair[0]) % 4 * 4 + (4 - pair[1]) % 4
        return remote(ref, ref, ga_send, ga_recv.at[opposite], me.pair_peer(pair))

    a_landed = []

    def a_here(pair):
        a_landed.append(pair)
        start(a_tp(pair, 0, me.lanes(0), 1))
        start(a_tp(pair, 1, me.lanes(0), 3))
        if len(a_landed) > PASSED:
            start(a_tp(pair, 2, me.lanes(0), 2))

    a_passed, a_done = [0], [0]

    def a_pass_on(count):
        for pair in a_landed[a_passed[0] : min(a_passed[0] + count, PASSED)]:
            if sum(pair) % 2 == 0:
                a_tp(pair, 0, me.lanes(3), 1).wait_recv()
                start(a_tp(pair, 2, me.lanes(3), 1))
            else:
                a_tp(pair, 1, me.lanes(1), 3).wait_recv()
                start(a_tp(pair, 2, me.lanes(1), 3))
        a_passed[0] += count

    def a_finish(count):
        for n in range(a_done[0], min(a_done[0] + count, 16)):
            pair = a_landed[n]
            copies = 2 if pair in passed_on else 3
            all_here(hid_t.at[pl.ds(0, PART_A * copies), pl.ds(0, TP_ROWS)], gy_recv.at[pair[0] * 4 + pair[1], 1])
            start(a_sibling(pair, me.c))
        a_done[0] += count

    def b_sibling(half, j, k, c):
        ref = b_block(half, me.block(half, j, k, c))
        late = 1 if 2 in (j, k) else 0
        return remote(ref, ref, gather_send, gather_sib_recv.at[late], me.sibling())

    def b_tp(lanes, step):
        ref = hid_t.at[rows_of(d, PART_A, PART_B), lanes]
        return remote(ref, ref, gather_send, hy_recv.at[0], me.tp_peer(step))

    b_plane = gather_plane(
        me, b_block, start, (gather_send, gb_recv), lambda *at: start(b_sibling(*at, me.c))
    )
    for step in (1, 3, 2):
        start(b_tp(me.lanes(0), step))
    for pair in nearest[1:]:
        start(a_plane(pair))
    a_here((0, 0))
    for pair in nearest[1:5]:
        opposite = ((4 - pair[0]) % 4, (4 - pair[1]) % 4)
        a_plane(opposite).wait_recv()
        a_here(pair)
    all_here(hid_t.at[pl.ds(0, 3 * PART_B), pl.ds(0, TP_ROWS)], hy_recv.at[0])
    next(b_plane)
    next(b_plane)
    a_pass_on(1)
    for pair in nearest[5:]:
        opposite = ((4 - pair[0]) % 4, (4 - pair[1]) % 4)
        a_plane(opposite).wait_recv()
        a_here(pair)
    a_pass_on(3)
    next(b_plane)
    next(b_plane)
    a_pass_on(4)
    next(b_plane)
    a_pass_on(2)
    next(b_plane)
    a_pass_on(2)
    next(b_plane)
    next(b_plane)

    gate_up[...] = jnp.zeros_like(gate_up)
    squares[...] = jnp.zeros_like(squares)

    def expert(pair):
        chip = me.at(*pair, 0) // 2
        rows = hid_t[pl.ds(pl.multiple_of(chip * CHIP, 64), CHIP), :]
        gate_up[...] += jnp.dot(gate_up_t[chip], rows, preferred_element_type=F32)
        wide = rows.astype(F32)
        squares[...] += jnp.sum((wide * wide).reshape(CHIP // 8, 8, ROWS), axis=0)

    early = nearest[:9]
    a_finish(9)
    next(b_plane)
    a_finish(1)
    next(b_plane)
    all_here(hid_t.at[pl.ds(0, 9 * COLS)], gather_sib_recv.at[0])
    for n in range(2):
        for pair in early[3 * n : 3 * n + 3]:
            expert(pair)
        a_finish(2)
        next(b_plane)
    a_finish(16)
    for pair in early[6:]:
        expert(pair)
    all_here(hid_t.at[pl.ds(0, 7 * COLS)], gather_sib_recv.at[1])
    for pair in nearest[9:]:
        expert(pair)

    inverse_rms = lax.rsqrt(jnp.sum(squares[...], axis=0, keepdims=True) * (1.0 / D) + epsilon)
    gate_proj = gate_up[:UNITS, :] * inverse_rms
    up_proj = gate_up[UNITS:, :] * inverse_rms
    silu = gate_proj / (1.0 + jnp.exp(-gate_proj))
    act[...] = (silu * up_proj * weight_row[...]).astype(BF16)

    def from_core(pair, c):
        n = pair[0] * 4 + pair[1]
        return remote(
            contrib.at[rows_of(me.at(*pair, c), 0, COLS), :], from_sib.at[n],
            sum_send, sib_recv.at[n], me.sibling(),
        )

    def compute(pair):
        at = pl.ds(pl.multiple_of(me.at(*pair, 0) * COLS, 16), 2 * COLS)
        contrib[at, :] = jnp.dot(down_t[at, :], act[...], preferred_element_type=F32).astype(BF16)
        start(from_core(pair, 1 - me.c))

    sib_here = set()

    def sibling_here(pair):
        if pair not in sib_here:
            sib_here.add(pair)
            from_core(pair, me.c).wait_recv()

    def ya_rows(pair):
        return rows_of(me.at(*pair, me.c), 0, SUM_A)

    def ya_far(pair, step):
        n = pair[0] * 4 + pair[1]
        return remote(
            contrib.at[ya_rows(pair), me.lanes(2)], ya_pass.at[n],
            sum_send, yp_recv.at[n], me.tp_peer(step),
        )

    def ya_near(pair, step):
        n = pair[0] * 4 + pair[1]
        return remote(
            contrib.at[ya_rows(pair), me.lanes(step)], ya_ring.at[n, step - 1],
            sum_send, yr_recv.at[n], me.tp_peer(step),
        )

    passed_pairs = []

    def a_first(pair):
        sibling_here(pair)
        at = ya_rows(pair)
        theirs = from_sib[pair[0] * 4 + pair[1], :SUM_A, :]
        contrib[at, :] = (contrib[at, :].astype(F32) + theirs.astype(F32)).astype(BF16)
        if len(passed_pairs) < SUM_PASSED:
            passed_pairs.append(pair)
            far_step = 1 if sum(pair) % 2 == 0 else 3
            start(ya_far(pair, far_step))
            start(ya_near(pair, 4 - far_step))
        else:
            for step in (1, 3, 2):
                start(ya_near(pair, step))

    def a_second(pair):
        step = 1 if sum(pair) % 2 == 0 else 3
        ya_far(pair, step).wait_recv()
        at = ya_rows(pair)
        passed = ya_pass[pair[0] * 4 + pair[1]].astype(F32)
        contrib[at, me.lanes(step)] = (contrib[at, me.lanes(step)].astype(F32) + passed).astype(BF16)
        start(ya_near(pair, step))

    def a_give(pair):
        n = pair[0] * 4 + pair[1]
        return remote(
            a_sum.at[n], a_ring.at[n - 1], ar_send, ar_recv.at[0], me.pair_peer(pair)
        )

    def a_third(pair):
        n = pair[0] * 4 + pair[1]
        value = contrib[ya_rows(pair), own_lanes].astype(F32)
        steps = (1, 3) if pair in passed_pairs else (1, 3, 2)
        all_here(ya_ring.at[n, pl.ds(0, len(steps))], yr_recv.at[n])
        for step in steps:
            value = value + ya_ring[n, step - 1].astype(F32)
        a_sum[n] = value.astype(BF16)
        if n:
            start(a_give(pair))

    def b_own(half, j, k):
        return contrib.at[
            rows_of(me.block(half, j, k, me.c), SUM_A + half * (SUM_B // 2), SUM_B // 2), :
        ]

    def b_touch(half, j, k):
        pair = pair_of(half, j, k)
        sibling_here(pair)
        theirs = from_sib[
            pair[0] * 4 + pair[1], pl.ds(SUM_A + half * (SUM_B // 2), SUM_B // 2), :
        ]
        return b_own(half, j, k)[...].astype(F32) + theirs.astype(F32)

    def b_final(half, value):
        at = pl.ds(half * (SUM_B // 2), SUM_B // 2)
        plane_sum[at, :] = value
        plane_sum_b[at, :] = value.astype(BF16)

    b_back = scatter_plane(
        me, b_own, b_touch, b_final, start, all_here, (b_pass, b_ring, b_line),
        (sum_send, bp_recv, br_recv, bl_recv),
    )
    order = [(2, 2), (2, 1), (1, 2), (3, 2), (2, 3), (1, 1), (1, 3), (3, 1), (3, 3)]
    order += [(2, 0), (0, 2), (1, 0), (0, 1), (3, 0), (0, 3), (0, 0)]
    for n, pair in enumerate(order):
        compute(pair)
        if n in (3, 6, 9, 12):
            next(b_back)
        if n >= 3:
            a_first(order[n - 3])
        if n >= 14:
            a_second(order[n - 14])
    for n in range(13, 16):
        a_first(order[n])
        a_second(order[n - 11])
    next(b_back)
    next(b_back)
    for n in range(5, SUM_PASSED):
        a_second(order[n])
    for n, pair in enumerate(order):
        a_third(pair)
        if n in (3, 7, 11):
            next(b_back)
    next(b_back)

    def b_tp_sum(step):
        return remote(
            plane_sum_b.at[:, me.lanes(step)], tp_r.at[step - 1],
            tp_send, tp_recv.at[0], me.tp_peer(step),
        )

    for step in (2, 1, 3):
        start(b_tp_sum(step))
    moe = a_sum[0].astype(F32)
    all_here(a_ring, ar_recv.at[0])
    for pair in order[:-1]:
        moe = moe + a_ring[pair[0] * 4 + pair[1] - 1].astype(F32)
    out[:SUM_A, :] = (hid[:SUM_A, :] + moe).astype(BF16)
    moe = plane_sum[:, own_lanes]
    all_here(tp_r, tp_recv.at[0])
    for step in (1, 3, 2):
        moe = moe + tp_r[step - 1].astype(F32)
    out[SUM_A:, :] = (hid[SUM_A:, :] + moe).astype(BF16)

    for group in sends:
        a_blocks = hid_t.at[pl.ds(0, 15 * PART_A), pl.ds(0, TP_ROWS)]
        sized = {
            id(rs_send): part_r, id(ga_send): a_blocks, id(ar_send): a_ring, id(tp_send): tp_r
        }.get(id(group))
        if sized is None:
            sized = hid_t.at[pl.ds(0, group.total // (2 * ROWS))]
        assert group.total == 2 * math.prod(sized.shape), group.total
        remote(sized, sized, group, rs_recv.at[0], me.sibling()).copy.wait_send()


def local(
    queries, latent_cache, lengths, uv_weight, out_weight, residual, norm_gain,
    gate_weight, up_weight, down_weight, routes, route_weights,
):
    anywhere = pl.BlockSpec(memory_space=pl.ANY)
    vmem = pl.BlockSpec(memory_space=pltpu.VMEM)
    smem = pl.BlockSpec(memory_space=pltpu.SMEM)
    dma = pltpu.SemaphoreType.DMA
    scratch = [
        pltpu.VMEM((D // 128, 128), F32),
        pltpu.VMEM(routes.shape[::-1], jnp.int32),
        pltpu.VMEM(routes.shape[::-1], F32),
        pltpu.VMEM((OWN_ROWS, KEY, HEADS), BF16),
        pltpu.VMEM((OWN_ROWS, KEY, CTX), BF16),
        pltpu.VMEM((OWN_HEADS, LAT, VHEAD), BF16),
        pltpu.VMEM((COLS, INNER), BF16),
        pltpu.VMEM((COLS, TP_ROWS), BF16),
        pltpu.VMEM((UNITS, D), BF16),
        pltpu.VMEM((D // CHIP, 2 * UNITS, CHIP), BF16),
        pltpu.VMEM((D, UNITS), BF16),
        pltpu.VMEM((OWN_ROWS, HEADS, LAT), BF16),
        pltpu.VMEM((DP_ROWS, OWN_HEADS, LAT), BF16),
        pltpu.VMEM((LAT // 128, DP_ROWS * HALF_HEADS, 128), F32),
        pltpu.VMEM((ROWS, INNER), BF16),
        pltpu.VMEM((COLS, ROWS), F32),
        pltpu.VMEM((4, COLS, TP_ROWS), BF16),
        pltpu.VMEM((3, COLS, TP_ROWS), BF16),
        pltpu.VMEM((COLS, TP_ROWS), F32),
        pltpu.VMEM((D, ROWS), BF16),
        pltpu.VMEM((2 * UNITS, ROWS), F32),
        pltpu.VMEM((4, D // CHIP, 128), F32),
        pltpu.VMEM((8, ROWS), F32),
        pltpu.VMEM((UNITS, ROWS), BF16),
        pltpu.VMEM((D, ROWS), BF16),
        pltpu.VMEM((16, COLS, ROWS), BF16),
        pltpu.VMEM((SUM_B, ROWS), F32),
        pltpu.VMEM((SUM_B, ROWS), BF16),
        pltpu.VMEM((3, SUM_B, TP_ROWS), BF16),
        pltpu.VMEM((1, ROWS), F32),
        pltpu.VMEM((2, 2, SUM_B // 2, ROWS), BF16),
        pltpu.VMEM((2, 12, SUM_B // 2, ROWS), BF16),
        pltpu.VMEM((2, 3, SUM_B // 2, ROWS), BF16),
        pltpu.VMEM((15, SUM_A, TP_ROWS), BF16),
        pltpu.VMEM((16, SUM_A, TP_ROWS), BF16),
        pltpu.VMEM((16, SUM_A, TP_ROWS), BF16),
        pltpu.VMEM((16, 3, SUM_A, TP_ROWS), BF16),
        dma((14,)), dma((7,)),
        dma((2,)), dma((2, 16)), dma((2,)),
        dma((1,)), dma((1,)),
        dma((16,)), dma((16, 2)), dma((2, 16)), dma((2,)),
        dma((16,)), dma((16,)), dma((16,)), dma((1,)),
        dma((2, 2)), dma((2, 4)), dma((2,)), dma((1,)),
    ]
    return pl.pallas_call(
        kernel,
        out_shape=jax.ShapeDtypeStruct((COLS, TP_ROWS), BF16),
        in_specs=[smem] + [anywhere] * 11,
        out_specs=vmem,
        scratch_shapes=scratch,
        compiler_params=pltpu.CompilerParams(
            collective_id=0, has_side_effects=True, vmem_limit_bytes=62 * 1024 * 1024
        ),
        name="decode_step",
    )(
        lengths, jnp.swapaxes(queries, 1, 2), jnp.swapaxes(latent_cache, 1, 2), uv_weight,
        out_weight.T, residual.T, norm_gain.reshape(D // 128, 128),
        gate_weight[0], up_weight[0], down_weight[0], routes.T, route_weights.T,
    ).T


def solution(mesh):
    placed = (
        P(("dp", "tp"), None, None),
        P(("dp", "tp"), None, None),
        P(("dp", "tp")),
        P("tp", None, None),
        P("tp", "dp"),
        P(None, "dp"),
        P(),
        P("dp", None, "tp"),
        P("dp", None, "tp"),
        P("dp", "tp", None),
        P(),
        P(),
    )
    return jax.shard_map(
        local, mesh=mesh, in_specs=placed, out_specs=P("tp", "dp"), check_vma=False
    )
```
